32 devices in a mesh: dp: 8 (over y, x, core), seq: 4 (over z).
Axes of the slice: x: 2, y: 2, z: 4, core: 2. Of those that a mesh axis runs over, the one named last changes fastest.
Arguments:
- tokens: bfloat16 [8, 1024, 2048], P('dp', 'seq'), may hold values from -6 to 6
- cotangent: bfloat16 [8, 1024, 2048], P('dp', 'seq'), may hold values from -6 to 6
- doc_ids: int32 [8, 1024], P('dp'), may hold values from 0 to 64, as said below
- mix_in: float32 [2560, 2, 2048], P(('dp', 'seq')), may hold values from -0.125 to 0.125
- mix_out: float32 [2560, 2048], P(('dp', 'seq')), may hold values from -0.125 to 0.125
- gate_w: float32 [2560, 2, 160], P(('dp', 'seq')), may hold values from -0.5 to 0.5
- conv_w: float32 [4, 2560], P(None, ('dp', 'seq')), may hold values from -3 to 3
- conv_bias: float32 [2560], P(('dp', 'seq')), may hold values from -3 to 3
- gate_bias: float32 [2, 2560], P(None, ('dp', 'seq')), may hold values from -4 to 4
- decay_param: float32 [2560], P(('dp', 'seq')), may hold values from -13 to -4
- gain_one: float32 [2048], P(('dp', 'seq')), may hold values from 0.5 to 1.5
- gain_two: float32 [2048], P(('dp', 'seq')), may hold values from 0.5 to 1.5
- mlp_in: float32 [6144, 2, 2048], P(('dp', 'seq')), may hold values from -0.125 to 0.125
- mlp_out: float32 [6144, 2048], P(('dp', 'seq')), may hold values from -0.078125 to 0.078125
Outputs:
- layer_out: bfloat16 [8, 1024, 2048], P('dp', 'seq')
- input_grad: bfloat16 [8, 1024, 2048], P('dp', 'seq')
- grad_mix_in: float32 [2560, 2, 2048], P(('dp', 'seq'))
- grad_mix_out: float32 [2560, 2048], P(('dp', 'seq'))
- grad_gate_w: float32 [2560, 2, 160], P(('dp', 'seq'))
- grad_conv_w: float32 [4, 2560], P(None, ('dp', 'seq'))
- grad_conv_bias: float32 [2560], P(('dp', 'seq'))
- grad_gate_bias: float32 [2, 2560], P(None, ('dp', 'seq'))
- grad_decay: float32 [2560], P(('dp', 'seq'))
- grad_gain_one: float32 [2048], P(('dp', 'seq'))
- grad_gain_two: float32 [2048], P(('dp', 'seq'))
- grad_mlp_in: float32 [6144, 2, 2048], P(('dp', 'seq'))
- grad_mlp_out: float32 [6144, 2048], P(('dp', 'seq'))
The draws below stay inside these ranges and needn't reach their ends.
Inputs may be any that keep to these rules, and one draw needn't show every extreme that they name: doc_ids[s, t] numbers the document of token t of sequence s: 0 at the first token, rising by 0 or 1 from each token to the next; every sequence opens exactly 256 / 4 further documents, all within the first and the last 256 / 2 tokens of the sequence.
All inputs are finite; a program needn't handle non-finite values.
Results may differ from the reference program's by a relative error of at most 0.012.
The reference program's roundings to bfloat16 on the way count: a program that leaves them out, or rounds other values in their place, can miss the bound.
Values may be sent and summed in bfloat16 or wider, within the bound.
No kernel may reach another device: no remote copies, remote signals or barrier semaphores. Data moves between devices by JAX's collectives and lax.ppermute only.
A program may use at most 832 MiB of HBM per device.

```python
import jax
import jax.numpy as jnp
from jax import lax

D = 2048
R = 2560
NB = 16
FF = 6144
CW = 4
RUN = 256
BW = 160
LEN = 1024
SEQS = 8


def draw_doc_ids(key, part):
    key = jax.random.fold_in(key, 11)
    half = RUN // 2
    border = jnp.concatenate([jnp.arange(1, half), jnp.arange(LEN - half, LEN)]).astype(jnp.int32)
    row_keys = jax.random.split(key, SEQS)

    def one_row(row_key):
        ranks = jax.random.permutation(row_key, RUN - 1)
        chosen = jnp.where(ranks < RUN // 4, 1, 0).astype(jnp.int32)
        openings = jnp.zeros((LEN,), jnp.int32).at[border].add(chosen)
        return jnp.cumsum(openings)
    return jax.vmap(one_row)(row_keys).astype(jnp.int32)


def draw_decay_param(key, part):
    key = jax.random.fold_in(key, 5)
    spread = jax.random.uniform(key, (R,), jnp.float32)
    lowest = 0.1 / LEN
    highest = 0.05
    rates = lowest * jnp.exp(spread * jnp.log(highest / lowest))
    return jnp.log(jnp.expm1(rates / 4.0)).astype(jnp.float32)


def block_levels(rng, dims, pieces, smallest, top_value):
    factor_of = 1.0
    for axis_at, blocks in pieces:
        heights = jax.random.uniform(jax.random.fold_in(jax.random.fold_in(rng, 6), axis_at), (blocks,), jnp.float32, smallest / len(pieces), top_value / len(pieces))
        factor_of = factor_of * jnp.repeat(jnp.exp(heights), dims[axis_at] // blocks).reshape((-1,) + (1,) * (len(dims) - 1 - axis_at))
    return factor_of


def gaussian(key, extent, scale, limit, cuts=(), dtype=jnp.bfloat16):
    factor_of = block_levels(key, extent, cuts, -0.22, 0.18) if cuts else 1.0
    array = jax.random.normal(key, extent, jnp.float32) * scale * factor_of
    return jnp.minimum(jnp.maximum(array, -limit), limit).astype(dtype)


def setup_inputs(seed: int = 0) -> dict:
    arg_keys = jax.random.split(jax.random.key(seed), 15)
    return {
        "tokens": gaussian(arg_keys[0], (SEQS, LEN, D), 1.0, 6.0, ((0, 8), (1, 4))),
        "cotangent": gaussian(arg_keys[1], (SEQS, LEN, D), 1.0, 6.0, ((0, 8), (1, 4))),
        "doc_ids": draw_doc_ids(jax.random.fold_in(arg_keys[14], 71), 0),
        "mix_in": gaussian(arg_keys[3], (R, 2, D), D ** -0.5, 0.125, ((0, 32),), jnp.float32),
        "mix_out": gaussian(arg_keys[4], (R, D), R ** -0.5, 0.125, ((0, 32),), jnp.float32),
        "gate_w": gaussian(arg_keys[5], (R, 2, BW), BW ** -0.5, 0.5, ((0, 32),), jnp.float32),
        "conv_w": gaussian(arg_keys[6], (CW, R), CW ** -0.5, 3.0, ((1, 32),), jnp.float32),
        "conv_bias": gaussian(arg_keys[7], (R,), 0.5, 3.0, ((0, 32),), jnp.float32),
        "gate_bias": gaussian(arg_keys[8], (2, R), 1.0, 4.0, ((1, 32),), jnp.float32),
        "decay_param": draw_decay_param(jax.random.fold_in(arg_keys[14], 71), 0),
        "gain_one": jnp.clip(1.0 + 0.1 * jax.random.normal(arg_keys[10], (D,), jnp.float32), 0.5, 1.5),
        "gain_two": jnp.clip(1.0 + 0.1 * jax.random.normal(arg_keys[11], (D,), jnp.float32), 0.5, 1.5),
        "mlp_in": gaussian(arg_keys[12], (FF, 2, D), D ** -0.5, 0.125, ((0, 32),), jnp.float32),
        "mlp_out": gaussian(arg_keys[13], (FF, D), FF ** -0.5, 0.078125, ((0, 32),), jnp.float32),
    }


EPS = 1e-06
FLOOR = 0.0001
SHARP = 8.0
PRECISE = lax.Precision.HIGHEST

@jax.custom_vjp
def low(v):
    return lax.optimization_barrier(v.astype(jnp.bfloat16)).astype(jnp.float32)

@jax.custom_vjp
def low_back(v):
    return v

def low_keep(v):
    return (low(v), None)

def low_pass(kept, grad):
    return (grad,)

def back_keep(v):
    return (v, None)

def back_low(kept, grad):
    return (low(grad),)
low.defvjp(low_keep, low_pass)
low_back.defvjp(back_keep, back_low)

def rms_norm(values, gain_vec):
    return values * lax.rsqrt(lax.optimization_barrier(jnp.mean(values * values, axis=-1, keepdims=True)) + EPS) * gain_vec

def gate_rule(conv_out, gate_pre, decay_raw, fresh_start):
    recur_gate = jax.nn.sigmoid(gate_pre[0])
    entry_gate = jax.nn.sigmoid(gate_pre[1])
    decays = jnp.exp(-SHARP * jax.nn.softplus(decay_raw) * recur_gate)
    scaling = jnp.where(fresh_start, 1.0, jnp.sqrt(jnp.maximum(1.0 - decays * decays, FLOOR)))
    carried = jnp.where(fresh_start, 0.0, decays)
    return (carried, conv_out * entry_gate * scaling)

def row_forward(row_tokens, row_docs, params):
    mix_in, mix_out, gate_w, conv_w, conv_bias, gate_bias, decay_param, gain_one, gain_two, mlp_in, mlp_out = params
    length = row_tokens.shape[0]
    h_one = low(rms_norm(row_tokens, low(gain_one)))
    w_in = low(mix_in)
    y_pre = low_back(jnp.dot(h_one, w_in[:, 0, :].T, precision=PRECISE))
    u_vals = low(low_back(jnp.dot(h_one, w_in[:, 1, :].T, precision=PRECISE)))
    row_docs = row_docs.astype(jnp.int32)
    padded_docs = jnp.concatenate([jnp.full((3,), -1, jnp.int32), row_docs])
    u_ext = jnp.concatenate([jnp.zeros((3, R), jnp.float32), u_vals], 0)
    conv_taps = low(conv_w)
    conv_out = low(conv_bias)[None, :] + jnp.zeros((length, R), jnp.float32)
    for offset in range(CW):
        same_doc = jnp.where(padded_docs[3 - offset:3 - offset + length] == row_docs, 1.0, 0.0)[:, None]
        conv_out = conv_out + conv_taps[offset] * u_ext[3 - offset:3 - offset + length] * same_doc
    conv_low = low(conv_out)
    blocks = low(gate_w).reshape(NB, BW, 2, BW)
    gate_pre = jnp.einsum('tbj,bokj->ktbo', conv_low.reshape(length, NB, BW), blocks, precision=PRECISE).reshape(2, length, R)
    gate_pre = low_back(gate_pre + low(gate_bias)[:, None, :])
    fresh_start = (row_docs != padded_docs[2:2 + length])[:, None]
    carried, inputs = gate_rule(conv_low, gate_pre, low(decay_param), fresh_start)

    def advance(previous, element):
        updated = element[0] * previous + element[1]
        return (updated, updated)
    _, states = lax.scan(advance, jnp.zeros((R,), jnp.float32), (carried, inputs))
    mixed_out = low(jax.nn.gelu(y_pre) * states)
    x_one = row_tokens + low_back(jnp.dot(mixed_out, low(mix_out), precision=PRECISE))
    h_two = low(rms_norm(x_one, low(gain_two)))
    w_up = low(mlp_in)
    gate_vals = low_back(jnp.dot(h_two, w_up[:, 0, :].T, precision=PRECISE))
    up_vals = low_back(jnp.dot(h_two, w_up[:, 1, :].T, precision=PRECISE))
    hidden = low(jax.nn.gelu(gate_vals) * up_vals)
    return x_one + jnp.dot(hidden, low(mlp_out), precision=PRECISE)

def reference(tokens, cotangent, doc_ids, mix_in, mix_out, gate_w, conv_w, conv_bias, gate_bias, decay_param, gain_one, gain_two, mlp_in, mlp_out):
    params = (mix_in, mix_out, gate_w, conv_w, conv_bias, gate_bias, decay_param, gain_one, gain_two, mlp_in, mlp_out)

    def one_row(totals, element):
        row_tokens, row_cot, row_docs = element

        def forward(values, weights):
            return row_forward(values, row_docs, weights)
        result, pullback = jax.vjp(forward, row_tokens.astype(jnp.float32), params)
        d_tokens, d_params = pullback(row_cot.astype(jnp.float32))
        totals = jax.tree.map(lambda running, addend: running + addend, totals, d_params)
        return (totals, (result.astype(jnp.bfloat16), d_tokens.astype(jnp.bfloat16)))
    initial = jax.tree.map(jnp.zeros_like, params)
    totals, (layer_out, input_grad) = lax.scan(one_row, initial, (tokens, cotangent, doc_ids))
    return (layer_out, input_grad, totals[0], totals[1], totals[2], totals[3], totals[4], totals[5], totals[6], totals[7], totals[8], totals[9], totals[10])
```

```python
import functools

import jax
import jax.numpy as jnp
from jax import lax
from jax.experimental import pallas as pl
from jax.experimental.pallas import tpu as pltpu
from jax.sharding import PartitionSpec as P

EPS = 1e-06
FLOOR = 0.0001
SHARP = 8.0
HALO = 16
F32 = jnp.float32
BF16 = jnp.bfloat16
VMEM_LIMIT = 56 * 1024 * 1024
ANY = pl.BlockSpec(memory_space=pl.ANY)
ROOT = 0.7978845608028654
CUBE = 0.044715


def dot_nt(left, right):
    return lax.dot_general(left, right, (((1,), (1,)), ((), ())), preferred_element_type=F32)


def dot_nn(left, right):
    return lax.dot_general(left, right, (((1,), (0,)), ((), ())), preferred_element_type=F32)


def dot_tn(left, right):
    return lax.dot_general(left, right, (((0,), (0,)), ((), ())), preferred_element_type=F32)


def rms_norm(values, gain_vec):
    return values * lax.rsqrt(jnp.mean(values * values, axis=-1, keepdims=True) + EPS) * gain_vec


def gelu_parts(values):
    squared = values * values
    bend = jnp.tanh(ROOT * (values + CUBE * values * squared))
    half = 0.5 * (1.0 + bend)
    slope = half + 0.5 * values * (1.0 - bend * bend) * (ROOT * (1.0 + 3.0 * CUBE * squared))
    return values * half, slope


def gelu_value(values):
    bend = jnp.tanh(ROOT * (values + CUBE * values * values * values))
    return values * (0.5 * (1.0 + bend))


def plane_stages(count):
    bits = count.bit_length() - 1
    upper = list(range(1, bits))
    stages = []
    for place in range(len(upper)):
        pairs = []
        for source in range(count):
            shift = place if source % 2 == 0 else (place + 1) % len(upper)
            pairs.append((source, source ^ (1 << upper[shift])))
        stages.append(pairs)
    twin = [(source, source ^ 1) for source in range(count)]
    return stages, twin


def gather_rows(piece):
    stages, twin = plane_stages(lax.axis_size("dp"))
    held = [piece]
    other = [lax.ppermute(piece, "dp", twin)]
    for pairs in stages:
        arrived = [lax.ppermute(part, "dp", pairs) for part in held]
        held = held + arrived
        other = other + [lax.ppermute(part, "dp", twin) for part in arrived]
    return held + other


def scatter_rows(own, partner):
    stages, twin = plane_stages(lax.axis_size("dp"))
    held = own.astype(F32) + lax.ppermute(partner, "dp", twin).astype(F32)
    for pairs in reversed(stages):
        half = held.shape[0] // 2
        sent = held[half:].astype(BF16)
        held = held[:half] + lax.ppermute(sent, "dp", pairs).astype(F32)
    return held[0]


def hand_on(value, steps):
    count = lax.axis_size("seq")
    first, last = (max(0, -steps), min(count, count - steps))
    return lax.ppermute(value, "seq", [(source, source + steps) for source in range(first, last)])


def scan_into(keep, entry, cum_ref, state_ref, backward):
    rows, width = keep.shape
    groups = rows // 8
    mult = keep.reshape(groups, 8, width)
    total = entry.reshape(groups, 8, width)
    place = lax.broadcasted_iota(jnp.int32, (groups, 8, width), 1)
    for hop in (1, 2, 4):
        if backward:
            shift, valid = 8 - hop, place < 8 - hop
        else:
            shift, valid = hop, place >= hop
        near_mult = pltpu.roll(mult, shift, 1)
        near_total = pltpu.roll(total, shift, 1)
        total = jnp.where(valid, total + mult * near_total, total)
        mult = jnp.where(valid, mult * near_mult, mult)
    carry_total = jnp.zeros((1, width), F32)
    carry_mult = jnp.ones((1, width), F32)
    edge = 0 if backward else 7
    order = range(groups - 1, -1, -1) if backward else range(groups)
    for group in order:
        now_total = total[group] + mult[group] * carry_total
        now_mult = mult[group] * carry_mult
        state_ref[0, group * 8 : group * 8 + 8, :] = now_total
        cum_ref[0, group * 8 : group * 8 + 8, :] = now_mult
        carry_total = now_total[edge : edge + 1]
        carry_mult = now_mult[edge : edge + 1]
    return carry_mult, carry_total


def folded(refs):
    carry = refs[-1][0, 1:2, :]
    for ref in refs[-2::-1]:
        carry = ref[0, 1:2, :] + ref[0, 0:1, :] * carry
    return carry


def ends_block(mult, total):
    width = mult.shape[1]
    return jnp.concatenate([mult, total, jnp.zeros((6, width), F32)], 0)


def fetch_all(refs, buf, sems):
    for index, ref in enumerate(refs):
        pltpu.make_async_copy(ref, buf.at[index], sems.at[index]).start()


def fetched(refs, buf, sems, index):
    pltpu.make_async_copy(refs[0], buf.at[index], sems.at[index]).wait()


def mixer_enter_kernel(count, *refs):
    x_refs = refs[:count]
    (gain, wu, wy, wz, par, h_out, u_out, y_out, conv_out, r_out, e_out, k_out, m_out, a_out, s_out, ends, buf, sems) = refs[count:]
    step = pl.program_id(0)

    @pl.when(step == 0)
    def _():
        fetch_all(x_refs, buf, sems)

    fetched(x_refs, buf, sems, step)
    x_low = buf[step]
    rows = x_low.shape[0] - HALO
    width = wu.shape[0]
    x_val = x_low.astype(F32)
    h_low = rms_norm(x_val, gain[...]).astype(BF16)
    h_out[0] = h_low[HALO:]
    u_low = dot_nt(h_low, wu[...]).astype(BF16)
    u_out[0] = u_low
    y_out[0] = dot_nt(h_low[HALO:], wy[...])
    info = jnp.broadcast_to(x_val[0:1, :rows], (width, rows)).astype(BF16)
    across = lax.broadcasted_iota(jnp.int32, (rows, rows), 0)
    down = lax.broadcasted_iota(jnp.int32, (rows, rows), 1)
    same = dot_nt(jnp.where(across == down, 1.0, 0.0).astype(BF16), info)
    m_out[0] = same.astype(BF16)
    u_val = u_low.astype(F32)
    conv = par[4:5, :] + par[0:1, :] * u_val[HALO:]
    for back in (1, 2, 3):
        term = par[back : back + 1, :] * u_val[HALO - back : HALO - back + rows]
        conv = conv + jnp.where(same >= back, term, 0.0)
    conv_low = conv.astype(BF16)
    conv_out[0] = conv_low
    conv = conv_low.astype(F32)
    pre = dot_nt(conv_low, wz[...])
    recur = jax.nn.sigmoid(pre[:, :width] + par[5:6, :])
    enter = jax.nn.sigmoid(pre[:, width:] + par[6:7, :])
    keep = jnp.where(same >= 1.0, jnp.exp(par[7:8, :] * recur), 0.0)
    r_out[0] = recur
    e_out[0] = enter
    k_out[0] = keep
    inputs = conv * enter * jnp.sqrt(jnp.maximum(1.0 - keep * keep, FLOOR))
    mult, total = scan_into(keep, inputs, a_out, s_out, False)
    ends[0] = ends_block(mult, total)


def resident(shape):
    zeros = (0,) * len(shape)
    return pl.BlockSpec(shape, lambda step: zeros)


def per_piece(shape, first=0):
    rest = (0,) * len(shape)
    return pl.BlockSpec((1,) + shape, lambda step: (step + first,) + rest)


def call(kernel, grid, in_specs, out_specs, out_shape, scratch, flops, moved):
    return pl.pallas_call(
        kernel,
        grid=grid,
        in_specs=in_specs,
        out_specs=out_specs,
        out_shape=out_shape,
        scratch_shapes=scratch,
        compiler_params=pltpu.CompilerParams(
            vmem_limit_bytes=VMEM_LIMIT, dimension_semantics=("arbitrary",) * len(grid)
        ),
        cost_estimate=pl.CostEstimate(flops=int(flops), bytes_accessed=int(moved), transcendentals=0),
    )


def mixer_enter(pieces, gain, wu, wy, wz, par):
    count = len(pieces)
    tall, model = pieces[0].shape
    rows = tall - HALO
    width = wu.shape[0]

    def out(height, columns, dtype):
        return jax.ShapeDtypeStruct((count, height, columns), dtype)

    shapes = [
        out(rows, model, BF16),
        out(tall, width, BF16),
        out(rows, width, F32),
        out(rows, width, BF16),
        out(rows, width, F32),
        out(rows, width, F32),
        out(rows, width, F32),
        out(rows, width, BF16),
        out(rows, width, F32),
        out(rows, width, F32),
        out(8, width, F32),
    ]
    return call(
        functools.partial(mixer_enter_kernel, count),
        (count,),
        [ANY] * count + [resident(v.shape) for v in (gain, wu, wy, wz, par)],
        [per_piece(s.shape[1:]) for s in shapes],
        shapes,
        [pltpu.VMEM((count, tall, model), BF16), pltpu.SemaphoreType.DMA((count,))],
        2 * count * rows * model * width * 2,
        count * rows * (model * 4 + width * 34),
    )(*pieces, gain, wu, wy, wz, par)


def mixer_leave_kernel(hops, *refs):
    ends = refs[:hops]
    cum, local, y_pre, w_out, part = refs[hops:]
    states = local[0] + cum[0] * folded(ends)
    mixed = (gelu_value(y_pre[0]) * states).astype(BF16)
    part[0] = dot_nn(mixed, w_out[...]).astype(BF16)


def mixer_leave(ends, cum, local, y_pre, w_out, first, count):
    rows, width = cum.shape[1:]
    model = w_out.shape[1]
    return call(
        functools.partial(mixer_leave_kernel, len(ends)),
        (count,),
        [per_piece((8, width), first)] * len(ends)
        + [per_piece((rows, width), first)] * 3
        + [resident(w_out.shape)],
        per_piece((rows, model)),
        jax.ShapeDtypeStruct((count, rows, model), BF16),
        [],
        2 * count * rows * width * model,
        count * rows * (width * 12 + model * 2),
    )(*ends, cum, local, y_pre, w_out)


def head_back_kernel(count, hops, *refs):
    d_refs = refs[:count]
    ends = refs[count : count + hops]
    (cum, local, y_pre, keep_ref, w_out, dy_out, mixed_out, cb_out, lb_out, ends_out, buf, sems) = refs[count + hops :]
    step = pl.program_id(0)

    @pl.when(step == 0)
    def _():
        fetch_all(d_refs, buf, sems)

    fetched(d_refs, buf, sems, step)
    d_mixed = dot_nt(buf[step], w_out[...])
    states = local[0] + cum[0] * folded(ends)
    value, slope = gelu_parts(y_pre[0])
    mixed_out[0] = (value * states).astype(BF16)
    dy_out[0] = (slope * d_mixed * states).astype(BF16)
    keep = keep_ref[0]
    width = keep.shape[1]
    next_keep = jnp.concatenate([keep[1:], jnp.ones((1, width), F32)], 0)
    mult, total = scan_into(next_keep, d_mixed * value, cb_out, lb_out, True)
    ends_out[0] = ends_block(mult * keep[0:1], total * keep[0:1])


def head_back(pieces, ends, cum, local, y_pre, keep, w_out):
    count = len(pieces)
    rows, model = pieces[0].shape
    width = cum.shape[2]

    def out(height, dtype):
        return jax.ShapeDtypeStruct((count, height, width), dtype)

    shapes = [out(rows, BF16), out(rows, BF16), out(rows, F32), out(rows, F32), out(8, F32)]
    return call(
        functools.partial(head_back_kernel, count, len(ends)),
        (count,),
        [ANY] * count
        + [per_piece((8, width))] * len(ends)
        + [per_piece((rows, width))] * 4
        + [resident(w_out.shape)],
        [per_piece(s.shape[1:]) for s in shapes],
        shapes,
        [pltpu.VMEM((count, rows, model), BF16), pltpu.SemaphoreType.DMA((count,))],
        2 * count * rows * width * model,
        count * rows * (width * 28 + model * 2),
    )(*pieces, *ends, cum, local, y_pre, keep, w_out)


def tail_back_kernel(hops, *refs):
    ends = refs[:hops]
    later = refs[hops : 2 * hops]
    (cb, lb, cum, local, r_ref, e_ref, k_ref, conv_ref, u_ref, m_ref, wz, par, du_out, edge_out, gw_out, small_out) = refs[2 * hops :]
    step = pl.program_id(0)

    @pl.when(step == 0)
    def _():
        gw_out[...] = jnp.zeros_like(gw_out)
        small_out[...] = jnp.zeros_like(small_out)

    state_in = folded(ends)
    d_states = lb[0] + cb[0] * folded(later)
    states = local[0] + cum[0] * state_in
    prev = jnp.concatenate([state_in, states[:-1]], 0)
    recur, enter, keep = r_ref[0], e_ref[0], k_ref[0]
    conv_low = conv_ref[0]
    conv = conv_low.astype(F32)
    rows, width = conv.shape
    spare = 1.0 - keep * keep
    scaling = jnp.sqrt(jnp.maximum(spare, FLOOR))
    weight = jnp.where(spare > FLOOR, 0.5, jnp.where(spare == FLOOR, 0.25, 0.0)) / scaling
    d_enter_sum = d_states * conv
    d_spare = d_enter_sum * enter * weight
    d_expo = (d_states * prev - 2.0 * keep * d_spare) * keep
    d_recur = d_expo * par[7:8, :] * recur * (1.0 - recur)
    d_enter = d_enter_sum * scaling * enter * (1.0 - enter)
    d_pre = jnp.concatenate([d_recur.astype(BF16), d_enter.astype(BF16)], 1)
    d_conv = d_states * enter * scaling + dot_nn(d_pre, wz[...])
    gw_out[...] += dot_tn(d_pre, conv_low)
    d_pre_val = d_pre.astype(F32)
    same = m_ref[0].astype(F32)
    u_val = u_ref[0].astype(F32)
    sums = []
    d_u = jnp.zeros((rows, width), F32)
    head = jnp.zeros((8, width), F32)
    for back in range(4):
        masked = d_conv if back == 0 else jnp.where(same >= back, d_conv, 0.0)
        sums.append(jnp.sum(masked * u_val[HALO - back : HALO - back + rows], axis=0, keepdims=True))
        moved = masked * par[back : back + 1, :]
        if back == 0:
            d_u = d_u + moved
        else:
            nothing = jnp.zeros((back, width), F32)
            d_u = d_u + jnp.concatenate([moved[back:], nothing], 0)
            head = head + jnp.concatenate([jnp.zeros((8 - back, width), F32), moved[:back]], 0)
    sums.append(jnp.sum(d_conv, axis=0, keepdims=True))
    sums.append(jnp.sum(d_pre_val[:, :width], axis=0, keepdims=True))
    sums.append(jnp.sum(d_pre_val[:, width:], axis=0, keepdims=True))
    sums.append(jnp.sum(d_expo * recur, axis=0, keepdims=True))
    small_out[...] += jnp.concatenate(sums, 0)
    du_out[0] = d_u.astype(BF16)
    edge_out[0, 0:8, :] = head
    edge_out[0, 8:16, :] = d_u[rows - 8 :]


def tail_back(ends, later, cb, lb, cum, local, recur, enter, keep, conv, u_ext, same, wz, par):
    count, rows, width = cb.shape
    shapes = [
        jax.ShapeDtypeStruct((count, rows, width), BF16),
        jax.ShapeDtypeStruct((count, 16, width), F32),
        jax.ShapeDtypeStruct(wz.shape, F32),
        jax.ShapeDtypeStruct((8, width), F32),
    ]
    tall = u_ext.shape[1]
    return call(
        functools.partial(tail_back_kernel, len(ends)),
        (count,),
        [per_piece((8, width))] * (2 * len(ends))
        + [per_piece((rows, width))] * 8
        + [per_piece((tall, width)), per_piece((rows, width)), resident(wz.shape), resident(par.shape)],
        [per_piece((rows, width)), per_piece((16, width)), resident(wz.shape), resident((8, width))],
        shapes,
        [],
        8 * count * rows * width * width,
        count * rows * width * 36,
    )(*ends, *later, cb, lb, cum, local, recur, enter, keep, conv, u_ext, same, wz, par)


def rows_times_kernel(terms, *refs):
    total = dot_nn(refs[0][0], refs[terms][...])
    for term in range(1, terms):
        total = total + dot_nn(refs[term][0], refs[terms + term][...])
    refs[-1][0] = total.astype(BF16)


def rows_times(lefts, rights, first, count):
    rows = lefts[0].shape[1]
    model = rights[0].shape[1]
    inner = sum(right.shape[0] for right in rights)
    return call(
        functools.partial(rows_times_kernel, len(lefts)),
        (count,),
        [per_piece(left.shape[1:], first) for left in lefts] + [resident(r.shape) for r in rights],
        per_piece((rows, model)),
        jax.ShapeDtypeStruct((count, rows, model), BF16),
        [],
        2 * count * rows * inner * model,
        count * rows * 2 * (inner + model) + 2 * inner * model,
    )(*lefts, *rights)


def mlp_kernel(count, *refs):
    h_refs = refs[:count]
    c_refs = refs[count : 2 * count]
    wg, wu, wo, hid_out, dg_out, du_out, h_buf, c_buf, h_sems, c_sems = refs[2 * count :]
    step = pl.program_id(0)

    @pl.when(step == 0)
    def _():
        fetch_all(h_refs, h_buf, h_sems)
        fetch_all(c_refs, c_buf, c_sems)

    def one_piece(index, carry):
        @pl.when(step == 0)
        def _():
            fetched(h_refs, h_buf, h_sems, index)
            fetched(c_refs, c_buf, c_sems, index)

        h_low = h_buf[index]
        gate = dot_nt(h_low, wg[...])
        up = dot_nt(h_low, wu[...])
        d_hidden = dot_nt(c_buf[index], wo[...])
        value, slope = gelu_parts(gate)
        hid_out[index] = (value * up).astype(BF16)
        dg_out[index] = (d_hidden * up * slope).astype(BF16)
        du_out[index] = (d_hidden * value).astype(BF16)
        return carry

    lax.fori_loop(0, count, one_piece, 0)


def mlp_middle(h_pieces, c_pieces, wg, wu, wo):
    count = len(h_pieces)
    rows, model = h_pieces[0].shape
    hidden = wg.shape[0]
    tile = next(t for t in (256, 128, hidden) if hidden % t == 0)
    shape = jax.ShapeDtypeStruct((count, rows, hidden), BF16)
    w_spec = pl.BlockSpec((tile, model), lambda step: (step, 0))
    out_spec = pl.BlockSpec((count, rows, tile), lambda step: (0, 0, step))
    return call(
        functools.partial(mlp_kernel, count),
        (hidden // tile,),
        [ANY] * (2 * count) + [w_spec] * 3,
        [out_spec] * 3,
        [shape] * 3,
        [
            pltpu.VMEM((count, rows, model), BF16),
            pltpu.VMEM((count, rows, model), BF16),
            pltpu.SemaphoreType.DMA((count,)),
            pltpu.SemaphoreType.DMA((count,)),
        ],
        6 * count * rows * model * hidden,
        count * rows * (4 * model + 6 * hidden) + 6 * model * hidden,
    )(*h_pieces, *c_pieces, wg, wu, wo)


def weight_grad(rows_left, rows_right):
    left = rows_left.reshape(-1, rows_left.shape[-1])
    right = rows_right.reshape(-1, rows_right.shape[-1])
    return dot_tn(left, right).astype(BF16)


def seq_gather(shard):
    return lax.all_gather(shard, "seq", axis=0, tiled=True)


def seq_scatter(whole):
    return lax.psum_scatter(whole, "seq", scatter_dimension=0, tiled=True)


def per_device(
    tokens,
    cotangent,
    doc_ids,
    mix_in,
    mix_out,
    gate_w,
    conv_w,
    conv_bias,
    gate_bias,
    decay_param,
    gain_one,
    gain_two,
    mlp_in,
    mlp_out,
):
    run_len, model = tokens.shape[1:]
    n_seq = lax.axis_size("seq")
    n_dev = lax.axis_size("dp") * n_seq
    own = mix_out.shape[0]
    block = gate_w.shape[2]
    chan = own * n_seq
    width = -(-chan // 128) * 128
    blocks = chan // block

    x_low = tokens.reshape(run_len, model)
    x_zero = x_low.astype(F32)
    cot_low = cotangent.reshape(run_len, model)
    lead = hand_on(x_low[run_len - HALO :], 1)
    first_token = lax.axis_index("seq") * run_len
    padded = jnp.concatenate([jnp.full((3,), -1, jnp.int32), doc_ids.reshape(-1)])
    own_docs = lax.dynamic_slice_in_dim(padded, first_token + 3, run_len)
    same = sum(
        jnp.where(lax.dynamic_slice_in_dim(padded, first_token + 3 - back, run_len) == own_docs, 1.0, 0.0)
        for back in (1, 2, 3)
    )
    info = jnp.pad(same, (0, model - run_len)).astype(BF16)[None]
    x_piece = jnp.concatenate([info, lead[1:], x_low], 0)

    small = jnp.concatenate(
        [
            gate_w.reshape(own, 2 * block),
            conv_w.T,
            conv_bias[:, None],
            gate_bias.T,
            decay_param[:, None],
        ],
        1,
    )
    extra = -(-small.shape[1] // 128) * 128
    small = jnp.pad(small, ((0, 0), (0, extra - small.shape[1])))
    w_u_all = seq_gather(jnp.concatenate([mix_in[:, 1, :], small], 1).astype(BF16))
    w_y = seq_gather(mix_in[:, 0, :].astype(BF16))
    w_out = seq_gather(mix_out.astype(BF16))
    w_gate = seq_gather(mlp_in[:, 0, :].astype(BF16))
    w_up = seq_gather(mlp_in[:, 1, :].astype(BF16))
    w_down = seq_gather(mlp_out.astype(BF16))
    gains = jnp.concatenate([gain_one, gain_two]).astype(BF16)[None]
    gains = lax.all_gather(gains, ("dp", "seq"), axis=0, tiled=True).astype(F32)
    part = gain_one.shape[0]
    g_one = gains[:, :part].reshape(1, model)
    g_two = gains[:, part:].reshape(1, model)

    def widened(rows):
        return jnp.pad(rows, ((0, width - chan), (0, 0)))

    w_u = widened(w_u_all[:, :model])
    w_y = widened(w_y)
    w_out = widened(w_out)
    gate_rows = w_u_all[:, model : model + 2 * block].reshape(blocks, block, 2, block)
    eye = jnp.eye(blocks, dtype=BF16)
    w_z = jnp.einsum("bogj,bc->gbocj", gate_rows, eye).reshape(2, chan, chan)
    w_z = jnp.pad(w_z, ((0, 0), (0, width - chan), (0, width - chan))).reshape(2 * width, width)
    par = w_u_all[:, model + 2 * block : model + 2 * block + 8].astype(F32).T
    decay_rate = -SHARP * jax.nn.softplus(par[7])
    decay_slope = -SHARP * jax.nn.sigmoid(par[7])
    par = jnp.pad(jnp.concatenate([par[:7], decay_rate[None]], 0), ((0, 0), (0, width - chan)))

    x_pieces = gather_rows(x_piece)
    count = len(x_pieces)
    half = count // 2
    (h_one, u_ext, y_pre, conv, recur, enter, keep, same, cum, local, ends) = mixer_enter(
        x_pieces, g_one, w_u, w_y, w_z, par
    )
    earlier = [hand_on(ends, steps) for steps in range(1, n_seq)]
    partner = mixer_leave(earlier, cum, local, y_pre, w_out, half, half)
    mine = mixer_leave(earlier, cum, local, y_pre, w_out, 0, half)
    x_one = x_zero + scatter_rows(mine, partner)
    n_two, norm_two_back = jax.vjp(rms_norm, x_one, g_two)
    h_two = n_two.astype(BF16)

    c_pieces = gather_rows(cot_low)
    h_pieces = gather_rows(h_two)
    hidden, d_gate, d_up = mlp_middle(h_pieces, c_pieces, w_gate, w_up, w_down)
    partner = rows_times([d_gate, d_up], [w_gate, w_up], half, half)
    mine = rows_times([d_gate, d_up], [w_gate, w_up], 0, half)
    d_h_two = scatter_rows(mine, partner)
    h_all = jnp.concatenate(h_pieces, 0)
    c_all = jnp.concatenate(c_pieces, 0)
    grad_down = seq_scatter(weight_grad(hidden, c_all))
    grad_gate = seq_scatter(weight_grad(d_gate, h_all))
    grad_up = seq_scatter(weight_grad(d_up, h_all))
    partner = rows_times([hidden], [w_down], half, half)
    mine = rows_times([hidden], [w_down], 0, half)
    layer_out = (x_one + scatter_rows(mine, partner)).astype(BF16).reshape(1, run_len, model)
    d_x_norm, d_gain_two = norm_two_back(d_h_two)
    d_x_one = cot_low.astype(F32) + d_x_norm
    d_mix = d_x_one.astype(BF16)

    d_pieces = gather_rows(d_mix)
    d_y, mixed, cum_back, local_back, ends_back = head_back(
        d_pieces, earlier, cum, local, y_pre, keep, w_out
    )
    later = [hand_on(ends_back, -steps) for steps in range(1, n_seq)]
    grad_out = seq_scatter(weight_grad(mixed, jnp.concatenate(d_pieces, 0))[:chan])
    grad_y = seq_scatter(weight_grad(d_y, h_one)[:chan])
    d_u, edges, grad_z, sums = tail_back(
        earlier, later, cum_back, local_back, cum, local, recur, enter, keep, conv, u_ext, same, w_z, par
    )
    from_next = hand_on(edges[:, :8], -1)
    d_u = lax.dynamic_update_slice(d_u, (edges[:, 8:] + from_next).astype(BF16), (0, run_len - 8, 0))
    partner = rows_times([d_y, d_u], [w_y, w_u], half, half)
    mine = rows_times([d_y, d_u], [w_y, w_u], 0, half)
    d_h_one = scatter_rows(mine, partner)
    _, norm_one_back = jax.vjp(rms_norm, x_zero, g_one)
    d_x_zero, d_gain_one = norm_one_back(d_h_one)
    input_grad = (d_x_one + d_x_zero).astype(BF16).reshape(1, run_len, model)

    grad_u = weight_grad(d_u, h_one)[:chan]
    grad_z = grad_z.reshape(2, width, width)[:, :chan, :chan].reshape(2, blocks, block, blocks, block)
    grad_z = jnp.stack([grad_z[:, b, :, b, :] for b in range(blocks)], 1)
    grad_z = jnp.transpose(grad_z, (1, 2, 0, 3)).reshape(chan, 2 * block)
    sums = sums[:, :chan]
    sums = jnp.concatenate([sums[:7], (sums[7] * decay_slope)[None]], 0).T
    tail = jnp.concatenate([grad_z, sums], 1)
    tail = jnp.pad(tail, ((0, 0), (0, extra - tail.shape[1]))).astype(BF16)
    grad_u = seq_scatter(jnp.concatenate([grad_u, tail], 1))
    tail = grad_u[:, model:].astype(F32)
    grad_mix_in = jnp.stack([grad_y.astype(F32), grad_u[:, :model].astype(F32)], 1)
    at = 2 * block
    d_gains = jnp.concatenate([d_gain_one.reshape(n_dev, part), d_gain_two.reshape(n_dev, part)], 1)
    d_gains = lax.psum_scatter(d_gains, ("dp", "seq"), scatter_dimension=0, tiled=True)[0]
    return (
        layer_out,
        input_grad,
        grad_mix_in,
        grad_out.astype(F32),
        tail[:, :at].reshape(own, 2, block),
        tail[:, at : at + 4].T,
        tail[:, at + 4],
        tail[:, at + 5 : at + 7].T,
        tail[:, at + 7],
        d_gains[:part],
        d_gains[part:],
        jnp.stack([grad_gate.astype(F32), grad_up.astype(F32)], 1),
        grad_down.astype(F32),
    )


def solution(mesh):
    rows = P(("dp", "seq"))
    placed = (
        P("dp", "seq", None),
        P("dp", "seq", None),
        P("dp", None),
        P(("dp", "seq"), None, None),
        P(("dp", "seq"), None),
        P(("dp", "seq"), None, None),
        P(None, ("dp", "seq")),
        rows,
        P(None, ("dp", "seq")),
        rows,
        rows,
        rows,
        P(("dp", "seq"), None, None),
        P(("dp", "seq"), None),
    )
    return jax.shard_map(
        per_device,
        mesh=mesh,
        in_specs=placed,
        out_specs=placed[:2] + placed[3:],
        check_vma=False,
    )
```

```python
import functools

import jax
import jax.numpy as jnp
from jax import lax
from jax.experimental import pallas as pl
from jax.experimental.pallas import tpu as pltpu
from jax.sharding import PartitionSpec as P

EPS = 1e-06
FLOOR = 0.0001
SHARP = 8.0
HALO = 16
F32 = jnp.float32
BF16 = jnp.bfloat16
VMEM_LIMIT = 56 * 1024 * 1024
ANY = pl.BlockSpec(memory_space=pl.ANY)
ROOT = 0.7978845608028654
CUBE = 0.044715


def dot_nt(left, right):
    return lax.dot_general(left, right, (((1,), (1,)), ((), ())), preferred_element_type=F32)


def dot_nn(left, right):
    return lax.dot_general(left, right, (((1,), (0,)), ((), ())), preferred_element_type=F32)


def dot_tn(left, right):
    return lax.dot_general(left, right, (((0,), (0,)), ((), ())), preferred_element_type=F32)


def rms_norm(values, gain_vec):
    return values * lax.rsqrt(jnp.mean(values * values, axis=-1, keepdims=True) + EPS) * gain_vec


def gelu_parts(values):
    squared = values * values
    bend = jnp.tanh(ROOT * (values + CUBE * values * squared))
    half = 0.5 * (1.0 + bend)
    slope = half + 0.5 * values * (1.0 - bend * bend) * (ROOT * (1.0 + 3.0 * CUBE * squared))
    return values * half, slope


def gelu_value(values):
    bend = jnp.tanh(ROOT * (values + CUBE * values * values * values))
    return values * (0.5 * (1.0 + bend))


def plane_stages(count):
    bits = count.bit_length() - 1
    upper = list(range(1, bits))
    stages = []
    for place in range(len(upper)):
        pairs = []
        for source in range(count):
            shift = place if source % 2 == 0 else (place + 1) % len(upper)
            pairs.append((source, source ^ (1 << upper[shift])))
        stages.append(pairs)
    twin = [(source, source ^ 1) for source in range(count)]
    return stages, twin


def gather_rows(piece, fills=(), filled=None):
    stages, twin = plane_stages(lax.axis_size("dp"))
    held = [piece] + [None] * (2 ** len(stages) - 1)
    for wave in range(1, len(stages) + 1):
        members = [m for m in range(len(held)) if bin(m).count("1") == wave]
        tops = [m.bit_length() - 1 for m in members]
        sent = [held[m ^ (1 << top)] for m, top in zip(members, tops)]
        arrived = [lax.ppermute(part, "dp", stages[top]) for part, top in zip(sent, tops)]
        if wave <= len(fills):
            arrived, made = lax.optimization_barrier((arrived, fills[wave - 1](sent)))
            if filled is not None:
                filled.append(made)
        for m, part in zip(members, arrived):
            held[m] = part
    return held + [lax.ppermute(part, "dp", twin) for part in held]


def after(value, *others):
    return lax.optimization_barrier((value, others))[0]


def total_of(terms):
    return sum(term.astype(F32) for term in terms)


def scatter_tail(terms, stages, waits):
    for place, pairs in enumerate(reversed(stages)):
        split = len(terms) // 2
        sent = [total_of(those).astype(BF16) for those in terms[split:]]
        got = [lax.ppermute(part, "dp", pairs) for part in sent]
        if place < len(waits):
            got = waits[place](sent, got)
        terms = [[*those, one] for those, one in zip(terms, got)]
    return total_of(terms[0])


def scatter_rows(make, count, wait):
    stages, twin = plane_stages(lax.axis_size("dp"))
    quarter = count // 4
    theirs = make([3], quarter, ())[0]
    there = lax.ppermute(theirs, "dp", twin)
    far = make([1], quarter, (theirs,))[0]
    sent = [total_of([far[k], there[k]]).astype(BF16) for k in range(quarter)]
    got = [lax.ppermute(part, "dp", stages[-1]) for part in sent]
    split = quarter // 2
    theirs, near = make([2, 0], quarter, (sent,))
    theirs, near, got[split:] = lax.optimization_barrier((theirs, near, got[split:]))
    there = lax.ppermute(theirs, "dp", twin)
    terms = [[near[k], there[k], got[k]] for k in range(quarter)]
    return scatter_tail(terms, stages[:-1], [wait] if wait else [])


def beside(work):
    def wait(sent, got):
        return after(got, work(sent))

    return wait


def piece_order(count):
    stages, twin = plane_stages(count)
    orders = []
    for device in range(count):
        held, other = [device], [twin[device][1]]
        for pairs in stages:
            held = held + [pairs[place][1] for place in held]
            other = other + [pairs[place][1] for place in other]
        orders.append(held + other)
    return orders


def hand_on(value, steps):
    count = lax.axis_size("seq")
    first, last = (max(0, -steps), min(count, count - steps))
    return lax.ppermute(value, "seq", [(source, source + steps) for source in range(first, last)])


def scan_into(keep, entry, cum_ref, state_ref, backward):
    rows, width = keep.shape
    groups = rows // 8
    mult = keep.reshape(groups, 8, width)
    total = entry.reshape(groups, 8, width)
    place = lax.broadcasted_iota(jnp.int32, (groups, 8, width), 1)
    for hop in (1, 2, 4):
        if backward:
            shift, valid = 8 - hop, place < 8 - hop
        else:
            shift, valid = hop, place >= hop
        near_mult = pltpu.roll(mult, shift, 1)
        near_total = pltpu.roll(total, shift, 1)
        total = jnp.where(valid, total + mult * near_total, total)
        mult = jnp.where(valid, mult * near_mult, mult)
    carry_total = jnp.zeros((1, width), F32)
    carry_mult = jnp.ones((1, width), F32)
    edge = 0 if backward else 7
    order = range(groups - 1, -1, -1) if backward else range(groups)
    for group in order:
        now_total = total[group] + mult[group] * carry_total
        now_mult = mult[group] * carry_mult
        state_ref[0, group * 8 : group * 8 + 8, :] = now_total
        cum_ref[0, group * 8 : group * 8 + 8, :] = now_mult
        carry_total = now_total[edge : edge + 1]
        carry_mult = now_mult[edge : edge + 1]
    return carry_mult, carry_total


def folded(refs):
    carry = refs[-1][0, 1:2, :]
    for ref in refs[-2::-1]:
        carry = ref[0, 1:2, :] + ref[0, 0:1, :] * carry
    return carry


def ends_block(mult, total):
    width = mult.shape[1]
    return jnp.concatenate([mult, total, jnp.zeros((6, width), F32)], 0)


def fetch_all(refs, buf, sems):
    for index, ref in enumerate(refs):
        pltpu.make_async_copy(ref, buf.at[index], sems.at[index]).start()


def fetched(refs, buf, sems, index):
    pltpu.make_async_copy(refs[0], buf.at[index], sems.at[index]).wait()


def put(buf, whole, sems, index):
    return pltpu.make_async_copy(buf.at[index], whole.at[index], sems.at[index])


def padded_rows(rows, width):
    missing = width - rows.shape[0]
    return jnp.concatenate([rows, jnp.zeros((missing, rows.shape[1]), rows.dtype)], 0) if missing else rows


def first_norm_kernel(count, *refs):
    x_refs, top_refs = refs[:count], refs[count : 2 * count]
    gain, all_out, h_out, m_out, buf, top, sems, top_sems = refs[2 * count :]
    step = pl.program_id(0)

    @pl.when(step == 0)
    def _():
        fetch_all(top_refs, top, top_sems)
        fetch_all(x_refs, buf, sems)

    fetched(top_refs, top, top_sems, step)
    fetched(x_refs, buf, sems, step)
    rows, width = m_out.shape[1:]
    top_val = top[step].astype(F32)
    info = jnp.broadcast_to(top_val[0:1, :rows], (width, rows)).astype(BF16)
    across = lax.broadcasted_iota(jnp.int32, (rows, rows), 0)
    down = lax.broadcasted_iota(jnp.int32, (rows, rows), 1)
    m_out[0] = dot_nt(jnp.where(across == down, 1.0, 0.0).astype(BF16), info).astype(BF16)
    all_out[0, :HALO] = rms_norm(top_val, gain[...]).astype(BF16)
    h_low = rms_norm(buf[step].astype(F32), gain[...]).astype(BF16)
    all_out[0, HALO:] = h_low
    h_out[0] = h_low


def first_norm(pieces, tops, gain, width):
    count = len(pieces)
    rows, model = pieces[0].shape
    shapes = [
        jax.ShapeDtypeStruct((count, rows + HALO, model), BF16),
        jax.ShapeDtypeStruct((count, rows, model), BF16),
        jax.ShapeDtypeStruct((count, rows, width), BF16),
    ]
    return call(
        functools.partial(first_norm_kernel, count),
        (count,),
        [ANY] * (2 * count) + [resident(gain.shape)],
        [per_piece(s.shape[1:]) for s in shapes],
        shapes,
        [
            pltpu.VMEM((count, rows, model), BF16),
            pltpu.VMEM((count, HALO, model), BF16),
            pltpu.SemaphoreType.DMA((count,)),
            pltpu.SemaphoreType.DMA((count,)),
        ],
        count * rows * model * 8,
        count * rows * model * 6,
    )(*pieces, *tops, gain)


def mixer_enter_kernel(
    h_ref, m_ref, wu, wy, wz, par, u_out, y_out, conv_out, r_out, e_out, k_out, a_out, s_out, ends, wu_all, wy_all
):
    width = wz.shape[1]

    @pl.when(pl.program_id(0) == 0)
    def _():
        wu_all[...] = padded_rows(wu[...], width)
        wy_all[...] = padded_rows(wy[...], width)

    h_low = h_ref[0]
    rows = h_low.shape[0] - HALO
    u_low = dot_nt(h_low, wu_all[...]).astype(BF16)
    u_out[0] = u_low
    y_out[0] = dot_nt(h_low[HALO:], wy_all[...])
    same = m_ref[0].astype(F32)
    u_val = u_low.astype(F32)
    conv = par[4:5, :] + par[0:1, :] * u_val[HALO:]
    for back in (1, 2, 3):
        term = par[back : back + 1, :] * u_val[HALO - back : HALO - back + rows]
        conv = conv + jnp.where(same >= back, term, 0.0)
    conv_low = conv.astype(BF16)
    conv_out[0] = conv_low
    conv = conv_low.astype(F32)
    pre = dot_nt(conv_low, wz[...])
    recur = jax.nn.sigmoid(pre[:, :width] + par[5:6, :])
    enter = jax.nn.sigmoid(pre[:, width:] + par[6:7, :])
    keep = jnp.where(same >= 1.0, jnp.exp(par[7:8, :] * recur), 0.0)
    r_out[0] = recur
    e_out[0] = enter
    k_out[0] = keep
    inputs = conv * enter * jnp.sqrt(jnp.maximum(1.0 - keep * keep, FLOOR))
    mult, total = scan_into(keep, inputs, a_out, s_out, False)
    ends[0] = ends_block(mult, total)


def resident(shape):
    zeros = (0,) * len(shape)
    return pl.BlockSpec(shape, lambda step: zeros)


def per_piece(shape, first=0):
    rest = (0,) * len(shape)
    return pl.BlockSpec((1,) + shape, lambda step: (step + first,) + rest)


def call(kernel, grid, in_specs, out_specs, out_shape, scratch, flops, moved):
    return pl.pallas_call(
        kernel,
        grid=grid,
        in_specs=in_specs,
        out_specs=out_specs,
        out_shape=out_shape,
        scratch_shapes=scratch,
        compiler_params=pltpu.CompilerParams(
            vmem_limit_bytes=VMEM_LIMIT, dimension_semantics=("arbitrary",) * len(grid)
        ),
        cost_estimate=pl.CostEstimate(flops=int(flops), bytes_accessed=int(moved), transcendentals=0),
    )


def mixer_enter(h_all, same, w_in, wz, par):
    count, tall, model = h_all.shape
    rows = tall - HALO
    chan = w_in.shape[0]
    width = wz.shape[1]

    def out(height, columns, dtype):
        return jax.ShapeDtypeStruct((count, height, columns), dtype)

    shapes = [out(tall, width, BF16), out(rows, width, F32), out(rows, width, BF16)]
    shapes += [out(rows, width, F32)] * 5 + [out(8, width, F32)]
    return call(
        mixer_enter_kernel,
        (count,),
        [
            per_piece((tall, model)),
            per_piece((rows, width)),
            pl.BlockSpec((chan, model), lambda step: (0, 0)),
            pl.BlockSpec((chan, model), lambda step: (0, 1)),
            resident(wz.shape),
            resident(par.shape),
        ],
        [per_piece(s.shape[1:]) for s in shapes],
        shapes,
        [pltpu.VMEM((width, model), BF16), pltpu.VMEM((width, model), BF16)],
        2 * count * rows * model * width * 2,
        count * rows * (model * 2 + width * 32),
    )(h_all, same, w_in, w_in, wz, par)


def column_tile(model):
    return next(t for t in (512, 256, 128) if model % t == 0)


def group_of(shape, blocks, pieces):
    first, stride = blocks[0], (blocks[-1] - blocks[0]) // max(1, len(blocks) - 1)
    rest = (0,) * len(shape)
    return pl.BlockSpec((pieces,) + shape, lambda group, step: (first + stride * group,) + rest)


def group_outs(rows, tile, steps, blocks, pieces):
    def spec(place):
        def index(group, step):
            at = jnp.clip((group - place) * steps + step, 0, steps - 1)
            return (0, 0, at)

        return pl.BlockSpec((pieces, rows, tile), index)

    return [spec(place) for place in range(len(blocks))]


def put_group(outs, total):
    for place, out in enumerate(outs):

        @pl.when(pl.program_id(0) == place)
        def _(out=out):
            out[...] = total.reshape(out.shape)


def fold_piece(refs, index):
    carry = refs[-1][index, 1:2, :]
    for ref in refs[-2::-1]:
        carry = ref[index, 1:2, :] + ref[index, 0:1, :] * carry
    return carry


def mixer_leave_kernel(hops, pieces, groups, *refs):
    ends = refs[:hops]
    cum, local, y_pre, w_out = refs[hops : hops + 4]
    mixed = refs[-1]
    rows = cum.shape[1]

    @pl.when(pl.program_id(1) == 0)
    def _():
        for index in range(pieces):
            states = local[index] + cum[index] * fold_piece(ends, index)
            mixed[index * rows : index * rows + rows, :] = (gelu_value(y_pre[index]) * states).astype(BF16)

    right = padded_rows(w_out[...], mixed.shape[1])
    put_group(refs[hops + 4 : hops + 4 + groups], dot_nn(mixed[...], right).astype(BF16))


def mixer_leave(ends, cum, local, y_pre, w_out, blocks, pieces):
    rows, width = cum.shape[1:]
    model = w_out.shape[1]
    tile = column_tile(model)
    steps = model // tile
    groups = len(blocks)
    return call(
        functools.partial(mixer_leave_kernel, len(ends), pieces, groups),
        (groups, steps),
        [group_of((8, width), blocks, pieces)] * len(ends)
        + [group_of((rows, width), blocks, pieces)] * 3
        + [pl.BlockSpec((w_out.shape[0], tile), lambda group, step: (0, step))],
        group_outs(rows, tile, steps, blocks, pieces),
        [jax.ShapeDtypeStruct((pieces, rows, model), BF16)] * groups,
        [pltpu.VMEM((pieces * rows, width), BF16)],
        2 * groups * pieces * rows * width * model,
        groups * pieces * rows * (width * 12 + model * 2),
    )(*ends, cum, local, y_pre, w_out)


def head_back_kernel(count, hops, *refs):
    d_refs = refs[:count]
    ends = refs[count : count + hops]
    (cum, local, y_pre, keep_ref, w_out, dy_out, mixed_out, cb_out, lb_out, ends_out, all_out, buf, w_all, sems, all_sems) = refs[count + hops :]
    step = pl.program_id(0)

    @pl.when(step == 0)
    def _():
        fetch_all(d_refs, buf, sems)
        w_all[...] = padded_rows(w_out[...], w_all.shape[0])

    fetched(d_refs, buf, sems, step)
    put(buf, all_out, all_sems, step).start()
    d_mixed = dot_nt(buf[step], w_all[...])
    states = local[0] + cum[0] * folded(ends)
    value, slope = gelu_parts(y_pre[0])
    mixed_out[0] = (value * states).astype(BF16)
    dy_out[0] = (slope * d_mixed * states).astype(BF16)
    keep = keep_ref[0]
    width = keep.shape[1]
    next_keep = jnp.concatenate([keep[1:], jnp.ones((1, width), F32)], 0)
    mult, total = scan_into(next_keep, d_mixed * value, cb_out, lb_out, True)
    ends_out[0] = ends_block(mult * keep[0:1], total * keep[0:1])

    @pl.when(step == count - 1)
    def _():
        for index in range(count):
            put(buf, all_out, all_sems, index).wait()


def head_back(pieces, ends, cum, local, y_pre, keep, w_out):
    count = len(pieces)
    rows, model = pieces[0].shape
    width = cum.shape[2]

    def out(height, dtype):
        return jax.ShapeDtypeStruct((count, height, width), dtype)

    shapes = [out(rows, BF16), out(rows, BF16), out(rows, F32), out(rows, F32), out(8, F32)]
    return call(
        functools.partial(head_back_kernel, count, len(ends)),
        (count,),
        [ANY] * count
        + [per_piece((8, width))] * len(ends)
        + [per_piece((rows, width))] * 4
        + [resident(w_out.shape)],
        [per_piece(s.shape[1:]) for s in shapes] + [ANY],
        shapes + [jax.ShapeDtypeStruct((count, rows, model), BF16)],
        [
            pltpu.VMEM((count, rows, model), BF16),
            pltpu.VMEM((width, model), BF16),
            pltpu.SemaphoreType.DMA((count,)),
            pltpu.SemaphoreType.DMA((count,)),
        ],
        2 * count * rows * width * model,
        count * rows * (width * 28 + model * 2),
    )(*pieces, *ends, cum, local, y_pre, keep, w_out)


def tail_back_kernel(hops, *refs):
    ends = refs[:hops]
    later = refs[hops : 2 * hops]
    (cb, lb, cum, local, r_ref, e_ref, k_ref, conv_ref, u_ref, m_ref, wz, par, du_out, edge_out, fold_out, small_out, gw_out) = refs[2 * hops :]
    step = pl.program_id(0)

    @pl.when(step == 0)
    def _():
        gw_out[...] = jnp.zeros_like(gw_out)
        small_out[...] = jnp.zeros_like(small_out)

    state_in = folded(ends)
    d_states = lb[0] + cb[0] * folded(later)
    states = local[0] + cum[0] * state_in
    prev = jnp.concatenate([state_in, states[:-1]], 0)
    recur, enter, keep = r_ref[0], e_ref[0], k_ref[0]
    conv_low = conv_ref[0]
    conv = conv_low.astype(F32)
    rows, width = conv.shape
    spare = 1.0 - keep * keep
    scaling = jnp.sqrt(jnp.maximum(spare, FLOOR))
    weight = jnp.where(spare > FLOOR, 0.5, jnp.where(spare == FLOOR, 0.25, 0.0)) / scaling
    d_enter_sum = d_states * conv
    d_spare = d_enter_sum * enter * weight
    d_expo = (d_states * prev - 2.0 * keep * d_spare) * keep
    d_recur = d_expo * par[7:8, :] * recur * (1.0 - recur)
    d_enter = d_enter_sum * scaling * enter * (1.0 - enter)
    d_pre = jnp.concatenate([d_recur.astype(BF16), d_enter.astype(BF16)], 1)
    d_conv = d_states * enter * scaling + dot_nn(d_pre, wz[...])
    gw_out[...] += dot_tn(d_pre, conv_low)
    d_pre_val = d_pre.astype(F32)
    same = m_ref[0].astype(F32)
    u_val = u_ref[0].astype(F32)
    sums = []
    d_u = jnp.zeros((rows, width), F32)
    head = jnp.zeros((8, width), F32)
    for back in range(4):
        masked = d_conv if back == 0 else jnp.where(same >= back, d_conv, 0.0)
        sums.append(jnp.sum(masked * u_val[HALO - back : HALO - back + rows], axis=0, keepdims=True))
        moved = masked * par[back : back + 1, :]
        if back == 0:
            d_u = d_u + moved
        else:
            nothing = jnp.zeros((back, width), F32)
            d_u = d_u + jnp.concatenate([moved[back:], nothing], 0)
            head = head + jnp.concatenate([jnp.zeros((8 - back, width), F32), moved[:back]], 0)
    sums.append(jnp.sum(d_conv, axis=0, keepdims=True))
    sums.append(jnp.sum(d_pre_val[:, :width], axis=0, keepdims=True))
    sums.append(jnp.sum(d_pre_val[:, width:], axis=0, keepdims=True))
    sums.append(jnp.sum(d_expo * recur, axis=0, keepdims=True))
    small_out[...] += jnp.concatenate(sums, 0)
    du_out[0] = d_u.astype(BF16)
    edge_out[0, 0:8, :] = head
    edge_out[0, 8:16, :] = d_u[rows - 8 :]

    @pl.when(step == pl.num_programs(0) - 1)
    def _():
        block = fold_out.shape[1]
        row = lax.broadcasted_iota(jnp.int32, (width, width), 0)
        column = lax.broadcasted_iota(jnp.int32, (width, width), 1)
        inside = None
        for start in range(0, width, block):
            here = (row >= start) & (row < start + block) & (column >= start) & (column < start + block)
            inside = here if inside is None else inside | here
        row = lax.broadcasted_iota(jnp.int32, (width, block), 0)
        column = lax.broadcasted_iota(jnp.int32, (width, block), 1)
        fold = None
        for start in range(0, width, block):
            here = row - start == column
            fold = here if fold is None else fold | here
        fold = jnp.where(fold, 1.0, 0.0).astype(BF16)
        for gate in (0, 1):
            whole = jnp.where(inside, gw_out[gate * width : gate * width + width, :], 0.0).astype(BF16)
            fold_out[gate * width : gate * width + width, :] = dot_nn(whole, fold).astype(BF16)


def tail_back(ends, later, cb, lb, cum, local, recur, enter, keep, conv, u_ext, same, wz, par, block):
    count, rows, width = cb.shape
    shapes = [
        jax.ShapeDtypeStruct((count, rows, width), BF16),
        jax.ShapeDtypeStruct((count, 16, width), F32),
        jax.ShapeDtypeStruct((2 * width, block), BF16),
        jax.ShapeDtypeStruct((8, width), F32),
    ]
    tall = u_ext.shape[1]
    return call(
        functools.partial(tail_back_kernel, len(ends)),
        (count,),
        [per_piece((8, width))] * (2 * len(ends))
        + [per_piece((rows, width))] * 8
        + [per_piece((tall, width)), per_piece((rows, width)), resident(wz.shape), resident(par.shape)],
        [per_piece((rows, width)), per_piece((16, width)), resident((2 * width, block)), resident((8, width))],
        shapes,
        [pltpu.VMEM(wz.shape, F32)],
        8 * count * rows * width * width,
        count * rows * width * 36,
    )(*ends, *later, cb, lb, cum, local, recur, enter, keep, conv, u_ext, same, wz, par)


def rows_times_kernel(terms, gained, *refs):
    lefts, rights = refs[:terms], refs[terms : 2 * terms]
    outs = refs[2 * terms + gained :]
    total = None
    for left, right in zip(lefts, rights):
        pieces, rows, inner = left.shape
        term = dot_nn(left[...].reshape(pieces * rows, inner), padded_rows(right[...], inner))
        total = term if total is None else total + term
    if gained:
        factor = refs[2 * terms][...].reshape(total.shape).astype(F32)
        outs[-1][0] = jnp.sum(total * factor, axis=0, keepdims=True)
        outs = outs[:-1]
    put_group(outs, total.astype(BF16))


def rows_times(lefts, rights, blocks, pieces, factor=None):
    rows = lefts[0].shape[1]
    model = rights[0][2]
    tile = column_tile(model)
    steps = model // tile
    groups = len(blocks)
    inner = sum(right.shape[0] for right, _, _ in rights)
    gained = 0 if factor is None else 1

    def right_spec(right, place):
        return pl.BlockSpec((right.shape[0], tile), lambda group, step: (0, place * steps + step))

    out_specs = group_outs(rows, tile, steps, blocks, pieces)
    shapes = [jax.ShapeDtypeStruct((pieces, rows, model), BF16)] * groups
    extra_specs = []
    if gained:
        first, stride = blocks[0], (blocks[-1] - blocks[0]) // max(1, groups - 1)
        out_specs.append(pl.BlockSpec((1, 1, tile), lambda group, step: (group, 0, step)))
        shapes.append(jax.ShapeDtypeStruct((groups, 1, model), F32))
        extra_specs.append(
            pl.BlockSpec((pieces, rows, tile), lambda group, step: (first + stride * group, 0, step))
        )
    return call(
        functools.partial(rows_times_kernel, len(lefts), gained),
        (groups, steps),
        [group_of(left.shape[1:], blocks, pieces) for left in lefts]
        + [right_spec(right, place) for right, place, _ in rights]
        + extra_specs,
        out_specs,
        shapes,
        [],
        2 * groups * pieces * rows * inner * model,
        groups * pieces * rows * 2 * (inner + model) + 2 * inner * model,
    )(*lefts, *[right for right, _, _ in rights], *([factor] if gained else []))


def assemble_kernel(count, *refs):
    parts, whole, buf, sems, all_sems = refs[:count], refs[count], *refs[count + 1 :]
    fetch_all(parts, buf, sems)
    for index in range(count):
        fetched(parts, buf, sems, index)
        put(buf, whole, all_sems, index).start()
    for index in range(count):
        put(buf, whole, all_sems, index).wait()


def assemble(pieces):
    count = len(pieces)
    shape = (count,) + pieces[0].shape
    return call(
        functools.partial(assemble_kernel, count),
        (1,),
        [ANY] * count,
        ANY,
        jax.ShapeDtypeStruct(shape, pieces[0].dtype),
        [pltpu.VMEM(shape, pieces[0].dtype), pltpu.SemaphoreType.DMA((count,)), pltpu.SemaphoreType.DMA((count,))],
        0,
        4 * count * pieces[0].size,
    )(*pieces)


def mlp_enter_kernel(count, *refs):
    h_refs = refs[:count]
    wg, wu, hid_out, turn_out, value_out, all_out, buf, sems, all_sems = refs[count:]
    step = pl.program_id(0)
    pair = 2 if count % 2 == 0 else 1
    rows, tile = hid_out.shape[1:]

    @pl.when(step == 0)
    def _():
        fetch_all(h_refs, buf, sems)

    def some_pieces(index, carry):
        @pl.when(step == 0)
        def _():
            for place in range(pair):
                fetched(h_refs, buf, sems, index * pair + place)
                put(buf, all_out, all_sems, index * pair + place).start()

        span = pl.ds(index * pair, pair)
        h_low = buf[span].reshape(pair * rows, buf.shape[2])
        gate = dot_nt(h_low, wg[...])
        up = dot_nt(h_low, wu[...])
        value, slope = gelu_parts(gate)
        shape = (pair, rows, tile)
        hid_out[span] = (value * up).astype(BF16).reshape(shape)
        turn_out[span] = (up * slope).reshape(shape)
        value_out[span] = value.reshape(shape)
        return carry

    lax.fori_loop(0, count // pair, some_pieces, 0)

    @pl.when(step == pl.num_programs(0) - 1)
    def _():
        for index in range(count):
            put(buf, all_out, all_sems, index).wait()


def hidden_tile(hidden):
    return next(t for t in (256, 128, hidden) if hidden % t == 0)


def mlp_enter(h_pieces, w_both):
    count = len(h_pieces)
    rows, model = h_pieces[0].shape
    hidden = w_both.shape[0]
    tile = hidden_tile(hidden)
    out_spec = pl.BlockSpec((count, rows, tile), lambda step: (0, 0, step))
    return call(
        functools.partial(mlp_enter_kernel, count),
        (hidden // tile,),
        [ANY] * count
        + [pl.BlockSpec((tile, model), lambda step: (step, 0)), pl.BlockSpec((tile, model), lambda step: (step, 1))],
        [out_spec] * 3 + [ANY],
        [
            jax.ShapeDtypeStruct((count, rows, hidden), BF16),
            jax.ShapeDtypeStruct((count, rows, hidden), F32),
            jax.ShapeDtypeStruct((count, rows, hidden), F32),
            jax.ShapeDtypeStruct((count, rows, model), BF16),
        ],
        [
            pltpu.VMEM((count, rows, model), BF16),
            pltpu.SemaphoreType.DMA((count,)),
            pltpu.SemaphoreType.DMA((count,)),
        ],
        4 * count * rows * model * hidden,
        count * rows * (4 * model + 10 * hidden) + 4 * model * hidden,
    )(*h_pieces, w_both, w_both)


def mlp_back_kernel(c_ref, wo, turn, value, dg_out, du_out):
    count, rows, tile = dg_out.shape
    pair = 2 if count % 2 == 0 else 1

    def some_pieces(index, carry):
        span = pl.ds(index * pair, pair)
        d_hidden = dot_nt(c_ref[span].reshape(pair * rows, c_ref.shape[2]), wo[...])
        d_hidden = d_hidden.reshape(pair, rows, tile)
        dg_out[span] = (d_hidden * turn[span]).astype(BF16)
        du_out[span] = (d_hidden * value[span]).astype(BF16)
        return carry

    lax.fori_loop(0, count // pair, some_pieces, 0)


def mlp_back(c_all, w_down, turn, value):
    count, rows, model = c_all.shape
    hidden = w_down.shape[0]
    tile = hidden_tile(hidden)
    spec = pl.BlockSpec((count, rows, tile), lambda step: (0, 0, step))
    return call(
        mlp_back_kernel,
        (hidden // tile,),
        [resident(c_all.shape), pl.BlockSpec((tile, model), lambda step: (step, 0)), spec, spec],
        [spec] * 2,
        [jax.ShapeDtypeStruct((count, rows, hidden), BF16)] * 2,
        [],
        2 * count * rows * model * hidden,
        count * rows * (2 * model + 12 * hidden) + 2 * model * hidden,
    )(c_all, w_down, turn, value)


def weight_grad(rows_left, rows_right):
    left = rows_left.reshape(-1, rows_left.shape[-1])
    right = rows_right.reshape(-1, rows_right.shape[-1])
    return dot_tn(left, right).astype(BF16)


def seq_gather(shard):
    return lax.all_gather(shard, "seq", axis=0, tiled=True)


def seq_scatter(whole):
    return lax.psum_scatter(whole, "seq", scatter_dimension=0, tiled=True)


def per_device(
    tokens,
    cotangent,
    doc_ids,
    mix_in,
    mix_out,
    gate_w,
    conv_w,
    conv_bias,
    gate_bias,
    decay_param,
    gain_one,
    gain_two,
    mlp_in,
    mlp_out,
):
    run_len, model = tokens.shape[1:]
    n_seq = lax.axis_size("seq")
    n_dev = lax.axis_size("dp") * n_seq
    own = mix_out.shape[0]
    block = gate_w.shape[2]
    chan = own * n_seq
    width = -(-chan // 128) * 128
    blocks = chan // block

    x_low = tokens.reshape(run_len, model)
    x_pieces = gather_rows(x_low)
    x_zero = x_low.astype(F32)
    cot_low = cotangent.reshape(run_len, model)
    lead = hand_on(x_low[run_len - HALO :], 1)
    part = gain_one.shape[0]
    gains = jnp.concatenate([gain_one, gain_two]).astype(BF16)[None]
    my_run = lax.axis_index("seq")
    first_token = my_run * run_len
    places = lax.broadcasted_iota(jnp.int32, (n_seq, 1), 0)
    gain_rows = jnp.where(places == my_run, gains, jnp.zeros((), BF16))
    for hop in range(1, n_seq):
        ring = [(source, (source + hop) % n_seq) for source in range(n_seq)]
        arrived = lax.ppermute(gains, "seq", ring)
        gain_rows = jnp.where(places == (my_run - hop) % n_seq, arrived, gain_rows)
    gain_rows = jnp.pad(gain_rows.reshape(1, -1), ((0, 0), (0, model - 2 * part * n_seq)))
    padded = jnp.concatenate([jnp.full((3,), -1, jnp.int32), doc_ids.reshape(-1)])
    own_docs = lax.dynamic_slice_in_dim(padded, first_token + 3, run_len)
    same = sum(
        jnp.where(lax.dynamic_slice_in_dim(padded, first_token + 3 - back, run_len) == own_docs, 1.0, 0.0)
        for back in (1, 2, 3)
    )
    info = jnp.pad(same, (0, model - run_len)).astype(BF16)[None]
    tops = gather_rows(jnp.concatenate([info, gain_rows, lead[2:]], 0))
    count = len(tops)
    half = count // 2

    small = jnp.concatenate(
        [
            gate_w.reshape(own, 2 * block),
            conv_w.T,
            conv_bias[:, None],
            gate_bias.T,
            decay_param[:, None],
        ],
        1,
    )
    extra = -(-small.shape[1] // 128) * 128
    small = jnp.pad(small, ((0, 0), (0, extra - small.shape[1])))
    w_in = seq_gather(jnp.concatenate([mix_in[:, 1, :], mix_in[:, 0, :], small], 1).astype(BF16))
    w_out = seq_gather(mix_out.astype(BF16))
    mlp_in, mlp_out = after((mlp_in, mlp_out), lead)
    both_shard = mlp_in.astype(BF16).reshape(-1, 2 * model)
    down_shard = mlp_out.astype(BF16)
    w_both = seq_gather(both_shard)
    w_down = seq_gather(down_shard)

    w_small = w_in[:, 2 * model :]
    gate_rows = w_small[:, : 2 * block].reshape(blocks, block, 2, block)
    eye = jnp.eye(blocks, dtype=BF16)
    w_z = jnp.einsum("bogj,bc->gbocj", gate_rows, eye).reshape(2, chan, chan)
    w_z = jnp.pad(w_z, ((0, 0), (0, width - chan), (0, width - chan))).reshape(2 * width, width)
    par = w_small[:, 2 * block : 2 * block + 8].astype(F32).T
    decay_rate = -SHARP * jax.nn.softplus(par[7])
    decay_slope = -SHARP * jax.nn.sigmoid(par[7])
    par = jnp.pad(jnp.concatenate([par[:7], decay_rate[None]], 0), ((0, 0), (0, width - chan)))

    orders = jnp.asarray(piece_order(count), jnp.int32)
    order = lax.dynamic_index_in_dim(after(orders, lead), lax.axis_index("dp"), 0, False)
    places = lax.broadcasted_iota(jnp.int32, (count, 1), 0)
    gain_rows = jnp.zeros((count, 2 * part * n_seq), F32)
    for index, piece in enumerate(tops):
        row = piece[1:2, : 2 * part * n_seq].astype(F32)
        gain_rows = jnp.where(places == order[index], row, gain_rows)
    gain_rows = gain_rows.reshape(n_dev, 2 * part)
    g_one = gain_rows[:, :part].reshape(1, model)
    g_two = gain_rows[:, part:].reshape(1, model)

    h_all, h_one, same = first_norm(x_pieces, tops, g_one, width)
    entered = mixer_enter(after(h_all, both_shard, down_shard), same, w_in, w_z, par)
    (u_ext, y_pre, conv, recur, enter, keep, cum, local, ends) = entered
    c_pieces = gather_rows(after(cot_low, *x_pieces), [lambda sent: ends])
    ends = after(ends, w_out)
    earlier = [hand_on(ends, steps) for steps in range(1, n_seq)]
    earlier, c_pieces = lax.optimization_barrier((earlier, c_pieces[:half])), c_pieces
    earlier, c_pieces[:half] = earlier

    def leaving(blocks_at, pieces, before):
        return mixer_leave(earlier, cum, local, after(y_pre, *before), w_out, blocks_at, pieces)

    kept = []
    x_one = x_zero + scatter_rows(leaving, count, None)
    n_two, norm_two_back = jax.vjp(rms_norm, x_one, g_two)
    h_two = n_two.astype(BF16)

    h_pieces = gather_rows(h_two, [lambda sent: assemble(after(c_pieces, *sent))], kept)
    c_all = kept.pop()
    hidden, turn, value, h_all = mlp_enter(h_pieces, w_both)
    grad_down = weight_grad(hidden, c_all)
    turn = after(turn, grad_down)
    grad_down = seq_scatter(grad_down)
    d_gate, d_up = mlp_back(c_all, w_down, turn, value)

    def d_entering(blocks_at, pieces, before):
        d_one = after(d_gate, *before)
        return rows_times([d_one, d_up], [(w_both, 0, model), (w_both, 1, model)], blocks_at, pieces)

    def gate_grad(sent):
        kept.append(weight_grad(after(d_gate, sent), h_all))
        return kept[-1]

    def up_grad(sent):
        kept.append(weight_grad(after(d_up, sent), h_all))
        return kept[-1]

    d_h_two = scatter_rows(d_entering, count, beside(gate_grad))
    grad_gate = seq_scatter(kept[-1])
    d_x_norm, d_gain_two = norm_two_back(d_h_two)
    d_x_one = cot_low.astype(F32) + d_x_norm
    d_mix = d_x_one.astype(BF16)

    def mlp_leaving(blocks_at, pieces, before):
        return rows_times([after(hidden, *before)], [(w_down, 0, model)], blocks_at, pieces)

    stages, twin = plane_stages(lax.axis_size("dp"))

    def mlp_out_rows(sent):
        nonlocal hidden
        hidden = after(hidden, sent)
        return mlp_leaving([1, 0], half, ())

    def up_grad_and_sums(sent):
        theirs, mine = kept.pop()
        there = lax.ppermute(theirs, "dp", twin)
        far = [total_of([mine[k], there[k]]).astype(BF16) for k in range(half // 2, half)]
        kept.append((mine, there, far))
        return up_grad(sent), far

    d_pieces = gather_rows(d_mix, [mlp_out_rows, up_grad_and_sums], kept)
    kept.pop()
    grad_up = kept.pop()
    mine, there, far = kept.pop()
    d_y, mixed, cum_back, local_back, ends_back, d_all = head_back(
        after(d_pieces, far), earlier, cum, local, y_pre, keep, w_out
    )
    got = [lax.ppermute(part, "dp", stages[-1]) for part in far]
    ends_back, got = lax.optimization_barrier((ends_back, got))
    later = [hand_on(ends_back, -steps) for steps in range(1, n_seq)]
    grad_y = weight_grad(after(d_y, ends_back), h_one)[:chan]
    grad_out = weight_grad(after(mixed, ends_back), d_all)[:chan]
    grad_y_out = jnp.concatenate([grad_y, grad_out], 1)
    later, grad_y_out = lax.optimization_barrier((later, grad_y_out))
    grad_up = seq_scatter(grad_up)
    grad_y_out = seq_scatter(grad_y_out)

    def tail_work(sent, got):
        nonlocal tailed
        tailed = tail_back(
            earlier, after(later, sent), cum_back, local_back, cum, local, recur, enter, keep, conv, u_ext, same, w_z, par, block
        )
        tailed, got = lax.optimization_barrier((tailed, got))
        return got

    tailed = None
    terms = [[mine[k], there[k], got[k]] for k in range(half // 2)]
    layer_out = x_one + scatter_tail(terms, stages[:-1], [tail_work])
    layer_out = layer_out.astype(BF16).reshape(1, run_len, model)
    d_u, edges, grad_z, sums = tailed
    from_next = hand_on(edges[:, :8], -1)
    grad_z = jnp.concatenate([grad_z[:chan], grad_z[width : width + chan]], 1)
    sums = sums[:, :chan]
    sums = jnp.concatenate([sums[:7], (sums[7] * decay_slope)[None]], 0).T
    tail = jnp.concatenate([grad_z, sums.astype(BF16)], 1)
    tail = jnp.pad(tail, ((0, 0), (0, extra - tail.shape[1])))
    from_next, layer_out = lax.optimization_barrier((from_next, layer_out))
    d_u = lax.dynamic_update_slice(d_u, (edges[:, 8:] + from_next).astype(BF16), (0, run_len - 8, 0))
    gain_terms = []

    def d_leaving(blocks_at, pieces, before):
        *part_rows, gain_term = rows_times(
            [after(d_y, *before), d_u], [(w_in, 1, model), (w_in, 0, model)], blocks_at, pieces, h_one
        )
        gain_terms.append(gain_term.sum(0))
        return part_rows

    def u_grad(sent):
        kept.append(weight_grad(after(d_u, sent, grad_down, grad_gate, grad_up, grad_y_out), h_one))
        return kept[-1]

    d_h_one = scatter_rows(d_leaving, count, beside(u_grad))
    grad_u = seq_scatter(jnp.concatenate([kept[-1][:chan], tail], 1))
    _, norm_one_back = jax.vjp(lambda values: rms_norm(values, g_one), x_zero)
    input_grad = (d_x_one + norm_one_back(d_h_one)[0]).astype(BF16)
    d_gain_one = sum(gain_terms) / g_one
    d_gains = jnp.concatenate([d_gain_one.reshape(n_dev, part), d_gain_two.reshape(n_dev, part)], 1)
    grads = lax.optimization_barrier((kept[-1], grad_gate, grad_up, grad_down, grad_y_out))[1:]
    rest = (d_gains, *grads)
    input_grad, rest = lax.optimization_barrier((input_grad, rest))
    (d_gains, grad_gate, grad_up, grad_down, grad_y_out) = rest
    input_grad = input_grad.reshape(1, run_len, model)
    d_gains = lax.all_to_all(d_gains, ("dp", "seq"), 0, 0, tiled=True).sum(0)

    tail = grad_u[:, model:].astype(F32)
    grad_mix_in = jnp.stack([grad_y_out[:, :model].astype(F32), grad_u[:, :model].astype(F32)], 1)
    at = 2 * block
    return (
        layer_out,
        input_grad,
        grad_mix_in,
        grad_y_out[:, model:].astype(F32),
        tail[:, :at].reshape(own, 2, block),
        tail[:, at : at + 4].T,
        tail[:, at + 4],
        tail[:, at + 5 : at + 7].T,
        tail[:, at + 7],
        d_gains[:part],
        d_gains[part:],
        jnp.stack([grad_gate.astype(F32), grad_up.astype(F32)], 1),
        grad_down.astype(F32),
    )


def solution(mesh):
    rows = P(("dp", "seq"))
    placed = (
        P("dp", "seq", None),
        P("dp", "seq", None),
        P("dp", None),
        P(("dp", "seq"), None, None),
        P(("dp", "seq"), None),
        P(("dp", "seq"), None, None),
        P(None, ("dp", "seq")),
        rows,
        P(None, ("dp", "seq")),
        rows,
        rows,
        rows,
        P(("dp", "seq"), None, None),
        P(("dp", "seq"), None),
    )
    return jax.shard_map(
        per_device,
        mesh=mesh,
        in_specs=placed,
        out_specs=placed[:2] + placed[3:],
        check_vma=False,
    )
```

```python
import functools

import jax
import jax.numpy as jnp
from jax import lax
from jax.experimental import pallas as pl
from jax.experimental.pallas import tpu as pltpu
from jax.sharding import PartitionSpec as P

EPS = 1e-06
FLOOR = 0.0001
SHARP = 8.0
HALO = 16
F32 = jnp.float32
BF16 = jnp.bfloat16
VMEM_LIMIT = 56 * 1024 * 1024
ANY = pl.BlockSpec(memory_space=pl.ANY)
ROOT = 0.7978845608028654
CUBE = 0.044715
SLOW = 4.5
RATE = 650e6
SWEEP = 25e-6


def dot_nt(left, right):
    return lax.dot_general(left, right, (((1,), (1,)), ((), ())), preferred_element_type=F32)


def dot_nn(left, right):
    return lax.dot_general(left, right, (((1,), (0,)), ((), ())), preferred_element_type=F32)


def dot_tn(left, right):
    return lax.dot_general(left, right, (((0,), (0,)), ((), ())), preferred_element_type=F32)


def rms_norm(values, gain_vec):
    return values * lax.rsqrt(jnp.mean(values * values, axis=-1, keepdims=True) + EPS) * gain_vec


def gelu_parts(values):
    squared = values * values
    bend = jnp.tanh(ROOT * (values + CUBE * values * squared))
    half = 0.5 * (1.0 + bend)
    slope = half + 0.5 * values * (1.0 - bend * bend) * (ROOT * (1.0 + 3.0 * CUBE * squared))
    return values * half, slope


def gelu_value(values):
    bend = jnp.tanh(ROOT * (values + CUBE * values * values * values))
    return values * (0.5 * (1.0 + bend))


def plane_stages(count):
    bits = count.bit_length() - 1
    upper = list(range(1, bits))
    stages = []
    for place in range(len(upper)):
        pairs = []
        for source in range(count):
            shift = place if source % 2 == 0 else (place + 1) % len(upper)
            pairs.append((source, source ^ (1 << upper[shift])))
        stages.append(pairs)
    twin = [(source, source ^ 1) for source in range(count)]
    return stages, twin


def gather_rows(piece, beside=()):
    stages, twin = plane_stages(lax.axis_size("dp"))
    held = [piece] + [None] * (2 ** len(stages) - 1)
    done = []
    before = ()

    def arrival(m):
        top = m.bit_length() - 1
        return lax.ppermute(held[m ^ (1 << top)], "dp", stages[top])

    for members, work in beside:
        arrived = [arrival(m) for m in members]
        sent = [held[m ^ (1 << (m.bit_length() - 1))] for m in members]
        arrived, made = lax.optimization_barrier((arrived, work((sent, before), done)))
        before = arrived
        done.append(made)
        for m, part in zip(members, arrived):
            held[m] = part
    for m in range(1, len(held)):
        if held[m] is None:
            held[m] = arrival(m)
    return held + [lax.ppermute(part, "dp", twin) for part in held], done


def after(value, *others):
    return lax.optimization_barrier((value, others))[0]


def total_of(terms):
    return sum(array[place].astype(F32) for array, place in terms)


def scatter_tail(terms, stages, waits):
    for place, pairs in enumerate(reversed(stages)):
        split = len(terms) // 2
        sent = add_rows(terms[split:])
        got = [lax.ppermute(part, "dp", pairs) for part in sent]
        if place < len(waits):
            got = waits[place](sent, got)
        terms = [[*those, (one[None], 0)] for those, one in zip(terms, got)]
    return terms[0]


def scatter_terms(make, count, wait, low_wait=None):
    stages, twin = plane_stages(lax.axis_size("dp"))
    quarter = count // 4
    theirs = make([3], quarter, ())[0]
    there = lax.ppermute(theirs, "dp", twin)
    far = make([1], quarter, (theirs,))[0]
    sent = add_rows([[(far, k), (there, k)] for k in range(quarter)])
    got = [lax.ppermute(part, "dp", stages[-1]) for part in sent]
    split = quarter // 2
    theirs, near = make([2, 0], quarter, (sent,))
    theirs, near, got[split:] = lax.optimization_barrier((theirs, near, got[split:]))
    there = lax.ppermute(theirs, "dp", twin)
    if low_wait is not None:
        got[:split] = low_wait(sent, got[:split])
    terms = [[(near, k), (there, k), (got[k][None], 0)] for k in range(quarter)]
    return scatter_tail(terms, stages[:-1], [wait] if wait else [])


def scatter_rows(make, count, wait):
    return total_of(scatter_terms(make, count, wait))


def beside(work, done):
    def wait(sent, got):
        got, made = lax.optimization_barrier((got, work(sent)))
        done.append(made)
        return got

    return wait


def piece_order(count):
    stages, twin = plane_stages(count)
    orders = []
    for device in range(count):
        held, other = [device], [twin[device][1]]
        for pairs in stages:
            held = held + [pairs[place][1] for place in held]
            other = other + [pairs[place][1] for place in other]
        orders.append(held + other)
    return orders


def hand_on(value, steps):
    count = lax.axis_size("seq")
    first, last = (max(0, -steps), min(count, count - steps))
    return lax.ppermute(value, "seq", [(source, source + steps) for source in range(first, last)])


def scan_into(keep, entry, cum_ref, state_ref, backward):
    rows, width = keep.shape
    groups = rows // 8
    mult = keep.reshape(groups, 8, width)
    total = entry.reshape(groups, 8, width)
    place = lax.broadcasted_iota(jnp.int32, (groups, 8, width), 1)
    for hop in (1, 2, 4):
        if backward:
            shift, valid = 8 - hop, place < 8 - hop
        else:
            shift, valid = hop, place >= hop
        near_mult = pltpu.roll(mult, shift, 1)
        near_total = pltpu.roll(total, shift, 1)
        total = jnp.where(valid, total + mult * near_total, total)
        mult = jnp.where(valid, mult * near_mult, mult)
    carry_total = jnp.zeros((1, width), F32)
    carry_mult = jnp.ones((1, width), F32)
    edge = 0 if backward else 7
    order = range(groups - 1, -1, -1) if backward else range(groups)
    for group in order:
        now_total = total[group] + mult[group] * carry_total
        now_mult = mult[group] * carry_mult
        state_ref[0, group * 8 : group * 8 + 8, :] = now_total
        cum_ref[0, group * 8 : group * 8 + 8, :] = now_mult
        carry_total = now_total[edge : edge + 1]
        carry_mult = now_mult[edge : edge + 1]
    return carry_mult, carry_total


def folded(refs, piece):
    at = pl.ds(piece, 1)
    carry = refs[-1][1, at, :]
    for ref in refs[-2::-1]:
        carry = ref[1, at, :] + ref[0, at, :] * carry
    return carry


def put_ends(ref, piece, mult, total):
    ref[0, pl.ds(piece, 1), :] = mult
    ref[1, pl.ds(piece, 1), :] = total


def fetch_all(refs, buf, sems):
    for index, ref in enumerate(refs):
        pltpu.make_async_copy(ref, buf.at[index], sems.at[index]).start()


def fetched(refs, buf, sems, index):
    pltpu.make_async_copy(refs[0], buf.at[index], sems.at[index]).wait()


def put(buf, whole, sems, index):
    return pltpu.make_async_copy(buf.at[index], whole.at[index], sems.at[index])


def padded_rows(rows, width):
    missing = width - rows.shape[0]
    return jnp.concatenate([rows, jnp.zeros((missing, rows.shape[1]), rows.dtype)], 0) if missing else rows


def first_norm_kernel(count, *refs):
    x_refs, top_refs = refs[:count], refs[count : 2 * count]
    gain, all_out, h_out, m_out, buf, top, sems, top_sems = refs[2 * count :]
    step = pl.program_id(0)

    @pl.when(step == 0)
    def _():
        fetch_all(top_refs, top, top_sems)
        fetch_all(x_refs, buf, sems)

    fetched(top_refs, top, top_sems, step)
    fetched(x_refs, buf, sems, step)
    rows, width = m_out.shape[1:]
    top_val = top[step].astype(F32)
    info = jnp.broadcast_to(top_val[0:1, :rows], (width, rows)).astype(BF16)
    across = lax.broadcasted_iota(jnp.int32, (rows, rows), 0)
    down = lax.broadcasted_iota(jnp.int32, (rows, rows), 1)
    m_out[0] = dot_nt(jnp.where(across == down, 1.0, 0.0).astype(BF16), info).astype(BF16)
    all_out[0, :HALO] = rms_norm(top_val, gain[...]).astype(BF16)
    h_low = rms_norm(buf[step].astype(F32), gain[...]).astype(BF16)
    all_out[0, HALO:] = h_low
    h_out[0] = h_low


def first_norm(pieces, tops, gain, width):
    count = len(pieces)
    rows, model = pieces[0].shape
    shapes = [
        jax.ShapeDtypeStruct((count, rows + HALO, model), BF16),
        jax.ShapeDtypeStruct((count, rows, model), BF16),
        jax.ShapeDtypeStruct((count, rows, width), BF16),
    ]
    return call(
        functools.partial(first_norm_kernel, count),
        (count,),
        [ANY] * (2 * count) + [resident(gain.shape)],
        [per_piece(s.shape[1:]) for s in shapes],
        shapes,
        [
            pltpu.VMEM((count, rows, model), BF16),
            pltpu.VMEM((count, HALO, model), BF16),
            pltpu.SemaphoreType.DMA((count,)),
            pltpu.SemaphoreType.DMA((count,)),
        ],
        2.6e-6 * count * rows * model,
    )(*pieces, *tops, gain)


def block_masks(width, block):
    row = lax.broadcasted_iota(jnp.int32, (width, width), 0)
    column = lax.broadcasted_iota(jnp.int32, (width, width), 1)
    inside = None
    for start in range(0, width, block):
        here = (row >= start) & (row < start + block) & (column >= start) & (column < start + block)
        inside = here if inside is None else inside | here
    row = lax.broadcasted_iota(jnp.int32, (width, block), 0)
    column = lax.broadcasted_iota(jnp.int32, (width, block), 1)
    fold = None
    for start in range(0, width, block):
        here = row - start == column
        fold = here if fold is None else fold | here
    return inside, jnp.where(fold, 1.0, 0.0).astype(BF16)


def softplus(values):
    small = jnp.exp(-jnp.abs(values))
    grown = 1.0 + small
    exact = jnp.where(grown == 1.0, small, jnp.log(grown) * small / jnp.where(grown == 1.0, 1.0, grown - 1.0))
    return jnp.maximum(values, 0.0) + exact


def mixer_enter_kernel(
    block,
    h_ref,
    m_ref,
    wu,
    wy,
    small,
    u_out,
    y_out,
    conv_out,
    r_out,
    e_out,
    k_out,
    a_out,
    s_out,
    ends,
    wz,
    par,
    wu_all,
    wy_all,
):
    width = wz.shape[1]

    @pl.when(pl.program_id(0) == 0)
    def _():
        wu_all[...] = padded_rows(wu[...], width)
        wy_all[...] = padded_rows(wy[...], width)
        rows = padded_rows(small[...], width)
        inside, fold = block_masks(width, block)
        for gate in (0, 1):
            spread = dot_nt(rows[:, gate * block : gate * block + block], fold)
            wz[gate * width : gate * width + width, :] = jnp.where(inside, spread, 0.0).astype(BF16)
        row = lax.broadcasted_iota(jnp.int32, (width, width), 0)
        column = lax.broadcasted_iota(jnp.int32, (width, width), 1)
        same = jnp.where(row == column, 1.0, 0.0).astype(BF16)
        turned = dot_tn(rows[:, 2 * block : 2 * block + 8], same)
        par[0:8, :] = turned
        par[8:16, :] = turned
        par[7:8, :] = -SHARP * softplus(turned[7:8, :])

    h_low = h_ref[0]
    rows = h_low.shape[0] - HALO
    u_low = dot_nt(h_low, wu_all[...]).astype(BF16)
    u_out[0] = u_low
    y_out[0] = dot_nt(h_low[HALO:], wy_all[...])
    same = m_ref[0].astype(F32)
    u_val = u_low.astype(F32)
    conv = par[4:5, :] + par[0:1, :] * u_val[HALO:]
    for back in (1, 2, 3):
        term = par[back : back + 1, :] * u_val[HALO - back : HALO - back + rows]
        conv = conv + jnp.where(same >= back, term, 0.0)
    conv_low = conv.astype(BF16)
    conv_out[0] = conv_low
    conv = conv_low.astype(F32)
    pre = dot_nt(conv_low, wz[...])
    recur = jax.nn.sigmoid(pre[:, :width] + par[5:6, :])
    enter = jax.nn.sigmoid(pre[:, width:] + par[6:7, :])
    keep = jnp.where(same >= 1.0, jnp.exp(par[7:8, :] * recur), 0.0)
    r_out[0] = recur
    e_out[0] = enter
    k_out[0] = keep
    inputs = conv * enter * jnp.sqrt(jnp.maximum(1.0 - keep * keep, FLOOR))
    mult, total = scan_into(keep, inputs, a_out, s_out, False)
    put_ends(ends, pl.program_id(0), mult, total)


def resident(shape):
    zeros = (0,) * len(shape)
    return pl.BlockSpec(shape, lambda step: zeros)


def per_piece(shape, first=0):
    rest = (0,) * len(shape)
    return pl.BlockSpec((1,) + shape, lambda step: (step + first,) + rest)


def call(kernel, grid, in_specs, out_specs, out_shape, scratch, micros):
    return pl.pallas_call(
        kernel,
        grid=grid,
        in_specs=in_specs,
        out_specs=out_specs,
        out_shape=out_shape,
        scratch_shapes=scratch,
        compiler_params=pltpu.CompilerParams(
            vmem_limit_bytes=VMEM_LIMIT, dimension_semantics=("arbitrary",) * len(grid)
        ),
        cost_estimate=pl.CostEstimate(flops=int(micros / SLOW * 1.15e9), bytes_accessed=1024, transcendentals=0),
    )


def mixer_enter(h_all, same, w_in, extra, block):
    count, tall, model = h_all.shape
    rows = tall - HALO
    chan = w_in.shape[0]
    width = same.shape[2]

    def out(height, columns, dtype):
        return jax.ShapeDtypeStruct((count, height, columns), dtype)

    shapes = [out(tall, width, BF16), out(rows, width, F32), out(rows, width, BF16)]
    shapes += [out(rows, width, F32)] * 5
    fixed = [jax.ShapeDtypeStruct((2, count, width), F32)]
    fixed += [jax.ShapeDtypeStruct((2 * width, width), BF16), jax.ShapeDtypeStruct((16, width), F32)]
    return call(
        functools.partial(mixer_enter_kernel, block),
        (count,),
        [
            per_piece((tall, model)),
            per_piece((rows, width)),
            pl.BlockSpec((chan, model), lambda step: (0, 0)),
            pl.BlockSpec((chan, model), lambda step: (0, 1)),
            pl.BlockSpec((chan, extra), lambda step: (0, 3 * model // extra)),
        ],
        [per_piece(s.shape[1:]) for s in shapes] + [resident(s.shape) for s in fixed],
        shapes + fixed,
        [pltpu.VMEM((width, model), BF16), pltpu.VMEM((width, model), BF16)],
        SWEEP * count * rows * width,
    )(h_all, same, w_in, w_in, w_in)


def column_tile(model):
    return next(t for t in (512, 256, 128) if model % t == 0)


def group_of(shape, blocks, pieces):
    first, stride = blocks[0], (blocks[-1] - blocks[0]) // max(1, len(blocks) - 1)
    rest = (0,) * len(shape)
    return pl.BlockSpec((pieces,) + shape, lambda group, step: (first + stride * group,) + rest)


def group_outs(rows, tile, steps, blocks, pieces):
    def spec(place):
        def index(group, step):
            at = jnp.clip((group - place) * steps + step, 0, steps - 1)
            return (0, 0, at)

        return pl.BlockSpec((pieces, rows, tile), index)

    return [spec(place) for place in range(len(blocks))]


def put_group(outs, total):
    for place, out in enumerate(outs):

        @pl.when(pl.program_id(0) == place)
        def _(out=out):
            out[...] = total.reshape(out.shape)


def mixer_leave_kernel(hops, pieces, blocks, *refs):
    groups = len(blocks)
    first, stride = blocks[0], (blocks[-1] - blocks[0]) // max(1, groups - 1)
    ends = refs[:hops]
    cum, local, y_pre, w_out = refs[hops : hops + 4]
    mixed = refs[-1]
    rows = cum.shape[1]

    @pl.when(pl.program_id(1) == 0)
    def _():
        for index in range(pieces):
            piece = (first + stride * pl.program_id(0)) * pieces + index
            states = local[index] + cum[index] * folded(ends, piece)
            mixed[index * rows : index * rows + rows, :] = (gelu_value(y_pre[index]) * states).astype(BF16)

    right = padded_rows(w_out[...], mixed.shape[1])
    put_group(refs[hops + 4 : hops + 4 + groups], dot_nn(mixed[...], right).astype(BF16))


def mixer_leave(ends, cum, local, y_pre, w_in, model, blocks, pieces):
    rows, width = cum.shape[1:]
    tile = column_tile(model)
    steps = model // tile
    groups = len(blocks)
    return call(
        functools.partial(mixer_leave_kernel, len(ends), pieces, blocks),
        (groups, steps),
        [pl.BlockSpec(ends[0].shape, lambda group, step: (0, 0, 0))] * len(ends)
        + [group_of((rows, width), blocks, pieces)] * 3
        + [pl.BlockSpec((w_in.shape[0], tile), lambda group, step: (0, 2 * steps + step))],
        group_outs(rows, tile, steps, blocks, pieces),
        [jax.ShapeDtypeStruct((pieces, rows, model), BF16)] * groups,
        [pltpu.VMEM((pieces * rows, width), BF16)],
        3.5 + 3.5 * groups * pieces / 2,
    )(*ends, cum, local, y_pre, w_in)


def head_back_kernel(count, hops, *refs):
    d_refs = refs[:count]
    ends = refs[count : count + hops]
    (cum, local, y_pre, keep_ref, w_out, dy_out, mixed_out, cb_out, lb_out, ends_out, all_out, buf, w_all, sems, all_sems) = refs[count + hops :]
    step = pl.program_id(0)

    @pl.when(step == 0)
    def _():
        fetch_all(d_refs, buf, sems)
        w_all[...] = padded_rows(w_out[...], w_all.shape[0])

    fetched(d_refs, buf, sems, step)
    put(buf, all_out, all_sems, step).start()
    d_mixed = dot_nt(buf[step], w_all[...])
    states = local[0] + cum[0] * folded(ends, step)
    value, slope = gelu_parts(y_pre[0])
    mixed_out[0] = (value * states).astype(BF16)
    dy_out[0] = (slope * d_mixed * states).astype(BF16)
    keep = keep_ref[0]
    width = keep.shape[1]
    next_keep = jnp.concatenate([keep[1:], jnp.ones((1, width), F32)], 0)
    mult, total = scan_into(next_keep, d_mixed * value, cb_out, lb_out, True)
    put_ends(ends_out, step, mult * keep[0:1], total * keep[0:1])

    @pl.when(step == count - 1)
    def _():
        for index in range(count):
            put(buf, all_out, all_sems, index).wait()


def head_back(pieces, ends, cum, local, y_pre, keep, w_in):
    count = len(pieces)
    rows, model = pieces[0].shape
    width = cum.shape[2]

    def out(height, dtype):
        return jax.ShapeDtypeStruct((count, height, width), dtype)

    shapes = [out(rows, BF16), out(rows, BF16), out(rows, F32), out(rows, F32)]
    ends_shape = jax.ShapeDtypeStruct((2, count, width), F32)
    return call(
        functools.partial(head_back_kernel, count, len(ends)),
        (count,),
        [ANY] * count
        + [resident(ends[0].shape)] * len(ends)
        + [per_piece((rows, width))] * 4
        + [pl.BlockSpec((w_in.shape[0], model), lambda step: (0, 2))],
        [per_piece(s.shape[1:]) for s in shapes] + [resident(ends_shape.shape), ANY],
        shapes + [ends_shape, jax.ShapeDtypeStruct((count, rows, model), BF16)],
        [
            pltpu.VMEM((count, rows, model), BF16),
            pltpu.VMEM((width, model), BF16),
            pltpu.SemaphoreType.DMA((count,)),
            pltpu.SemaphoreType.DMA((count,)),
        ],
        SWEEP * count * rows * width,
    )(*pieces, *ends, cum, local, y_pre, keep, w_in)


def tail_back_kernel(hops, *refs):
    ends = refs[:hops]
    later = refs[hops : 2 * hops]
    (cb, lb, cum, local, r_ref, e_ref, k_ref, conv_ref, u_ref, m_ref, wz, par, du_out, edge_out, fold_out, small_out, gw_out) = refs[2 * hops :]
    step = pl.program_id(0)

    @pl.when(step == 0)
    def _():
        gw_out[...] = jnp.zeros_like(gw_out)
        small_out[...] = jnp.zeros_like(small_out)

    state_in = folded(ends, step)
    d_states = lb[0] + cb[0] * folded(later, step)
    states = local[0] + cum[0] * state_in
    prev = jnp.concatenate([state_in, states[:-1]], 0)
    recur, enter, keep = r_ref[0], e_ref[0], k_ref[0]
    conv_low = conv_ref[0]
    conv = conv_low.astype(F32)
    rows, width = conv.shape
    spare = 1.0 - keep * keep
    scaling = jnp.sqrt(jnp.maximum(spare, FLOOR))
    weight = jnp.where(spare > FLOOR, 0.5, jnp.where(spare == FLOOR, 0.25, 0.0)) / scaling
    d_enter_sum = d_states * conv
    d_spare = d_enter_sum * enter * weight
    d_expo = (d_states * prev - 2.0 * keep * d_spare) * keep
    d_recur = d_expo * par[7:8, :] * recur * (1.0 - recur)
    d_enter = d_enter_sum * scaling * enter * (1.0 - enter)
    d_pre = jnp.concatenate([d_recur.astype(BF16), d_enter.astype(BF16)], 1)
    d_conv = d_states * enter * scaling + dot_nn(d_pre, wz[...])
    gw_out[...] += dot_tn(d_pre, conv_low)
    d_pre_val = d_pre.astype(F32)
    same = m_ref[0].astype(F32)
    u_val = u_ref[0].astype(F32)
    sums = []
    d_u = jnp.zeros((rows, width), F32)
    head = jnp.zeros((8, width), F32)
    for back in range(4):
        masked = d_conv if back == 0 else jnp.where(same >= back, d_conv, 0.0)
        sums.append(jnp.sum(masked * u_val[HALO - back : HALO - back + rows], axis=0, keepdims=True))
        moved = masked * par[back : back + 1, :]
        if back == 0:
            d_u = d_u + moved
        else:
            nothing = jnp.zeros((back, width), F32)
            d_u = d_u + jnp.concatenate([moved[back:], nothing], 0)
            head = head + jnp.concatenate([jnp.zeros((8 - back, width), F32), moved[:back]], 0)
    sums.append(jnp.sum(d_conv, axis=0, keepdims=True))
    sums.append(jnp.sum(d_pre_val[:, :width], axis=0, keepdims=True))
    sums.append(jnp.sum(d_pre_val[:, width:], axis=0, keepdims=True))
    sums.append(jnp.sum(d_expo * recur, axis=0, keepdims=True))
    small_out[...] += jnp.concatenate(sums, 0)
    du_out[0] = d_u.astype(BF16)
    edge_out[0, 0:8, :] = head
    edge_out[0, 8:16, :] = d_u[rows - 8 :]

    @pl.when(step == pl.num_programs(0) - 1)
    def _():
        inside, fold = block_masks(width, fold_out.shape[1])
        for gate in (0, 1):
            whole = jnp.where(inside, gw_out[gate * width : gate * width + width, :], 0.0).astype(BF16)
            fold_out[gate * width : gate * width + width, :] = dot_nn(whole, fold).astype(BF16)


def tail_back(ends, later, cb, lb, cum, local, recur, enter, keep, conv, u_ext, same, wz, par, block):
    count, rows, width = cb.shape
    shapes = [
        jax.ShapeDtypeStruct((count, rows, width), BF16),
        jax.ShapeDtypeStruct((count, 16, width), F32),
        jax.ShapeDtypeStruct((2 * width, block), BF16),
        jax.ShapeDtypeStruct((8, width), F32),
    ]
    tall = u_ext.shape[1]
    return call(
        functools.partial(tail_back_kernel, len(ends)),
        (count,),
        [resident(ends[0].shape)] * (2 * len(ends))
        + [per_piece((rows, width))] * 8
        + [per_piece((tall, width)), per_piece((rows, width)), resident(wz.shape), resident(par.shape)],
        [per_piece((rows, width)), per_piece((16, width)), resident((2 * width, block)), resident((8, width))],
        shapes,
        [pltpu.VMEM(wz.shape, F32)],
        SWEEP * count * rows * width,
    )(*ends, *later, cb, lb, cum, local, recur, enter, keep, conv, u_ext, same, wz, par)


def rows_times_kernel(terms, gained, *refs):
    lefts, rights = refs[:terms], refs[terms : 2 * terms]
    outs = refs[2 * terms + gained :]
    total = None
    for left, right in zip(lefts, rights):
        pieces, rows, inner = left.shape
        term = dot_nn(left[...].reshape(pieces * rows, inner), padded_rows(right[...], inner))
        total = term if total is None else total + term
    if gained:
        factor = refs[2 * terms][...].reshape(total.shape).astype(F32)
        outs[-1][0] = jnp.sum(total * factor, axis=0, keepdims=True)
        outs = outs[:-1]
    put_group(outs, total.astype(BF16))


def rows_times(lefts, rights, blocks, pieces, factor=None):
    rows = lefts[0].shape[1]
    model = rights[0][2]
    tile = column_tile(model)
    steps = model // tile
    groups = len(blocks)
    inner = sum(right.shape[0] for right, _, _ in rights)
    gained = 0 if factor is None else 1

    def right_spec(right, place):
        return pl.BlockSpec((right.shape[0], tile), lambda group, step: (0, place * steps + step))

    out_specs = group_outs(rows, tile, steps, blocks, pieces)
    shapes = [jax.ShapeDtypeStruct((pieces, rows, model), BF16)] * groups
    extra_specs = []
    if gained:
        first, stride = blocks[0], (blocks[-1] - blocks[0]) // max(1, groups - 1)
        out_specs.append(pl.BlockSpec((1, 1, tile), lambda group, step: (group, 0, step)))
        shapes.append(jax.ShapeDtypeStruct((groups, 1, model), F32))
        extra_specs.append(
            pl.BlockSpec((pieces, rows, tile), lambda group, step: (first + stride * group, 0, step))
        )
    return call(
        functools.partial(rows_times_kernel, len(lefts), gained),
        (groups, steps),
        [group_of(left.shape[1:], blocks, pieces) for left in lefts]
        + [right_spec(right, place) for right, place, _ in rights]
        + extra_specs,
        out_specs,
        shapes,
        [],
        3 + 2 * groups * pieces * rows * inner * model / RATE,
    )(*lefts, *[right for right, _, _ in rights], *([factor] if gained else []))


def assemble_kernel(count, *refs):
    parts, whole, buf, sems, all_sems = refs[:count], refs[count], *refs[count + 1 :]
    fetch_all(parts, buf, sems)
    for index in range(count):
        fetched(parts, buf, sems, index)
        put(buf, whole, all_sems, index).start()
    for index in range(count):
        put(buf, whole, all_sems, index).wait()


def assemble(pieces):
    count = len(pieces)
    shape = (count,) + pieces[0].shape
    return call(
        functools.partial(assemble_kernel, count),
        (1,),
        [ANY] * count,
        ANY,
        jax.ShapeDtypeStruct(shape, pieces[0].dtype),
        [pltpu.VMEM(shape, pieces[0].dtype), pltpu.SemaphoreType.DMA((count,)), pltpu.SemaphoreType.DMA((count,))],
        6.5,
    )(*pieces)


def mlp_kernel(count, first, *refs):
    sources = count if first else 1
    h_refs = refs[:count] if first else [refs[0].at[index] for index in range(count)]
    c_ref, wg, wu, wo, hid_out, dg_out, du_out = refs[sources : sources + 7]
    rest = refs[sources + 7 :]
    all_out = rest[0] if first else None
    h_buf, c_buf, h_sems, c_sems, all_sems = rest[-5:]
    step = pl.program_id(0)
    pair = 2 if count % 2 == 0 else 1
    rows, tile = hid_out.shape[1:]
    model = h_buf.shape[2]

    @pl.when(step == 0)
    def _():
        for index in range(count):
            pltpu.make_async_copy(h_refs[index], h_buf.at[index], h_sems.at[index]).start()
            pltpu.make_async_copy(c_ref.at[index], c_buf.at[index], c_sems.at[index]).start()

    def some_pieces(index, carry):
        @pl.when(step == 0)
        def _():
            for place in range(pair):
                at = index * pair + place
                fetched(h_refs, h_buf, h_sems, at)
                pltpu.make_async_copy(c_ref.at[0], c_buf.at[at], c_sems.at[at]).wait()
                if first:
                    put(h_buf, all_out, all_sems, at).start()

        span = pl.ds(index * pair, pair)
        h_low = h_buf[span].reshape(pair * rows, model)
        gate = dot_nt(h_low, wg[...])
        up = dot_nt(h_low, wu[...])
        d_hidden = dot_nt(c_buf[span].reshape(pair * rows, model), wo[...])
        value, slope = gelu_parts(gate)
        shape = (pair, rows, tile)
        hid_out[span] = (value * up).astype(BF16).reshape(shape)
        dg_out[span] = (d_hidden * up * slope).astype(BF16).reshape(shape)
        du_out[span] = (d_hidden * value).astype(BF16).reshape(shape)
        return carry

    lax.fori_loop(0, count // pair, some_pieces, 0)

    if first:

        @pl.when(step == pl.num_programs(0) - 1)
        def _():
            for index in range(count):
                put(h_buf, all_out, all_sems, index).wait()


def hidden_tile(hidden):
    return next(t for t in (256, 128, hidden) if hidden % t == 0)


def mlp_part(h_rows, c_all, weights):
    first = isinstance(h_rows, list)
    count, rows, model = c_all.shape
    hidden = weights.shape[0]
    tile = hidden_tile(hidden)
    spec = pl.BlockSpec((count, rows, tile), lambda step: (0, 0, step))
    whole = jax.ShapeDtypeStruct((count, rows, model), BF16)
    sources = h_rows if first else [h_rows]

    def column(place):
        return pl.BlockSpec((tile, model), lambda step: (step, place))

    return call(
        functools.partial(mlp_kernel, count, first),
        (hidden // tile,),
        [ANY] * (len(sources) + 1) + [column(0), column(1), column(2)],
        [spec] * 3 + [ANY] * first,
        [jax.ShapeDtypeStruct((count, rows, hidden), BF16)] * 3 + [whole] * first,
        [
            pltpu.VMEM((count, rows, model), BF16),
            pltpu.VMEM((count, rows, model), BF16),
            pltpu.SemaphoreType.DMA((count,)),
            pltpu.SemaphoreType.DMA((count,)),
            pltpu.SemaphoreType.DMA((count,)),
        ],
        2 + 6 * count * rows * model * hidden / RATE,
    )(*sources, c_all, weights, weights, weights)


def mlp_grads_kernel(tiles, dg, du, hid, h_tile, c_tile, out, turned):
    step = pl.program_id(0)
    for place, left in enumerate((dg, du, hid)):

        @pl.when(step == place * tiles)
        def _(left=left):
            turned[...] = left[...].T

    @pl.when(step < 2 * tiles)
    def _():
        out[...] = dot_nn(turned[...], h_tile[...]).astype(BF16)

    @pl.when(step >= 2 * tiles)
    def _():
        out[...] = dot_nn(turned[...], c_tile[...]).astype(BF16)


def mlp_grads(d_gate, d_up, hidden, h_all, c_all):
    model = h_all.shape[2]
    lefts = [v.reshape(-1, v.shape[2]) for v in (d_gate, d_up, hidden)]
    rights = [v.reshape(-1, model) for v in (h_all, c_all)]
    inner, tall = lefts[0].shape
    tile = column_tile(model)
    tiles = model // tile
    return call(
        functools.partial(mlp_grads_kernel, tiles),
        (3 * tiles,),
        [resident((inner, tall))] * 3
        + [
            pl.BlockSpec((inner, tile), lambda step: (0, jnp.where(step < 2 * tiles, step % tiles, tiles - 1))),
            pl.BlockSpec((inner, tile), lambda step: (0, jnp.maximum(step - 2 * tiles, 0))),
        ],
        pl.BlockSpec((tall, tile), lambda step: (0, step)),
        jax.ShapeDtypeStruct((tall, 3 * model), BF16),
        [pltpu.VMEM((tall, inner), BF16)],
        3 + 6 * inner * tall * model / RATE,
    )(*lefts, *rights)


def weight_grads_kernel(tiles, count, *refs):
    lefts, rights, out, turned = refs[:count], refs[count : 2 * count], refs[2 * count], refs[2 * count + 1]
    step = pl.program_id(0)
    for place in range(count):

        @pl.when(step == place * tiles)
        def _(left=lefts[place]):
            turned[...] = left[...].T

        @pl.when((step >= place * tiles) & (step < (place + 1) * tiles))
        def _(right=rights[place]):
            out[...] = dot_nn(turned[...], right[...])[: out.shape[0]].astype(BF16)


def weight_grads(pairs, kept):
    lefts = [left.reshape(-1, left.shape[-1]) for left, _ in pairs]
    rights = [right.reshape(-1, right.shape[-1]) for _, right in pairs]
    count = len(pairs)
    inner, tall = lefts[0].shape
    model = rights[0].shape[1]
    tile = column_tile(model)
    tiles = model // tile

    def right_spec(place):
        return pl.BlockSpec((inner, tile), lambda step: (0, jnp.clip(step - place * tiles, 0, tiles - 1)))

    return call(
        functools.partial(weight_grads_kernel, tiles, count),
        (count * tiles,),
        [resident((inner, tall))] * count + [right_spec(place) for place in range(count)],
        pl.BlockSpec((kept, tile), lambda step: (0, step)),
        jax.ShapeDtypeStruct((kept, count * model), BF16),
        [pltpu.VMEM((tall, inner), BF16)],
        3 + 2 * count * inner * tall * model / RATE,
    )(*lefts, *rights)


def add_kernel(counts, *refs):
    at = 0
    for count, out in zip(counts, refs[sum(counts) :]):
        total = refs[at][0].astype(F32)
        for ref in refs[at + 1 : at + count]:
            total = total + ref[0].astype(F32)
        out[...] = total.astype(BF16)
        at += count


def add_rows(sums):
    arrays = [array for terms in sums for array, _ in terms]
    places = [index for terms in sums for _, index in terms]
    _, rows, width = arrays[0].shape
    steps = 4
    tall = rows // steps

    def spec(place):
        return pl.BlockSpec((1, tall, width), lambda step: (place, step, 0))

    counts = [len(terms) for terms in sums]
    return call(
        functools.partial(add_kernel, counts),
        (steps,),
        [spec(place) for place in places],
        [pl.BlockSpec((tall, width), lambda step: (step, 0))] * len(sums),
        [jax.ShapeDtypeStruct((rows, width), BF16)] * len(sums),
        [],
        1 + 0.6 * len(arrays),
    )(*arrays)


def last_kernel(terms, *refs):
    rows, base, gain, out = refs[terms:]
    total = refs[0][0].astype(F32)
    for ref in refs[1:terms]:
        total = total + ref[0].astype(F32)
    if gain is not None:
        x_val = rows[...].astype(F32)
        root = lax.rsqrt(jnp.mean(x_val * x_val, axis=-1, keepdims=True) + EPS)
        x_val = x_val * root
        total = total * gain[...]
        total = root * (total - x_val * jnp.mean(total * x_val, axis=-1, keepdims=True))
    out[...] = (base[...] + total).astype(BF16)


def last_rows(terms, base, rows=None, gain=None):
    tall, model = base.shape
    steps = 4
    block = pl.BlockSpec((tall // steps, model), lambda step: (step, 0))

    def spec(place):
        return pl.BlockSpec((1, tall // steps, model), lambda step: (place, step, 0))

    extra = [] if gain is None else [rows]
    kernel = last_kernel if gain is not None else lambda count, *refs: last_kernel(
        count, *refs[:count], None, refs[count], None, refs[count + 1]
    )
    return call(
        functools.partial(kernel, len(terms)),
        (steps,),
        [spec(place) for _, place in terms]
        + [block] * (len(extra) + 1)
        + ([] if gain is None else [resident(gain.shape)]),
        block,
        jax.ShapeDtypeStruct((tall, model), BF16),
        [],
        6.0,
    )(*[array for array, _ in terms], *extra, base, *([] if gain is None else [gain]))


def split_grads_kernel(one_gate, one_up, one_down, two_gate, two_up, two_down, both, down):
    cut = one_gate.shape[0]
    both[:cut, 0, :] = one_gate[...].astype(F32)
    both[:cut, 1, :] = one_up[...].astype(F32)
    both[cut:, 0, :] = two_gate[...].astype(F32)
    both[cut:, 1, :] = two_up[...].astype(F32)
    down[:cut, :] = one_down[...].astype(F32)
    down[cut:, :] = two_down[...].astype(F32)


def split_grads(one, two, model):
    rows = one.shape[0] + two.shape[0]
    tile = column_tile(model)
    steps = model // tile

    def spec(part, place):
        return pl.BlockSpec((part.shape[0], tile), lambda step: (0, place * steps + step))

    return call(
        split_grads_kernel,
        (steps,),
        [spec(part, place) for part in (one, two) for place in range(3)],
        [
            pl.BlockSpec((rows, 2, tile), lambda step: (0, 0, step)),
            pl.BlockSpec((rows, tile), lambda step: (0, step)),
        ],
        [jax.ShapeDtypeStruct((rows, 2, model), F32), jax.ShapeDtypeStruct((rows, model), F32)],
        [],
        6.0,
    )(one, one, one, two, two, two)


def seq_gather(shard):
    return lax.all_gather(shard, "seq", axis=0, tiled=True)


def seq_scatter(whole):
    return lax.psum_scatter(whole, "seq", scatter_dimension=0, tiled=True)


def per_device(
    tokens,
    cotangent,
    doc_ids,
    mix_in,
    mix_out,
    gate_w,
    conv_w,
    conv_bias,
    gate_bias,
    decay_param,
    gain_one,
    gain_two,
    mlp_in,
    mlp_out,
):
    run_len, model = tokens.shape[1:]
    n_seq = lax.axis_size("seq")
    n_dev = lax.axis_size("dp") * n_seq
    own = mix_out.shape[0]
    block = gate_w.shape[2]
    chan = own * n_seq
    width = -(-chan // 128) * 128
    blocks = chan // block

    x_low = tokens.reshape(run_len, model)
    x_pieces, _ = gather_rows(x_low)
    x_zero = x_low.astype(F32)
    cot_low = cotangent.reshape(run_len, model)
    lead = hand_on(x_low[run_len - HALO :], 1)
    part = gain_one.shape[0]
    gains = jnp.concatenate([gain_one, gain_two]).astype(BF16)[None]
    my_run = lax.axis_index("seq")
    first_token = my_run * run_len
    places = lax.broadcasted_iota(jnp.int32, (n_seq, 1), 0)
    gain_rows = jnp.where(places == my_run, gains, jnp.zeros((), BF16))
    for hop in range(1, n_seq):
        ring = [(source, (source + hop) % n_seq) for source in range(n_seq)]
        arrived = lax.ppermute(gains, "seq", ring)
        gain_rows = jnp.where(places == (my_run - hop) % n_seq, arrived, gain_rows)
    gain_rows = jnp.pad(gain_rows.reshape(1, -1), ((0, 0), (0, model - 2 * part * n_seq)))
    padded = jnp.concatenate([jnp.full((3,), -1, jnp.int32), doc_ids.reshape(-1)])
    own_docs = lax.dynamic_slice_in_dim(padded, first_token + 3, run_len)
    same = sum(
        jnp.where(lax.dynamic_slice_in_dim(padded, first_token + 3 - back, run_len) == own_docs, 1.0, 0.0)
        for back in (1, 2, 3)
    )
    info = jnp.pad(same, (0, model - run_len)).astype(BF16)[None]
    tops, _ = gather_rows(jnp.concatenate([info, gain_rows, lead[2:]], 0))
    count = len(tops)
    half = count // 2

    small = jnp.concatenate(
        [
            gate_w.reshape(own, 2 * block),
            conv_w.T,
            conv_bias[:, None],
            gate_bias.T,
            decay_param[:, None],
        ],
        1,
    )
    extra = -(-small.shape[1] // 128) * 128
    small = jnp.pad(small, ((0, 0), (0, extra - small.shape[1])))
    w_in = jnp.concatenate([mix_in[:, 1, :], mix_in[:, 0, :], mix_out, small], 1).astype(BF16)
    w_in = seq_gather(w_in)
    mlp_in, mlp_out = after((mlp_in, mlp_out), lead)
    shard = jnp.concatenate([mlp_in.astype(BF16).reshape(-1, 2 * model), mlp_out.astype(BF16)], 1)
    cut = 2 * shard.shape[0] // 3
    shards = [shard[:cut], shard[cut:]]
    w_one, w_two = [seq_gather(rows) for rows in shards]

    orders = jnp.asarray(piece_order(count), jnp.int32)
    order = lax.dynamic_index_in_dim(after(orders, lead), lax.axis_index("dp"), 0, False)
    places = lax.broadcasted_iota(jnp.int32, (count, 1), 0)
    gain_rows = jnp.zeros((count, 2 * part * n_seq), F32)
    for index, piece in enumerate(tops):
        row = piece[1:2, : 2 * part * n_seq].astype(F32)
        gain_rows = jnp.where(places == order[index], row, gain_rows)
    gain_rows = gain_rows.reshape(n_dev, 2 * part)
    g_one = gain_rows[:, :part].reshape(1, model)
    g_two = gain_rows[:, part:].reshape(1, model)

    h_all, h_one, same = first_norm(x_pieces, tops, g_one, width)
    c_pieces, (same, entered) = gather_rows(
        after(cot_low, *x_pieces),
        [
            ((1,), lambda sent, done: same),
            ((2, 3), lambda sent, done: mixer_enter(after(h_all, shards), done[0], w_in, extra, block)),
        ],
    )
    (u_ext, y_pre, conv, recur, enter, keep, cum, local, ends, w_z, par) = entered
    earlier = [hand_on(ends, steps) for steps in range(1, n_seq)]

    def leaving(blocks_at, pieces, before):
        return mixer_leave(earlier, cum, local, after(y_pre, *before), w_in, model, blocks_at, pieces)

    kept = []
    x_one = x_zero + scatter_rows(leaving, count, None)
    n_two, norm_two_back = jax.vjp(rms_norm, x_one, g_two)
    h_two = n_two.astype(BF16)

    h_pieces, (c_all,) = gather_rows(h_two, [((1, 2), lambda sent, done: assemble(after(c_pieces, sent)))])
    hid_one, gate_one, up_one, h_all = mlp_part(h_pieces, c_all, w_one)
    grad_one = mlp_grads(gate_one, up_one, hid_one, h_all, c_all)
    hid_two, gate_two, up_two = mlp_part(after(h_all, grad_one), c_all, w_two)
    grad_one = seq_scatter(grad_one)

    def d_entering(blocks_at, pieces, before):
        lefts = [after(gate_one, *before), up_one, gate_two, up_two]
        rights = [(w_one, 0, model), (w_one, 1, model), (w_two, 0, model), (w_two, 1, model)]
        return rows_times(lefts, rights, blocks_at, pieces)

    def second_grads(sent, done):
        return mlp_grads(after(gate_two, sent), up_two, hid_two, h_all, c_all)

    def mlp_leaving(blocks_at, pieces, before):
        return rows_times([after(hid_one, *before), hid_two], [(w_one, 2, model), (w_two, 2, model)], blocks_at, pieces)

    def mlp_out_rows(sent):
        return mlp_leaving([1, 0], half, (sent,))

    d_h_two = scatter_rows(d_entering, count, beside(mlp_out_rows, kept))
    d_x_norm, d_gain_two = norm_two_back(d_h_two)
    d_x_one = cot_low.astype(F32) + d_x_norm
    d_mix = d_x_one.astype(BF16)

    stages, twin = plane_stages(lax.axis_size("dp"))

    def mlp_out_sums(sent, done):
        theirs, mine = after(kept.pop(), sent)
        there = lax.ppermute(theirs, "dp", twin)
        return mine, there, add_rows([[(mine, k), (there, k)] for k in range(half // 2, half)])

    d_pieces, done = gather_rows(d_mix, [((1, 2), second_grads), ((3,), mlp_out_sums)])
    grad_two, (mine, there, far) = done
    grad_two = seq_scatter(after(grad_two, grad_one))
    d_y, mixed, cum_back, local_back, ends_back, d_all = head_back(
        after(d_pieces, far), earlier, cum, local, y_pre, keep, w_in
    )
    got = [lax.ppermute(part, "dp", stages[-1]) for part in far]
    mixed, got = lax.optimization_barrier((mixed, got))
    later = [hand_on(ends_back, -steps) for steps in range(1, n_seq)]
    grad_y_out = weight_grads([(after(d_y, ends_back), h_one), (mixed, d_all)], chan)
    later, grad_y_out = lax.optimization_barrier((later, grad_y_out))
    grad_y_out = seq_scatter(after(grad_y_out, grad_two))
    d_u, edges, grad_z, sums = tail_back(
        earlier, later, cum_back, local_back, cum, local, recur, enter, keep, conv, u_ext, same, w_z, par, block
    )
    from_next = hand_on(edges[:, :8], -1)
    terms = [[(mine, k), (there, k), (got[k][None], 0)] for k in range(half // 2)]
    held = terms[half // 4 :]
    arrays = after([[array for array, _ in those] for those in held], edges)
    layer_sums = add_rows([[(v, at) for v, (_, at) in zip(vs, those)] for vs, those in zip(arrays, held)])
    from_next, layer_sums = lax.optimization_barrier((from_next, layer_sums))
    layer_got = [lax.ppermute(part, "dp", stages[-2]) for part in layer_sums]
    grad_z = jnp.concatenate([grad_z[:chan], grad_z[width : width + chan]], 1)
    sums = sums[:, :chan]
    sums = jnp.concatenate([sums[:7], (sums[7] * (-SHARP * jax.nn.sigmoid(par[15, :chan])))[None]], 0).T
    tail = jnp.concatenate([grad_z, sums.astype(BF16)], 1)
    tail = jnp.pad(tail, ((0, 0), (0, extra - tail.shape[1])))
    d_u = lax.dynamic_update_slice(d_u, (edges[:, 8:] + from_next).astype(BF16), (0, run_len - 8, 0))
    gain_terms = []

    def d_leaving(blocks_at, pieces, before):
        *part_rows, gain_term = rows_times(
            [after(d_y, *before), d_u], [(w_in, 1, model), (w_in, 0, model)], blocks_at, pieces, h_one
        )
        gain_terms.append(gain_term.sum(0))
        if blocks_at == [1]:
            part_rows[0], layer_got[:] = lax.optimization_barrier((part_rows[0], layer_got))
        return part_rows

    def u_grad(sent):
        return weight_grads([(after(d_u, sent), h_one)], chan)

    d_h_one = scatter_terms(d_leaving, count, None, beside(u_grad, kept))
    grad_u = seq_scatter(after(jnp.concatenate([kept.pop(), tail], 1), grad_y_out))
    input_grad = last_rows(d_h_one, d_x_one, x_low, g_one).reshape(1, run_len, model)
    terms = [[*those, (one[None], 0)] for those, one in zip(terms, layer_got)]
    layer_terms = scatter_tail(terms, stages[:-2], [])
    layer_out = last_rows(layer_terms, x_one).reshape(1, run_len, model)
    d_gain_one = sum(gain_terms) / g_one
    d_gains = jnp.concatenate([d_gain_one.reshape(n_dev, part), d_gain_two.reshape(n_dev, part)], 1)
    d_gains = lax.all_to_all(after(d_gains, input_grad), ("dp", "seq"), 0, 0, tiled=True).sum(0)
    grad_mlp_in, grad_mlp_out = split_grads(after(grad_one, input_grad), grad_two, model)

    tail = grad_u[:, model:].astype(F32)
    grad_mix_in = jnp.stack([grad_y_out[:, :model].astype(F32), grad_u[:, :model].astype(F32)], 1)
    at = 2 * block
    return (
        layer_out,
        input_grad,
        grad_mix_in,
        grad_y_out[:, model:].astype(F32),
        tail[:, :at].reshape(own, 2, block),
        tail[:, at : at + 4].T,
        tail[:, at + 4],
        tail[:, at + 5 : at + 7].T,
        tail[:, at + 7],
        d_gains[:part],
        d_gains[part:],
        grad_mlp_in,
        grad_mlp_out,
    )


def solution(mesh):
    rows = P(("dp", "seq"))
    placed = (
        P("dp", "seq", None),
        P("dp", "seq", None),
        P("dp", None),
        P(("dp", "seq"), None, None),
        P(("dp", "seq"), None),
        P(("dp", "seq"), None, None),
        P(None, ("dp", "seq")),
        rows,
        P(None, ("dp", "seq")),
        rows,
        rows,
        rows,
        P(("dp", "seq"), None, None),
        P(("dp", "seq"), None),
    )
    return jax.shard_map(
        per_device,
        mesh=mesh,
        in_specs=placed,
        out_specs=placed[:2] + placed[3:],
        check_vma=False,
    )
```

```python
import functools

import jax
import jax.numpy as jnp
from jax import lax
from jax.experimental import pallas as pl
from jax.experimental.pallas import tpu as pltpu
from jax.sharding import PartitionSpec as P

EPS = 1e-06
FLOOR = 0.0001
SHARP = 8.0
HALO = 16
F32 = jnp.float32
BF16 = jnp.bfloat16
MEBI = 1024 * 1024
ANY = pl.BlockSpec(memory_space=pl.ANY)
ROOT = 0.7978845608028654
CUBE = 0.044715
SLOW = 4.5
RATE = 650e6
SWEEP = 25e-6


def dot_nt(left, right):
    return lax.dot_general(left, right, (((1,), (1,)), ((), ())), preferred_element_type=F32)


def dot_nn(left, right):
    return lax.dot_general(left, right, (((1,), (0,)), ((), ())), preferred_element_type=F32)


def dot_tn(left, right):
    return lax.dot_general(left, right, (((0,), (0,)), ((), ())), preferred_element_type=F32)


def rms_norm(values, gain_vec):
    return values * lax.rsqrt(jnp.mean(values * values, axis=-1, keepdims=True) + EPS) * gain_vec


def gelu_parts(values):
    squared = values * values
    bend = jnp.tanh(ROOT * (values + CUBE * values * squared))
    half = 0.5 * (1.0 + bend)
    slope = half + 0.5 * values * (1.0 - bend * bend) * (ROOT * (1.0 + 3.0 * CUBE * squared))
    return values * half, slope


def gelu_value(values):
    bend = jnp.tanh(ROOT * (values + CUBE * values * values * values))
    return values * (0.5 * (1.0 + bend))


def plane_stages(count):
    bits = count.bit_length() - 1
    upper = list(range(1, bits))
    stages = []
    for place in range(len(upper)):
        pairs = []
        for source in range(count):
            shift = place if source % 2 == 0 else (place + 1) % len(upper)
            pairs.append((source, source ^ (1 << upper[shift])))
        stages.append(pairs)
    twin = [(source, source ^ 1) for source in range(count)]
    return stages, twin


def gather_rows(piece, beside=()):
    stages, twin = plane_stages(lax.axis_size("dp"))
    held = [piece] + [None] * (2 ** len(stages) - 1)
    done = []
    before = ()

    def arrival(m):
        top = m.bit_length() - 1
        return lax.ppermute(held[m ^ (1 << top)], "dp", stages[top])

    for members, work in beside:
        arrived = [arrival(m) for m in members]
        sent = [held[m ^ (1 << (m.bit_length() - 1))] for m in members]
        arrived, made = lax.optimization_barrier((arrived, work((sent, before), done)))
        before = arrived
        done.append(made)
        for m, part in zip(members, arrived):
            held[m] = part
    for m in range(1, len(held)):
        if held[m] is None:
            held[m] = arrival(m)
    return held + [lax.ppermute(part, "dp", twin) for part in held], done


def after(value, *others):
    return lax.optimization_barrier((value, others))[0]


def total_of(terms):
    return sum(array[place].astype(F32) for array, place in terms)


def scatter_tail(terms, stages, waits, late=()):
    for place, pairs in enumerate(reversed(stages)):
        split = len(terms) // 2
        sent = add_rows(terms[split:])
        if late:
            sent, late = lax.optimization_barrier((sent, late))
            terms = [[*those, (one[None], 0)] for those, one in zip(terms, late)] + terms[split:]
            late = ()
        got = [lax.ppermute(part, "dp", pairs) for part in sent]
        if place < len(waits):
            got = waits[place](sent, got)
        terms = [[*those, (one[None], 0)] for those, one in zip(terms, got)]
    return terms[0]


def scatter_terms(make, count, wait, low_wait=None):
    stages, twin = plane_stages(lax.axis_size("dp"))
    quarter = count // 4
    theirs = make([3], quarter, ())[0]
    there = lax.ppermute(theirs, "dp", twin)
    far = make([1], quarter, (theirs,))[0]
    sent = add_rows([[(far, k), (there, k)] for k in range(quarter)])
    got = [lax.ppermute(part, "dp", stages[-1]) for part in sent]
    split = quarter // 2
    theirs, near = make([2, 0], quarter, (sent,))
    theirs, near, got[split:] = lax.optimization_barrier((theirs, near, got[split:]))
    there = lax.ppermute(theirs, "dp", twin)
    terms = [[(near, k), (there, k)] for k in range(quarter)]
    terms = terms[:split] + [[*terms[k], (got[k][None], 0)] for k in range(split, quarter)]
    late = got[:split]
    if low_wait is not None:
        late = low_wait(sent, late)
    return scatter_tail(terms, stages[:-1], [wait] if wait else [], late)


def scatter_rows(make, count, wait):
    return total_of(scatter_terms(make, count, wait))


def beside(work, done):
    def wait(sent, got):
        got, made = lax.optimization_barrier((got, work(sent)))
        done.append(made)
        return got

    return wait


def piece_order(count):
    stages, twin = plane_stages(count)
    orders = []
    for device in range(count):
        held, other = [device], [twin[device][1]]
        for pairs in stages:
            held = held + [pairs[place][1] for place in held]
            other = other + [pairs[place][1] for place in other]
        orders.append(held + other)
    return orders


def hand_on(value, steps):
    count = lax.axis_size("seq")
    first, last = (max(0, -steps), min(count, count - steps))
    return lax.ppermute(value, "seq", [(source, source + steps) for source in range(first, last)])


def scan_into(keep, entry, cum_ref, state_ref, backward):
    rows, width = keep.shape
    groups = rows // 8
    mult = keep.reshape(groups, 8, width)
    total = entry.reshape(groups, 8, width)
    place = lax.broadcasted_iota(jnp.int32, (groups, 8, width), 1)
    for hop in (1, 2, 4):
        if backward:
            shift, valid = 8 - hop, place < 8 - hop
        else:
            shift, valid = hop, place >= hop
        near_mult = pltpu.roll(mult, shift, 1)
        near_total = pltpu.roll(total, shift, 1)
        total = jnp.where(valid, total + mult * near_total, total)
        mult = jnp.where(valid, mult * near_mult, mult)
    carry_total = jnp.zeros((1, width), F32)
    carry_mult = jnp.ones((1, width), F32)
    edge = 0 if backward else 7
    order = range(groups - 1, -1, -1) if backward else range(groups)
    for group in order:
        now_total = total[group] + mult[group] * carry_total
        now_mult = mult[group] * carry_mult
        state_ref[0, group * 8 : group * 8 + 8, :] = now_total
        cum_ref[0, group * 8 : group * 8 + 8, :] = now_mult
        carry_total = now_total[edge : edge + 1]
        carry_mult = now_mult[edge : edge + 1]
    return carry_mult, carry_total


def folded(refs, piece):
    at = pl.ds(piece, 1)
    carry = refs[-1][1, at, :]
    for ref in refs[-2::-1]:
        carry = ref[1, at, :] + ref[0, at, :] * carry
    return carry


def put_ends(ref, piece, mult, total):
    ref[0, pl.ds(piece, 1), :] = mult
    ref[1, pl.ds(piece, 1), :] = total


def fetch_all(refs, buf, sems):
    for index, ref in enumerate(refs):
        pltpu.make_async_copy(ref, buf.at[index], sems.at[index]).start()


def fetched(refs, buf, sems, index):
    pltpu.make_async_copy(refs[0], buf.at[index], sems.at[index]).wait()


def put(buf, whole, sems, index):
    return pltpu.make_async_copy(buf.at[index], whole.at[index], sems.at[index])


def padded_rows(rows, width):
    missing = width - rows.shape[0]
    return jnp.concatenate([rows, jnp.zeros((missing, rows.shape[1]), rows.dtype)], 0) if missing else rows


def first_norm_kernel(count, *refs):
    x_refs, top_refs = refs[:count], refs[count : 2 * count]
    gain, all_out, h_out, m_out, buf, top, sems, top_sems = refs[2 * count :]
    step = pl.program_id(0)

    @pl.when(step == 0)
    def _():
        fetch_all(top_refs, top, top_sems)
        fetch_all(x_refs, buf, sems)

    fetched(top_refs, top, top_sems, step)
    fetched(x_refs, buf, sems, step)
    rows, width = m_out.shape[1:]
    top_val = top[step].astype(F32)
    info = jnp.broadcast_to(top_val[0:1, :rows], (width, rows)).astype(BF16)
    across = lax.broadcasted_iota(jnp.int32, (rows, rows), 0)
    down = lax.broadcasted_iota(jnp.int32, (rows, rows), 1)
    m_out[0] = dot_nt(jnp.where(across == down, 1.0, 0.0).astype(BF16), info).astype(BF16)
    all_out[0, :HALO] = rms_norm(top_val, gain[...]).astype(BF16)
    h_low = rms_norm(buf[step].astype(F32), gain[...]).astype(BF16)
    all_out[0, HALO:] = h_low
    h_out[0] = h_low


def first_norm(pieces, tops, gain, width):
    count = len(pieces)
    rows, model = pieces[0].shape
    shapes = [
        jax.ShapeDtypeStruct((count, rows + HALO, model), BF16),
        jax.ShapeDtypeStruct((count, rows, model), BF16),
        jax.ShapeDtypeStruct((count, rows, width), BF16),
    ]
    return call(
        functools.partial(first_norm_kernel, count),
        (count,),
        [ANY] * (2 * count) + [resident(gain.shape)],
        [per_piece(s.shape[1:]) for s in shapes],
        shapes,
        [
            pltpu.VMEM((count, rows, model), BF16),
            pltpu.VMEM((count, HALO, model), BF16),
            pltpu.SemaphoreType.DMA((count,)),
            pltpu.SemaphoreType.DMA((count,)),
        ],
        2.6e-6 * count * rows * model,
        60,
    )(*pieces, *tops, gain)


def block_masks(width, block):
    row = lax.broadcasted_iota(jnp.int32, (width, width), 0)
    column = lax.broadcasted_iota(jnp.int32, (width, width), 1)
    inside = None
    for start in range(0, width, block):
        here = (row >= start) & (row < start + block) & (column >= start) & (column < start + block)
        inside = here if inside is None else inside | here
    row = lax.broadcasted_iota(jnp.int32, (width, block), 0)
    column = lax.broadcasted_iota(jnp.int32, (width, block), 1)
    fold = None
    for start in range(0, width, block):
        here = row - start == column
        fold = here if fold is None else fold | here
    return inside, jnp.where(fold, 1.0, 0.0).astype(BF16)


def sigmoid(values):
    return 0.5 * jnp.tanh(0.5 * values) + 0.5


def softplus(values):
    small = jnp.exp(-jnp.abs(values))
    grown = 1.0 + small
    exact = jnp.where(grown == 1.0, small, jnp.log(grown) * small / jnp.where(grown == 1.0, 1.0, grown - 1.0))
    return jnp.maximum(values, 0.0) + exact


def mixer_enter_kernel(
    block,
    h_ref,
    m_ref,
    wu,
    wy,
    small,
    u_out,
    y_out,
    conv_out,
    r_out,
    e_out,
    k_out,
    a_out,
    s_out,
    ends,
    wz,
    par,
    w_all,
    both,
):
    width = wz.shape[1]
    some, tall, model = h_ref.shape
    rows = tall - HALO
    place = pl.program_id(0) % some

    @pl.when(pl.program_id(0) == 0)
    def _():
        w_all[:width, :] = padded_rows(wu[...], width)
        w_all[width:, :] = padded_rows(wy[...], width)
        params = padded_rows(small[...], width)
        inside, fold = block_masks(width, block)
        for gate in (0, 1):
            spread = dot_nt(params[:, gate * block : gate * block + block], fold)
            wz[gate * width : gate * width + width, :] = jnp.where(inside, spread, 0.0).astype(BF16)
        row = lax.broadcasted_iota(jnp.int32, (width, width), 0)
        column = lax.broadcasted_iota(jnp.int32, (width, width), 1)
        same = jnp.where(row == column, 1.0, 0.0).astype(BF16)
        turned = dot_tn(params[:, 2 * block : 2 * block + 8], same)
        par[0:8, :] = turned
        par[8:16, :] = turned
        par[7:8, :] = -SHARP * softplus(turned[7:8, :])

    @pl.when(place == 0)
    def _():
        both[...] = dot_nt(h_ref[...].reshape(some * tall, model), w_all[...]).reshape(both.shape)

    u_low = both[place, :, :width].astype(BF16)
    u_out[0] = u_low
    y_out[0] = both[place, HALO:, width:]
    same = m_ref[0].astype(F32)
    u_val = u_low.astype(F32)
    conv = par[4:5, :] + par[0:1, :] * u_val[HALO:]
    for back in (1, 2, 3):
        term = par[back : back + 1, :] * u_val[HALO - back : HALO - back + rows]
        conv = conv + jnp.where(same >= back, term, 0.0)
    conv_low = conv.astype(BF16)
    conv_out[0] = conv_low
    conv = conv_low.astype(F32)
    pre = dot_nt(conv_low, wz[...])
    recur = sigmoid(pre[:, :width] + par[5:6, :])
    enter = sigmoid(pre[:, width:] + par[6:7, :])
    keep = jnp.where(same >= 1.0, jnp.exp(par[7:8, :] * recur), 0.0)
    r_out[0] = recur
    e_out[0] = enter
    k_out[0] = keep
    spare = jnp.maximum(1.0 - keep * keep, FLOOR)
    inputs = conv * enter * (spare * lax.rsqrt(spare))
    mult, total = scan_into(keep, inputs, a_out, s_out, False)
    put_ends(ends, pl.program_id(0), mult, total)


def resident(shape):
    zeros = (0,) * len(shape)
    return pl.BlockSpec(shape, lambda step: zeros)


def per_piece(shape, first=0):
    rest = (0,) * len(shape)
    return pl.BlockSpec((1,) + shape, lambda step: (step + first,) + rest)


def grown(memory, count, usual=8):
    return min(60, memory * max(count, usual) // usual)


def settings(micros, axes, memory):
    return dict(
        compiler_params=pltpu.CompilerParams(
            vmem_limit_bytes=memory * MEBI, dimension_semantics=("arbitrary",) * axes if axes else None
        ),
        cost_estimate=pl.CostEstimate(flops=int(micros / SLOW * 1.15e9), bytes_accessed=1024, transcendentals=0),
    )


def call(kernel, grid, in_specs, out_specs, out_shape, scratch, micros, memory, aliases={}):
    return pl.pallas_call(
        kernel,
        grid=grid,
        in_specs=in_specs,
        out_specs=out_specs,
        out_shape=out_shape,
        scratch_shapes=scratch,
        input_output_aliases=aliases,
        **settings(micros, len(grid), memory),
    )


def stream(kernel, grid, in_specs, out_specs, out_shape, micros):
    def outer(*refs):
        pltpu.emit_pipeline(kernel, grid=grid, in_specs=in_specs, out_specs=[out_specs])(*refs)

    here = pl.BlockSpec(memory_space=pltpu.HBM)
    return pl.pallas_call(
        outer,
        in_specs=[here] * len(in_specs),
        out_specs=here,
        out_shape=out_shape,
        **settings(micros, 0, 16),
    )


def mixer_enter(h_all, same, w_in, extra, block):
    count, tall, model = h_all.shape
    rows = tall - HALO
    chan = w_in.shape[0]
    width = same.shape[2]
    some = 1

    def out(height, columns, dtype):
        return jax.ShapeDtypeStruct((count, height, columns), dtype)

    shapes = [out(tall, width, BF16), out(rows, width, F32), out(rows, width, BF16)]
    shapes += [out(rows, width, F32)] * 5
    fixed = [jax.ShapeDtypeStruct((2, count, width), F32)]
    fixed += [jax.ShapeDtypeStruct((2 * width, width), BF16), jax.ShapeDtypeStruct((16, width), F32)]
    return call(
        functools.partial(mixer_enter_kernel, block),
        (count,),
        [
            pl.BlockSpec((some, tall, model), lambda step: (step // some, 0, 0)),
            per_piece((rows, width)),
            pl.BlockSpec((chan, model), lambda step: (0, 0)),
            pl.BlockSpec((chan, model), lambda step: (0, 1)),
            pl.BlockSpec((chan, extra), lambda step: (0, 3 * model // extra)),
        ],
        [per_piece(s.shape[1:]) for s in shapes] + [resident(s.shape) for s in fixed],
        shapes + fixed,
        [pltpu.VMEM((2 * width, model), BF16), pltpu.VMEM((some, tall, 2 * width), F32)],
        SWEEP * count * rows * width,
        grown(26, count),
    )(h_all, same, w_in, w_in, w_in)


def column_tile(model):
    return next(t for t in (512, 256, 128) if model % t == 0)


def group_of(shape, blocks, pieces):
    first, stride = blocks[0], (blocks[-1] - blocks[0]) // max(1, len(blocks) - 1)
    rest = (0,) * len(shape)
    return pl.BlockSpec((pieces,) + shape, lambda group, step: (first + stride * group,) + rest)


def group_outs(rows, tile, steps, blocks, pieces):
    def spec(place):
        def index(group, step):
            at = jnp.clip((group - place) * steps + step, 0, steps - 1)
            return (0, 0, at)

        return pl.BlockSpec((pieces, rows, tile), index)

    return [spec(place) for place in range(len(blocks))]


def put_group(outs, total):
    for place, out in enumerate(outs):

        @pl.when(pl.program_id(0) == place)
        def _(out=out):
            out[...] = total.reshape(out.shape)


def mixer_leave_kernel(hops, pieces, blocks, *refs):
    groups = len(blocks)
    first, stride = blocks[0], (blocks[-1] - blocks[0]) // max(1, groups - 1)
    ends = refs[:hops]
    cum, local, y_pre, w_out = refs[hops : hops + 4]
    mixed = refs[-1]
    rows = cum.shape[1]

    @pl.when(pl.program_id(1) == 0)
    def _():
        for index in range(pieces):
            piece = (first + stride * pl.program_id(0)) * pieces + index
            states = local[index] + cum[index] * folded(ends, piece)
            mixed[index * rows : index * rows + rows, :] = (gelu_value(y_pre[index]) * states).astype(BF16)

    right = padded_rows(w_out[...], mixed.shape[1])
    put_group(refs[hops + 4 : hops + 4 + groups], dot_nn(mixed[...], right).astype(BF16))


def mixer_leave(ends, cum, local, y_pre, w_in, model, blocks, pieces):
    rows, width = cum.shape[1:]
    tile = column_tile(model)
    steps = model // tile
    groups = len(blocks)
    return call(
        functools.partial(mixer_leave_kernel, len(ends), pieces, blocks),
        (groups, steps),
        [pl.BlockSpec(ends[0].shape, lambda group, step: (0, 0, 0))] * len(ends)
        + [group_of((rows, width), blocks, pieces)] * 3
        + [pl.BlockSpec((w_in.shape[0], tile), lambda group, step: (0, 2 * steps + step))],
        group_outs(rows, tile, steps, blocks, pieces),
        [jax.ShapeDtypeStruct((pieces, rows, model), BF16)] * groups,
        [pltpu.VMEM((pieces * rows, width), BF16)],
        3.5 + 3.5 * groups * pieces / 2,
        grown(20, pieces, 2),
    )(*ends, cum, local, y_pre, w_in)


def head_back_kernel(count, hops, *refs):
    d_refs = refs[:count]
    ends = refs[count : count + hops]
    (cum, local, y_pre, keep_ref, w_out, dy_out, mixed_out, cb_out, lb_out, ends_out, all_out, buf, w_all, d_some, sems, all_sems) = refs[count + hops :]
    some = 1
    step = pl.program_id(0)

    @pl.when(step == 0)
    def _():
        fetch_all(d_refs, buf, sems)
        w_all[...] = padded_rows(w_out[...], w_all.shape[0])

    @pl.when(step % some == 0)
    def _():
        for place in range(some):
            fetched(d_refs, buf, sems, step + place)
            put(buf, all_out, all_sems, step + place).start()
        rows, model = buf.shape[1:]
        d_some[...] = dot_nt(buf[pl.ds(step, some)].reshape(some * rows, model), w_all[...]).reshape(d_some.shape)

    d_mixed = d_some[step % some]
    states = local[0] + cum[0] * folded(ends, step)
    value, slope = gelu_parts(y_pre[0])
    mixed_out[0] = (value * states).astype(BF16)
    dy_out[0] = (slope * d_mixed * states).astype(BF16)
    keep = keep_ref[0]
    width = keep.shape[1]
    next_keep = jnp.concatenate([keep[1:], jnp.ones((1, width), F32)], 0)
    mult, total = scan_into(next_keep, d_mixed * value, cb_out, lb_out, True)
    put_ends(ends_out, step, mult * keep[0:1], total * keep[0:1])

    @pl.when(step == count - 1)
    def _():
        for index in range(count):
            put(buf, all_out, all_sems, index).wait()


def head_back(pieces, ends, cum, local, y_pre, keep, w_in):
    count = len(pieces)
    rows, model = pieces[0].shape
    width = cum.shape[2]

    def out(height, dtype):
        return jax.ShapeDtypeStruct((count, height, width), dtype)

    shapes = [out(rows, BF16), out(rows, BF16), out(rows, F32), out(rows, F32)]
    ends_shape = jax.ShapeDtypeStruct((2, count, width), F32)
    return call(
        functools.partial(head_back_kernel, count, len(ends)),
        (count,),
        [ANY] * count
        + [resident(ends[0].shape)] * len(ends)
        + [per_piece((rows, width))] * 4
        + [pl.BlockSpec((w_in.shape[0], model), lambda step: (0, 2))],
        [per_piece(s.shape[1:]) for s in shapes] + [resident(ends_shape.shape), ANY],
        shapes + [ends_shape, jax.ShapeDtypeStruct((count, rows, model), BF16)],
        [
            pltpu.VMEM((count, rows, model), BF16),
            pltpu.VMEM((width, model), BF16),
            pltpu.VMEM((1, rows, width), F32),
            pltpu.SemaphoreType.DMA((count,)),
            pltpu.SemaphoreType.DMA((count,)),
        ],
        SWEEP * count * rows * width,
        grown(25, count),
    )(*pieces, *ends, cum, local, y_pre, keep, w_in)


def tail_back_kernel(hops, block, *refs):
    ends = refs[:hops]
    later = refs[hops : 2 * hops]
    (cb, lb, cum, local, r_ref, e_ref, k_ref, conv_ref, u_ref, m_ref, wz, par, du_out, edge_out, tail_out, small_out, gw_out) = refs[2 * hops :]
    step = pl.program_id(0)

    @pl.when(step == 0)
    def _():
        gw_out[...] = jnp.zeros_like(gw_out)
        small_out[...] = jnp.zeros_like(small_out)

    state_in = folded(ends, step)
    d_states = lb[0] + cb[0] * folded(later, step)
    states = local[0] + cum[0] * state_in
    prev = jnp.concatenate([state_in, states[:-1]], 0)
    recur, enter, keep = r_ref[0], e_ref[0], k_ref[0]
    conv_low = conv_ref[0]
    conv = conv_low.astype(F32)
    rows, width = conv.shape
    spare = 1.0 - keep * keep
    floored = jnp.maximum(spare, FLOOR)
    root = lax.rsqrt(floored)
    scaling = floored * root
    weight = jnp.where(spare > FLOOR, 0.5, jnp.where(spare == FLOOR, 0.25, 0.0)) * root
    d_enter_sum = d_states * conv
    d_spare = d_enter_sum * enter * weight
    d_expo = (d_states * prev - 2.0 * keep * d_spare) * keep
    d_recur = d_expo * par[7:8, :] * recur * (1.0 - recur)
    d_enter = d_enter_sum * scaling * enter * (1.0 - enter)
    d_pre = jnp.concatenate([d_recur.astype(BF16), d_enter.astype(BF16)], 1)
    d_conv = d_states * enter * scaling + dot_nn(d_pre, wz[...])
    gw_out[...] += dot_tn(d_pre, conv_low)
    d_pre_val = d_pre.astype(F32)
    same = m_ref[0].astype(F32)
    u_val = u_ref[0].astype(F32)
    sums = []
    d_u = jnp.zeros((rows, width), F32)
    head = jnp.zeros((8, width), F32)
    for back in range(4):
        masked = d_conv if back == 0 else jnp.where(same >= back, d_conv, 0.0)
        sums.append(jnp.sum(masked * u_val[HALO - back : HALO - back + rows], axis=0, keepdims=True))
        moved = masked * par[back : back + 1, :]
        if back == 0:
            d_u = d_u + moved
        else:
            nothing = jnp.zeros((back, width), F32)
            d_u = d_u + jnp.concatenate([moved[back:], nothing], 0)
            head = head + jnp.concatenate([jnp.zeros((8 - back, width), F32), moved[:back]], 0)
    sums.append(jnp.sum(d_conv, axis=0, keepdims=True))
    sums.append(jnp.sum(d_pre_val[:, :width], axis=0, keepdims=True))
    sums.append(jnp.sum(d_pre_val[:, width:], axis=0, keepdims=True))
    sums.append(jnp.sum(d_expo * recur, axis=0, keepdims=True))
    small_out[...] += jnp.concatenate(sums, 0)
    du_out[0] = d_u.astype(BF16)
    edge_out[0, 0:8, :] = head
    edge_out[0, 8:16, :] = d_u[rows - 8 :]

    @pl.when(step == pl.num_programs(0) - 1)
    def _():
        kept, wide = tail_out.shape
        inside, fold = block_masks(width, block)
        parts = []
        for gate in (0, 1):
            whole = jnp.where(inside, gw_out[gate * width : gate * width + width, :], 0.0).astype(BF16)
            parts.append(dot_nn(whole, fold))
        sums = small_out[...]
        slope = -SHARP * sigmoid(par[15:16, :])
        sums = jnp.concatenate([sums[:7], sums[7:8] * slope], 0).astype(BF16)
        row = lax.broadcasted_iota(jnp.int32, (width, width), 0)
        column = lax.broadcasted_iota(jnp.int32, (width, width), 1)
        parts.append(dot_nt(jnp.where(row == column, 1.0, 0.0).astype(BF16), sums))
        parts.append(jnp.zeros((width, wide - 2 * block - 8), F32))
        tail_out[...] = jnp.concatenate(parts, 1)[:kept].astype(BF16)


def tail_back(ends, later, cb, lb, cum, local, recur, enter, keep, conv, u_ext, same, wz, par, block, into, wide):
    count, rows, width = cb.shape
    shapes = [
        jax.ShapeDtypeStruct((count, rows, width), BF16),
        jax.ShapeDtypeStruct((count, 16, width), F32),
        jax.ShapeDtypeStruct(into.shape, BF16),
    ]
    last = into.shape[1] // wide - 1
    tall = u_ext.shape[1]
    return call(
        functools.partial(tail_back_kernel, len(ends), block),
        (count,),
        [resident(ends[0].shape)] * (2 * len(ends))
        + [per_piece((rows, width))] * 8
        + [per_piece((tall, width)), per_piece((rows, width)), resident(wz.shape), resident(par.shape)],
        [per_piece((rows, width)), per_piece((16, width)), pl.BlockSpec((into.shape[0], wide), lambda step: (0, last))],
        shapes,
        [pltpu.VMEM((8, width), F32), pltpu.VMEM(wz.shape, F32)],
        SWEEP * count * rows * width,
        60,
    )(*ends, *later, cb, lb, cum, local, recur, enter, keep, conv, u_ext, same, wz, par)


def rows_times_kernel(terms, gained, *refs):
    lefts, rights = refs[:terms], refs[terms : 2 * terms]
    outs = refs[2 * terms + gained :]
    total = None
    for left, right in zip(lefts, rights):
        pieces, rows, inner = left.shape
        term = dot_nn(left[...].reshape(pieces * rows, inner), padded_rows(right[...], inner))
        total = term if total is None else total + term
    if gained:
        factor = refs[2 * terms][...].reshape(total.shape).astype(F32)
        outs[-1][0] = jnp.sum(total * factor, axis=0, keepdims=True)
        outs = outs[:-1]
    put_group(outs, total.astype(BF16))


def rows_times(lefts, rights, blocks, pieces, factor=None):
    rows = lefts[0].shape[1]
    model = rights[0][2]
    tile = column_tile(model)
    steps = model // tile
    groups = len(blocks)
    inner = sum(right.shape[0] for right, _, _ in rights)
    gained = 0 if factor is None else 1

    def right_spec(right, place):
        return pl.BlockSpec((right.shape[0], tile), lambda group, step: (0, place * steps + step))

    out_specs = group_outs(rows, tile, steps, blocks, pieces)
    shapes = [jax.ShapeDtypeStruct((pieces, rows, model), BF16)] * groups
    extra_specs = []
    if gained:
        first, stride = blocks[0], (blocks[-1] - blocks[0]) // max(1, groups - 1)
        out_specs.append(pl.BlockSpec((1, 1, tile), lambda group, step: (group, 0, step)))
        shapes.append(jax.ShapeDtypeStruct((groups, 1, model), F32))
        extra_specs.append(
            pl.BlockSpec((pieces, rows, tile), lambda group, step: (first + stride * group, 0, step))
        )
    return call(
        functools.partial(rows_times_kernel, len(lefts), gained),
        (groups, steps),
        [group_of(left.shape[1:], blocks, pieces) for left in lefts]
        + [right_spec(right, place) for right, place, _ in rights]
        + extra_specs,
        out_specs,
        shapes,
        [],
        3 + 2 * groups * pieces * rows * inner * model / RATE,
        grown(20, pieces, 4),
    )(*lefts, *[right for right, _, _ in rights], *([factor] if gained else []))


def assemble_kernel(count, *refs):
    parts, whole, buf, sems, all_sems = refs[:count], refs[count], *refs[count + 1 :]
    fetch_all(parts, buf, sems)
    for index in range(count):
        fetched(parts, buf, sems, index)
        put(buf, whole, all_sems, index).start()
    for index in range(count):
        put(buf, whole, all_sems, index).wait()


def assemble(pieces):
    count = len(pieces)
    shape = (count,) + pieces[0].shape
    return call(
        functools.partial(assemble_kernel, count),
        (1,),
        [ANY] * count,
        ANY,
        jax.ShapeDtypeStruct(shape, pieces[0].dtype),
        [pltpu.VMEM(shape, pieces[0].dtype), pltpu.SemaphoreType.DMA((count,)), pltpu.SemaphoreType.DMA((count,))],
        6.5,
        grown(16, count),
    )(*pieces)


def mlp_kernel(count, first, *refs):
    sources = count if first else 1
    h_refs = refs[:count] if first else [refs[0].at[index] for index in range(count)]
    c_ref, wg, wu, wo, hid_out, dg_out, du_out = refs[sources : sources + 7]
    rest = refs[sources + 7 :]
    all_out = rest[0] if first else None
    h_buf, c_buf, h_sems, c_sems, all_sems = rest[-5:]
    step = pl.program_id(0)
    pair = 2 if count % 2 == 0 else 1
    rows, tile = hid_out.shape[1:]
    model = h_buf.shape[2]

    @pl.when(step == 0)
    def _():
        for index in range(count):
            pltpu.make_async_copy(h_refs[index], h_buf.at[index], h_sems.at[index]).start()
            pltpu.make_async_copy(c_ref.at[index], c_buf.at[index], c_sems.at[index]).start()

    def some_pieces(index, carry):
        @pl.when(step == 0)
        def _():
            for place in range(pair):
                at = index * pair + place
                fetched(h_refs, h_buf, h_sems, at)
                pltpu.make_async_copy(c_ref.at[0], c_buf.at[at], c_sems.at[at]).wait()
                if first:
                    put(h_buf, all_out, all_sems, at).start()

        span = pl.ds(index * pair, pair)
        h_low = h_buf[span].reshape(pair * rows, model)
        gate = dot_nt(h_low, wg[...])
        up = dot_nt(h_low, wu[...])
        d_hidden = dot_nt(c_buf[span].reshape(pair * rows, model), wo[...])
        value, slope = gelu_parts(gate)
        shape = (pair, rows, tile)
        hid_out[span] = (value * up).astype(BF16).reshape(shape)
        dg_out[span] = (d_hidden * up * slope).astype(BF16).reshape(shape)
        du_out[span] = (d_hidden * value).astype(BF16).reshape(shape)
        return carry

    lax.fori_loop(0, count // pair, some_pieces, 0)

    if first:

        @pl.when(step == pl.num_programs(0) - 1)
        def _():
            for index in range(count):
                put(h_buf, all_out, all_sems, index).wait()


def hidden_tile(hidden):
    return next(t for t in (256, 128, hidden) if hidden % t == 0)


def mlp_part(h_rows, c_all, weights):
    first = isinstance(h_rows, list)
    count, rows, model = c_all.shape
    hidden = weights.shape[0]
    tile = hidden_tile(hidden)
    spec = pl.BlockSpec((count, rows, tile), lambda step: (0, 0, step))
    whole = jax.ShapeDtypeStruct((count, rows, model), BF16)
    sources = h_rows if first else [h_rows]

    def column(place):
        return pl.BlockSpec((tile, model), lambda step: (step, place))

    return call(
        functools.partial(mlp_kernel, count, first),
        (hidden // tile,),
        [ANY] * (len(sources) + 1) + [column(0), column(1), column(2)],
        [spec] * 3 + [ANY] * first,
        [jax.ShapeDtypeStruct((count, rows, hidden), BF16)] * 3 + [whole] * first,
        [
            pltpu.VMEM((count, rows, model), BF16),
            pltpu.VMEM((count, rows, model), BF16),
            pltpu.SemaphoreType.DMA((count,)),
            pltpu.SemaphoreType.DMA((count,)),
            pltpu.SemaphoreType.DMA((count,)),
        ],
        2 + 6 * count * rows * model * hidden / RATE,
        grown(42, count) if first else 60,
    )(*sources, c_all, weights, weights, weights)


def mlp_grads_kernel(dg, du, hid, h_tile, c_tile, out, turned, slots, sems):
    step = pl.program_id(0)
    steps = pl.num_programs(0)
    tall, tile = slots.shape[2:]
    model = steps * tile
    slot = step % 2

    def sending(place, at, slot):
        columns = pl.ds(pl.multiple_of(place * model + at * tile, tile), tile)
        return pltpu.make_async_copy(slots.at[slot, place], out.at[:, columns], sems.at[slot, place])

    @pl.when(step == 0)
    def _():
        for place, left in enumerate((dg, du, hid)):
            turned[place * tall : place * tall + tall, :] = left[...].T

    @pl.when(step >= 2)
    def _():
        for place in range(3):
            sending(place, step - 2, slot).wait()

    both = dot_nn(turned[: 2 * tall, :], h_tile[...]).astype(BF16)
    slots[slot, 0] = both[:tall]
    slots[slot, 1] = both[tall:]
    slots[slot, 2] = dot_nn(turned[2 * tall :, :], c_tile[...]).astype(BF16)
    for place in range(3):
        sending(place, step, slot).start()

    @pl.when(step == steps - 1)
    def _():
        for place in range(3):
            sending(place, step - 1, 1 - slot).wait()
            sending(place, step, slot).wait()


def mlp_grads(d_gate, d_up, hidden, h_all, c_all):
    model = h_all.shape[2]
    lefts = [v.reshape(-1, v.shape[2]) for v in (d_gate, d_up, hidden)]
    rights = [v.reshape(-1, model) for v in (h_all, c_all)]
    inner, tall = lefts[0].shape
    tile = min(column_tile(model), model // 2)
    return call(
        mlp_grads_kernel,
        (model // tile,),
        [resident((inner, tall))] * 3 + [pl.BlockSpec((inner, tile), lambda step: (0, step))] * 2,
        ANY,
        jax.ShapeDtypeStruct((tall, 3 * model), BF16),
        [
            pltpu.VMEM((3 * tall, inner), BF16),
            pltpu.VMEM((2, 3, tall, tile), BF16),
            pltpu.SemaphoreType.DMA((2, 3)),
        ],
        3 + 6 * inner * tall * model / RATE,
        grown(40, inner, 2048),
    )(*lefts, *rights)


def weight_grad_kernel(left, right, *refs):
    out, turned = refs[-2:]

    @pl.when(pl.program_id(0) == 0)
    def _():
        turned[...] = left[...].T

    out[...] = dot_nn(turned[...], right[...])[: out.shape[0]].astype(BF16)


def weight_grad(rows_left, rows_right, kept, wide=None, into=None, place=0):
    left = rows_left.reshape(-1, rows_left.shape[-1])
    right = rows_right.reshape(-1, rows_right.shape[-1])
    inner, tall = left.shape
    model = right.shape[1]
    tile = column_tile(model)
    steps = model // tile
    extra = [] if into is None else [into]
    wide = model if wide is None else wide
    shape = (kept, wide) if into is None else into.shape
    return pl.pallas_call(
        weight_grad_kernel,
        grid=(steps,),
        in_specs=[resident(left.shape), pl.BlockSpec((inner, tile), lambda step: (0, step))] + [ANY] * len(extra),
        out_specs=pl.BlockSpec((kept, tile), lambda step: (0, place * steps + step)),
        out_shape=jax.ShapeDtypeStruct(shape, BF16),
        scratch_shapes=[pltpu.VMEM((tall, inner), BF16)],
        input_output_aliases={2: 0} if extra else {},
        **settings(3 + 2 * inner * tall * model / RATE, 1, grown(16, inner, 2048)),
    )(left, right, *extra)


def add_kernel(counts, *refs):
    at = 0
    for count, out in zip(counts, refs[sum(counts) :]):
        total = refs[at][0].astype(F32)
        for ref in refs[at + 1 : at + count]:
            total = total + ref[0].astype(F32)
        out[...] = total.astype(BF16)
        at += count


def add_rows(sums):
    arrays = [array for terms in sums for array, _ in terms]
    places = [index for terms in sums for _, index in terms]
    _, rows, width = arrays[0].shape
    steps = 4
    tall = rows // steps

    def spec(place):
        return pl.BlockSpec((1, tall, width), lambda step: (place, step, 0))

    counts = [len(terms) for terms in sums]
    return call(
        functools.partial(add_kernel, counts),
        (steps,),
        [spec(place) for place in places],
        [pl.BlockSpec((tall, width), lambda step: (step, 0))] * len(sums),
        [jax.ShapeDtypeStruct((rows, width), BF16)] * len(sums),
        [],
        1 + 0.6 * len(arrays),
        12,
    )(*arrays)


def last_kernel(terms, *refs):
    rows, base, gain, out = refs[terms:]
    total = refs[0][0].astype(F32)
    for ref in refs[1:terms]:
        total = total + ref[0].astype(F32)
    if gain is not None:
        x_val = rows[...].astype(F32)
        root = lax.rsqrt(jnp.mean(x_val * x_val, axis=-1, keepdims=True) + EPS)
        x_val = x_val * root
        total = total * gain[...]
        total = root * (total - x_val * jnp.mean(total * x_val, axis=-1, keepdims=True))
    out[...] = (base[...] + total).astype(BF16)


def last_rows(terms, base, rows=None, gain=None):
    tall, model = base.shape
    steps = 4
    block = pl.BlockSpec((tall // steps, model), lambda step: (step, 0))

    def spec(place):
        return pl.BlockSpec((1, tall // steps, model), lambda step: (place, step, 0))

    extra = [] if gain is None else [rows]
    kernel = last_kernel if gain is not None else lambda count, *refs: last_kernel(
        count, *refs[:count], None, refs[count], None, refs[count + 1]
    )
    return stream(
        functools.partial(kernel, len(terms)),
        (steps,),
        [spec(place) for _, place in terms]
        + [block] * (len(extra) + 1)
        + ([] if gain is None else [resident(gain.shape)]),
        block,
        jax.ShapeDtypeStruct((tall, model), BF16),
        6.0,
    )(*[array for array, _ in terms], *extra, base, *([] if gain is None else [gain]))


def finish_grads_kernel(one_gate, one_up, one_down, two_gate, two_up, two_down, second, both, down, out):
    cut = one_gate.shape[0]
    both[:cut, 0, :] = one_gate[...].astype(F32)
    both[:cut, 1, :] = one_up[...].astype(F32)
    both[cut:, 0, :] = two_gate[...].astype(F32)
    both[cut:, 1, :] = two_up[...].astype(F32)
    down[:cut, :] = one_down[...].astype(F32)
    down[cut:, :] = two_down[...].astype(F32)
    out[...] = second[...].astype(F32)


def finish_grads(one, two, mix, model):
    rows = one.shape[0] + two.shape[0]
    own = mix.shape[0]
    tile = column_tile(model)
    steps = model // tile

    def spec(tall, place):
        return pl.BlockSpec((tall, tile), lambda step: (0, place * steps + step))

    return call(
        finish_grads_kernel,
        (steps,),
        [spec(part.shape[0], place) for part in (one, two) for place in range(3)] + [spec(own, 1)],
        [pl.BlockSpec((rows, 2, tile), lambda step: (0, 0, step)), spec(rows, 0), spec(own, 0)],
        [
            jax.ShapeDtypeStruct((rows, 2, model), F32),
            jax.ShapeDtypeStruct((rows, model), F32),
            jax.ShapeDtypeStruct((own, model), F32),
        ],
        [],
        5.0,
        16,
    )(one, one, one, two, two, two, mix)


def part_grads_kernel(block, first, second, tail, both, gate_w, rows):
    both[:, 0, :] = first[...].astype(F32)
    both[:, 1, :] = second[...].astype(F32)

    @pl.when(pl.program_id(0) == 0)
    def _():
        held = tail[...]
        gate_w[:, 0, :] = held[:, :block].astype(F32)
        gate_w[:, 1, :] = held[:, block : 2 * block].astype(F32)
        count = held.shape[0]
        row = lax.broadcasted_iota(jnp.int32, (count, count), 0)
        column = lax.broadcasted_iota(jnp.int32, (count, count), 1)
        rows[...] = dot_tn(held[:, 2 * block : 2 * block + 8], jnp.where(row == column, 1.0, 0.0).astype(BF16))


def part_grads(grads, last, model, wide, block):
    rows = grads.shape[0]
    tile = column_tile(model)
    steps = model // tile
    spec = pl.BlockSpec((rows, tile), lambda step: (0, step))
    return call(
        functools.partial(part_grads_kernel, block),
        (steps,),
        [spec, spec, pl.BlockSpec((rows, wide), lambda step: (0, model // wide))],
        [pl.BlockSpec((rows, 2, tile), lambda step: (0, 0, step)), resident((rows, 2, block)), resident((8, rows))],
        [
            jax.ShapeDtypeStruct((rows, 2, model), F32),
            jax.ShapeDtypeStruct((rows, 2, block), F32),
            jax.ShapeDtypeStruct((8, rows), F32),
        ],
        [],
        3.0,
        16,
    )(grads, last, last)


def seq_gather(shard):
    return lax.all_gather(shard, "seq", axis=0, tiled=True)


def seq_scatter(whole):
    return lax.psum_scatter(whole, "seq", scatter_dimension=0, tiled=True)


def per_device(
    tokens,
    cotangent,
    doc_ids,
    mix_in,
    mix_out,
    gate_w,
    conv_w,
    conv_bias,
    gate_bias,
    decay_param,
    gain_one,
    gain_two,
    mlp_in,
    mlp_out,
):
    run_len, model = tokens.shape[1:]
    n_seq = lax.axis_size("seq")
    n_dev = lax.axis_size("dp") * n_seq
    own = mix_out.shape[0]
    block = gate_w.shape[2]
    chan = own * n_seq
    width = -(-chan // 128) * 128
    blocks = chan // block

    x_low = tokens.reshape(run_len, model)
    x_pieces, _ = gather_rows(x_low)
    x_zero = x_low.astype(F32)
    cot_low = cotangent.reshape(run_len, model)
    lead = hand_on(x_low[run_len - HALO :], 1)
    part = gain_one.shape[0]
    gains = jnp.concatenate([gain_one, gain_two]).astype(BF16)[None]
    my_run = lax.axis_index("seq")
    first_token = my_run * run_len
    places = lax.broadcasted_iota(jnp.int32, (n_seq, 1), 0)
    gain_rows = jnp.where(places == my_run, gains, jnp.zeros((), BF16))
    for hop in range(1, n_seq):
        ring = [(source, (source + hop) % n_seq) for source in range(n_seq)]
        arrived = lax.ppermute(gains, "seq", ring)
        gain_rows = jnp.where(places == (my_run - hop) % n_seq, arrived, gain_rows)
    gain_rows = jnp.pad(gain_rows.reshape(1, -1), ((0, 0), (0, model - 2 * part * n_seq)))
    padded = jnp.concatenate([jnp.full((3,), -1, jnp.int32), doc_ids.reshape(-1)])
    own_docs = lax.dynamic_slice_in_dim(padded, first_token + 3, run_len)
    same = sum(
        jnp.where(lax.dynamic_slice_in_dim(padded, first_token + 3 - back, run_len) == own_docs, 1.0, 0.0)
        for back in (1, 2, 3)
    )
    info = jnp.pad(same, (0, model - run_len)).astype(BF16)[None]
    tops, _ = gather_rows(jnp.concatenate([info, gain_rows, lead[2:]], 0))
    count = len(tops)
    half = count // 2

    small = jnp.concatenate(
        [
            gate_w.reshape(own, 2 * block),
            conv_w.T,
            conv_bias[:, None],
            gate_bias.T,
            decay_param[:, None],
        ],
        1,
    )
    extra = -(-small.shape[1] // 128) * 128
    small = jnp.pad(small, ((0, 0), (0, extra - small.shape[1])))
    w_in = jnp.concatenate([mix_in[:, 1, :], mix_in[:, 0, :], mix_out, small], 1).astype(BF16)
    w_in = seq_gather(w_in)
    mlp_in, mlp_out = after((mlp_in, mlp_out), lead)
    shard = jnp.concatenate([mlp_in.astype(BF16).reshape(-1, 2 * model), mlp_out.astype(BF16)], 1)
    cut = 2 * shard.shape[0] // 3
    shards = [shard[:cut], shard[cut:]]
    w_one, w_two = [seq_gather(rows) for rows in shards]

    orders = jnp.asarray(piece_order(count), jnp.int32)
    order = lax.dynamic_index_in_dim(after(orders, lead), lax.axis_index("dp"), 0, False)
    places = lax.broadcasted_iota(jnp.int32, (count, 1), 0)
    gain_rows = jnp.zeros((count, 2 * part * n_seq), F32)
    for index, piece in enumerate(tops):
        row = piece[1:2, : 2 * part * n_seq].astype(F32)
        gain_rows = jnp.where(places == order[index], row, gain_rows)
    gain_rows = gain_rows.reshape(n_dev, 2 * part)
    g_one = gain_rows[:, :part].reshape(1, model)
    g_two = gain_rows[:, part:].reshape(1, model)

    h_all, h_one, same = first_norm(x_pieces, tops, g_one, width)
    c_pieces, (same, entered) = gather_rows(
        after(cot_low, *x_pieces),
        [
            ((1, 2), lambda sent, done: same),
            ((3,), lambda sent, done: mixer_enter(after(h_all, shards), done[0], w_in, extra, block)),
        ],
    )
    (u_ext, y_pre, conv, recur, enter, keep, cum, local, ends, w_z, par) = entered
    earlier = [hand_on(ends, steps) for steps in range(1, n_seq)]

    def leaving(blocks_at, pieces, before):
        return mixer_leave(earlier, cum, local, after(y_pre, *before), w_in, model, blocks_at, pieces)

    kept = []
    x_one = x_zero + scatter_rows(leaving, count, None)
    n_two, norm_two_back = jax.vjp(rms_norm, x_one, g_two)
    h_two = n_two.astype(BF16)

    h_pieces, (c_all,) = gather_rows(h_two, [((1, 2), lambda sent, done: assemble(after(c_pieces, sent)))])
    hid_one, gate_one, up_one, h_all = mlp_part(h_pieces, c_all, w_one)
    grad_one = mlp_grads(gate_one, up_one, hid_one, h_all, c_all)
    hid_two, gate_two, up_two = mlp_part(after(h_all, grad_one), c_all, w_two)
    grad_one = seq_scatter(grad_one)

    def d_entering(blocks_at, pieces, before):
        lefts = [after(gate_one, *before), up_one, gate_two, up_two]
        rights = [(w_one, 0, model), (w_one, 1, model), (w_two, 0, model), (w_two, 1, model)]
        return rows_times(lefts, rights, blocks_at, pieces)

    def second_grads(sent, done):
        return mlp_grads(after(gate_two, sent), up_two, hid_two, h_all, c_all), grad_one

    def mlp_leaving(blocks_at, pieces, before):
        return rows_times([after(hid_one, *before), hid_two], [(w_one, 2, model), (w_two, 2, model)], blocks_at, pieces)

    def mlp_out_rows(sent):
        return mlp_leaving([1, 0], half, (sent,))

    d_h_two = scatter_rows(d_entering, count, beside(mlp_out_rows, kept))
    d_x_norm, d_gain_two = norm_two_back(d_h_two)
    d_x_one = cot_low.astype(F32) + d_x_norm
    d_mix = d_x_one.astype(BF16)

    stages, twin = plane_stages(lax.axis_size("dp"))

    def mlp_out_sums(sent, done):
        theirs, mine = after(kept.pop(), sent)
        there = lax.ppermute(theirs, "dp", twin)
        return mine, there, add_rows([[(mine, k), (there, k)] for k in range(half // 2, half)])

    d_pieces, done = gather_rows(d_mix, [((1, 2), second_grads), ((3,), mlp_out_sums)])
    (grad_two, grad_one), (mine, there, far) = done
    grad_two = seq_scatter(after(grad_two, grad_one))
    d_y, mixed, cum_back, local_back, ends_back, d_all = head_back(
        after(d_pieces, far), earlier, cum, local, y_pre, keep, w_in
    )
    got = [lax.ppermute(part, "dp", stages[-1]) for part in far]
    mixed, got = lax.optimization_barrier((mixed, got))
    later = [hand_on(ends_back, -steps) for steps in range(1, n_seq)]
    wide = next(t for t in (128, 256, 512, 1024) if t >= 2 * block + 8 and model % t == 0)
    terms = [[(mine, k), (there, k), (got[k][None], 0)] for k in range(half // 2)]
    layer_sums = add_rows(terms[half // 4 :])
    grad_mix = weight_grad(after(d_y, ends_back, layer_sums), h_one, chan, 2 * model)
    grad_mix = weight_grad(mixed, d_all, chan, into=grad_mix, place=1)
    later, grad_mix, grad_two = lax.optimization_barrier((later, grad_mix, grad_two))
    grad_mix = seq_scatter(grad_mix)
    layer_got = [lax.ppermute(part, "dp", stages[-2]) for part in layer_sums]
    tailed = tail_back(
        earlier,
        later,
        cum_back,
        local_back,
        cum,
        local,
        recur,
        enter,
        keep,
        conv,
        u_ext,
        same,
        w_z,
        par,
        block,
        jax.ShapeDtypeStruct((chan, model + wide), BF16),
        wide,
    )
    (d_u, edges, grad_u), layer_got = lax.optimization_barrier((tailed, layer_got))
    terms = [[*those, (one[None], 0)] for those, one in zip(terms, layer_got)]
    from_next = hand_on(edges[:, :8], -1)
    layer_terms = scatter_tail(terms, stages[:-2], [])
    arrays = after([array for array, _ in layer_terms], edges)
    layer_out = last_rows([(v, at) for v, (_, at) in zip(arrays, layer_terms)], x_one)
    from_next, layer_out = lax.optimization_barrier((from_next, layer_out))
    layer_out = layer_out.reshape(1, run_len, model)
    d_u = lax.dynamic_update_slice(d_u, (edges[:, 8:] + from_next).astype(BF16), (0, run_len - 8, 0))
    gain_terms = []

    def d_leaving(blocks_at, pieces, before):
        *part_rows, gain_term = rows_times(
            [after(d_y, *before), d_u], [(w_in, 1, model), (w_in, 0, model)], blocks_at, pieces, h_one
        )
        gain_terms.append(gain_term.sum(0))
        return part_rows

    def u_grad(sent):
        return weight_grad(after(d_u, sent), h_one, chan, into=grad_u, place=0)

    def finished(sent):
        return finish_grads(after(grad_one, sent), grad_two, grad_mix, model)

    ready = []
    d_h_one = scatter_terms(d_leaving, count, beside(finished, ready), beside(u_grad, kept))
    grad_mlp_in, grad_mlp_out, grad_out = ready.pop()
    grad_u = seq_scatter(after(kept.pop(), grad_mix))
    input_grad = last_rows(d_h_one, d_x_one, x_low, g_one)
    d_gain_one = sum(gain_terms) / g_one
    d_gains = jnp.concatenate([d_gain_one.reshape(n_dev, part), d_gain_two.reshape(n_dev, part)], 1)
    d_gains = lax.all_to_all(after(d_gains, input_grad), ("dp", "seq"), 0, 0, tiled=True).sum(0)
    grad_mix_in, grad_gate_w, rows = part_grads(after(grad_mix, grad_out), grad_u, model, wide, block)
    return (
        layer_out,
        input_grad.reshape(1, run_len, model),
        grad_mix_in,
        grad_out,
        grad_gate_w,
        rows[:4],
        rows[4],
        rows[5:7],
        rows[7],
        d_gains[:part],
        d_gains[part:],
        grad_mlp_in,
        grad_mlp_out,
    )


def solution(mesh):
    rows = P(("dp", "seq"))
    placed = (
        P("dp", "seq", None),
        P("dp", "seq", None),
        P("dp", None),
        P(("dp", "seq"), None, None),
        P(("dp", "seq"), None),
        P(("dp", "seq"), None, None),
        P(None, ("dp", "seq")),
        rows,
        P(None, ("dp", "seq")),
        rows,
        rows,
        rows,
        P(("dp", "seq"), None, None),
        P(("dp", "seq"), None),
    )
    return jax.shard_map(
        per_device,
        mesh=mesh,
        in_specs=placed,
        out_specs=placed[:2] + placed[3:],
        check_vma=False,
    )
```

```python
import functools

import jax
import jax.numpy as jnp
from jax import lax
from jax.experimental import pallas as pl
from jax.experimental.pallas import tpu as pltpu
from jax.sharding import PartitionSpec as P

EPS = 1e-06
FLOOR = 0.0001
SHARP = 8.0
HALO = 16
F32 = jnp.float32
BF16 = jnp.bfloat16
MEBI = 1024 * 1024
ANY = pl.BlockSpec(memory_space=pl.ANY)
ROOT = 0.7978845608028654
CUBE = 0.044715
SLOW = 4.5
RATE = 650e6
SWEEP = 25e-6


def dot_nt(left, right):
    return lax.dot_general(left, right, (((1,), (1,)), ((), ())), preferred_element_type=F32)


def dot_nn(left, right):
    return lax.dot_general(left, right, (((1,), (0,)), ((), ())), preferred_element_type=F32)


def dot_tn(left, right):
    return lax.dot_general(left, right, (((0,), (0,)), ((), ())), preferred_element_type=F32)


def rms_norm(values, gain_vec):
    return values * lax.rsqrt(jnp.mean(values * values, axis=-1, keepdims=True) + EPS) * gain_vec


def gelu_parts(values):
    squared = values * values
    bend = jnp.tanh(ROOT * (values + CUBE * values * squared))
    half = 0.5 * (1.0 + bend)
    slope = half + 0.5 * values * (1.0 - bend * bend) * (ROOT * (1.0 + 3.0 * CUBE * squared))
    return values * half, slope


def gelu_value(values):
    bend = jnp.tanh(ROOT * (values + CUBE * values * values * values))
    return values * (0.5 * (1.0 + bend))


def plane_stages(count):
    bits = count.bit_length() - 1
    upper = list(range(1, bits))
    stages = []
    for place in range(len(upper)):
        pairs = []
        for source in range(count):
            shift = place if source % 2 == 0 else (place + 1) % len(upper)
            pairs.append((source, source ^ (1 << upper[shift])))
        stages.append(pairs)
    twin = [(source, source ^ 1) for source in range(count)]
    return stages, twin


def gather_rows(piece, beside=()):
    stages, twin = plane_stages(lax.axis_size("dp"))
    held = [piece] + [None] * (2 ** len(stages) - 1)
    done = []
    before = ()

    def arrival(m):
        top = m.bit_length() - 1
        return lax.ppermute(held[m ^ (1 << top)], "dp", stages[top])

    for members, work in beside:
        arrived = [arrival(m) for m in members]
        sent = [held[m ^ (1 << (m.bit_length() - 1))] for m in members]
        arrived, made = lax.optimization_barrier((arrived, work((sent, before), done)))
        before = arrived
        done.append(made)
        for m, part in zip(members, arrived):
            held[m] = part
    for m in range(1, len(held)):
        if held[m] is None:
            held[m] = arrival(m)
    return held + [lax.ppermute(part, "dp", twin) for part in held], done


def after(value, *others):
    return lax.optimization_barrier((value, others))[0]


def total_of(terms):
    return sum(array[place].astype(F32) for array, place in terms)


def scatter_tail(terms, stages, waits, late=()):
    for place, pairs in enumerate(reversed(stages)):
        split = len(terms) // 2
        sent = add_rows(terms[split:], 60)
        if late:
            sent, late = lax.optimization_barrier((sent, late))
            terms = [[*those, (one[None], 0)] for those, one in zip(terms, late)] + terms[split:]
            late = ()
        got = [lax.ppermute(part, "dp", pairs) for part in sent]
        if place < len(waits):
            got = waits[place](sent, got)
        terms = [[*those, (one[None], 0)] for those, one in zip(terms, got)]
    return terms[0]


def scatter_terms(make, count, wait, ahead=None):
    stages, twin = plane_stages(lax.axis_size("dp"))
    quarter = count // 4
    theirs = make([3], quarter, ())[0]
    there = lax.ppermute(theirs, "dp", twin)
    far = make([1], quarter, (theirs,))[0]
    sent = add_rows([[(far, k), (there, k)] for k in range(quarter)])
    got = [lax.ppermute(part, "dp", stages[-1]) for part in sent]
    split = quarter // 2
    theirs, near = make([2, 0], quarter, (sent,))
    extra = () if ahead is None else ahead(theirs)
    theirs, near, got[split:], extra = lax.optimization_barrier((theirs, near, got[split:], extra))
    there = lax.ppermute(theirs, "dp", twin)
    terms = [[(near, k), (there, k)] for k in range(quarter)]
    terms = terms[:split] + [[*terms[k], (got[k][None], 0)] for k in range(split, quarter)]
    late = got[:split]
    return scatter_tail(terms, stages[:-1], [wait] if wait else [], late), extra


def scatter_rows(make, count, wait):
    return total_of(scatter_terms(make, count, wait)[0])


def beside(work, done):
    def wait(sent, got):
        got, made = lax.optimization_barrier((got, work(sent)))
        done.append(made)
        return got

    return wait


def piece_order(count):
    stages, twin = plane_stages(count)
    orders = []
    for device in range(count):
        held, other = [device], [twin[device][1]]
        for pairs in stages:
            held = held + [pairs[place][1] for place in held]
            other = other + [pairs[place][1] for place in other]
        orders.append(held + other)
    return orders


def hand_on(value, steps):
    count = lax.axis_size("seq")
    first, last = (max(0, -steps), min(count, count - steps))
    return lax.ppermute(value, "seq", [(source, source + steps) for source in range(first, last)])


def scan_into(keep, entry, cum_ref, state_ref, backward):
    rows, width = keep.shape
    groups = rows // 8
    mult = keep.reshape(groups, 8, width)
    total = entry.reshape(groups, 8, width)
    place = lax.broadcasted_iota(jnp.int32, (groups, 8, width), 1)
    for hop in (1, 2, 4):
        if backward:
            shift, valid = 8 - hop, place < 8 - hop
        else:
            shift, valid = hop, place >= hop
        near_mult = pltpu.roll(mult, shift, 1)
        near_total = pltpu.roll(total, shift, 1)
        total = jnp.where(valid, total + mult * near_total, total)
        mult = jnp.where(valid, mult * near_mult, mult)
    carry_total = jnp.zeros((1, width), F32)
    carry_mult = jnp.ones((1, width), F32)
    edge = 0 if backward else 7
    order = range(groups - 1, -1, -1) if backward else range(groups)
    for group in order:
        now_total = total[group] + mult[group] * carry_total
        now_mult = mult[group] * carry_mult
        state_ref[0, group * 8 : group * 8 + 8, :] = now_total
        cum_ref[0, group * 8 : group * 8 + 8, :] = now_mult
        carry_total = now_total[edge : edge + 1]
        carry_mult = now_mult[edge : edge + 1]
    return carry_mult, carry_total


def folded(refs, piece):
    at = pl.ds(piece, 1)
    carry = refs[-1][1, at, :]
    for ref in refs[-2::-1]:
        carry = ref[1, at, :] + ref[0, at, :] * carry
    return carry


def put_ends(ref, piece, mult, total):
    ref[0, pl.ds(piece, 1), :] = mult
    ref[1, pl.ds(piece, 1), :] = total


def fetch_all(refs, buf, sems):
    for index, ref in enumerate(refs):
        pltpu.make_async_copy(ref, buf.at[index], sems.at[index]).start()


def fetched(refs, buf, sems, index):
    pltpu.make_async_copy(refs[0], buf.at[index], sems.at[index]).wait()


def put(buf, whole, sems, index):
    return pltpu.make_async_copy(buf.at[index], whole.at[index], sems.at[index])


def padded_rows(rows, width):
    missing = width - rows.shape[0]
    return jnp.concatenate([rows, jnp.zeros((missing, rows.shape[1]), rows.dtype)], 0) if missing else rows


def first_norm_kernel(count, *refs):
    x_refs, top_refs = refs[:count], refs[count : 2 * count]
    gain, all_out, h_out, m_out, buf, top, sems, top_sems = refs[2 * count :]
    step = pl.program_id(0)

    @pl.when(step == 0)
    def _():
        fetch_all(top_refs, top, top_sems)
        fetch_all(x_refs, buf, sems)

    fetched(top_refs, top, top_sems, step)
    fetched(x_refs, buf, sems, step)
    rows, width = m_out.shape[1:]
    top_val = top[step].astype(F32)
    info = jnp.broadcast_to(top_val[0:1, :rows], (width, rows)).astype(BF16)
    across = lax.broadcasted_iota(jnp.int32, (rows, rows), 0)
    down = lax.broadcasted_iota(jnp.int32, (rows, rows), 1)
    m_out[0] = dot_nt(jnp.where(across == down, 1.0, 0.0).astype(BF16), info).astype(BF16)
    all_out[0, :HALO] = rms_norm(top_val, gain[...]).astype(BF16)
    h_low = rms_norm(buf[step].astype(F32), gain[...]).astype(BF16)
    all_out[0, HALO:] = h_low
    h_out[0] = h_low


def first_norm(pieces, tops, gain, width):
    count = len(pieces)
    rows, model = pieces[0].shape
    shapes = [
        jax.ShapeDtypeStruct((count, rows + HALO, model), BF16),
        jax.ShapeDtypeStruct((count, rows, model), BF16),
        jax.ShapeDtypeStruct((count, rows, width), BF16),
    ]
    return call(
        functools.partial(first_norm_kernel, count),
        (count,),
        [ANY] * (2 * count) + [resident(gain.shape)],
        [per_piece(s.shape[1:]) for s in shapes],
        shapes,
        [
            pltpu.VMEM((count, rows, model), BF16),
            pltpu.VMEM((count, HALO, model), BF16),
            pltpu.SemaphoreType.DMA((count,)),
            pltpu.SemaphoreType.DMA((count,)),
        ],
        2.6e-6 * count * rows * model,
        60,
    )(*pieces, *tops, gain)


def block_masks(width, block):
    row = lax.broadcasted_iota(jnp.int32, (width, width), 0)
    column = lax.broadcasted_iota(jnp.int32, (width, width), 1)
    inside = None
    for start in range(0, width, block):
        here = (row >= start) & (row < start + block) & (column >= start) & (column < start + block)
        inside = here if inside is None else inside | here
    row = lax.broadcasted_iota(jnp.int32, (width, block), 0)
    column = lax.broadcasted_iota(jnp.int32, (width, block), 1)
    fold = None
    for start in range(0, width, block):
        here = row - start == column
        fold = here if fold is None else fold | here
    return inside, jnp.where(fold, 1.0, 0.0).astype(BF16)


def sigmoid(values):
    return 0.5 * jnp.tanh(0.5 * values) + 0.5


def softplus(values):
    small = jnp.exp(-jnp.abs(values))
    grown = 1.0 + small
    exact = jnp.where(grown == 1.0, small, jnp.log(grown) * small / jnp.where(grown == 1.0, 1.0, grown - 1.0))
    return jnp.maximum(values, 0.0) + exact


def mixer_enter_kernel(
    block,
    h_ref,
    m_ref,
    wu,
    wy,
    small,
    u_out,
    y_out,
    conv_out,
    r_out,
    e_out,
    k_out,
    a_out,
    s_out,
    ends,
    wz,
    par,
    w_all,
    both,
):
    width = wz.shape[1]
    some, tall, model = h_ref.shape
    rows = tall - HALO
    place = pl.program_id(0) % some

    @pl.when(pl.program_id(0) == 0)
    def _():
        w_all[:width, :] = padded_rows(wu[...], width)
        w_all[width:, :] = padded_rows(wy[...], width)
        params = padded_rows(small[...], width)
        inside, fold = block_masks(width, block)
        for gate in (0, 1):
            spread = dot_nt(params[:, gate * block : gate * block + block], fold)
            wz[gate * width : gate * width + width, :] = jnp.where(inside, spread, 0.0).astype(BF16)
        row = lax.broadcasted_iota(jnp.int32, (width, width), 0)
        column = lax.broadcasted_iota(jnp.int32, (width, width), 1)
        same = jnp.where(row == column, 1.0, 0.0).astype(BF16)
        turned = dot_tn(params[:, 2 * block : 2 * block + 8], same)
        par[0:8, :] = turned
        par[8:16, :] = turned
        par[7:8, :] = -SHARP * softplus(turned[7:8, :])

    @pl.when(place == 0)
    def _():
        both[...] = dot_nt(h_ref[...].reshape(some * tall, model), w_all[...]).reshape(both.shape)

    u_low = both[place, :, :width].astype(BF16)
    u_out[0] = u_low
    y_out[0] = both[place, HALO:, width:]
    same = m_ref[0].astype(F32)
    u_val = u_low.astype(F32)
    conv = par[4:5, :] + par[0:1, :] * u_val[HALO:]
    for back in (1, 2, 3):
        term = par[back : back + 1, :] * u_val[HALO - back : HALO - back + rows]
        conv = conv + jnp.where(same >= back, term, 0.0)
    conv_low = conv.astype(BF16)
    conv_out[0] = conv_low
    conv = conv_low.astype(F32)
    pre = dot_nt(conv_low, wz[...])
    recur = sigmoid(pre[:, :width] + par[5:6, :])
    enter = sigmoid(pre[:, width:] + par[6:7, :])
    keep = jnp.where(same >= 1.0, jnp.exp(par[7:8, :] * recur), 0.0)
    r_out[0] = recur
    e_out[0] = enter
    k_out[0] = keep
    spare = jnp.maximum(1.0 - keep * keep, FLOOR)
    inputs = conv * enter * (spare * lax.rsqrt(spare))
    mult, total = scan_into(keep, inputs, a_out, s_out, False)
    put_ends(ends, pl.program_id(0), mult, total)


def resident(shape):
    zeros = (0,) * len(shape)
    return pl.BlockSpec(shape, lambda step: zeros)


def per_piece(shape, first=0):
    rest = (0,) * len(shape)
    return pl.BlockSpec((1,) + shape, lambda step: (step + first,) + rest)


def grown(memory, count, usual=8):
    return min(60, memory * max(count, usual) // usual)


def settings(micros, axes, memory):
    return dict(
        compiler_params=pltpu.CompilerParams(
            vmem_limit_bytes=memory * MEBI, dimension_semantics=("arbitrary",) * axes if axes else None
        ),
        cost_estimate=pl.CostEstimate(flops=int(micros / SLOW * 1.15e9), bytes_accessed=1024, transcendentals=0),
    )


def call(kernel, grid, in_specs, out_specs, out_shape, scratch, micros, memory, aliases={}):
    return pl.pallas_call(
        kernel,
        grid=grid,
        in_specs=in_specs,
        out_specs=out_specs,
        out_shape=out_shape,
        scratch_shapes=scratch,
        input_output_aliases=aliases,
        **settings(micros, len(grid), memory),
    )


def stream(kernel, grid, in_specs, out_specs, out_shape, micros):
    def outer(*refs):
        pltpu.emit_pipeline(kernel, grid=grid, in_specs=in_specs, out_specs=[out_specs])(*refs)

    here = pl.BlockSpec(memory_space=pltpu.HBM)
    return pl.pallas_call(
        outer,
        in_specs=[here] * len(in_specs),
        out_specs=here,
        out_shape=out_shape,
        **settings(micros, 0, 16),
    )


def mixer_enter(h_all, same, w_in, extra, block):
    count, tall, model = h_all.shape
    rows = tall - HALO
    chan = w_in.shape[0]
    width = same.shape[2]
    some = 1

    def out(height, columns, dtype):
        return jax.ShapeDtypeStruct((count, height, columns), dtype)

    shapes = [out(tall, width, BF16), out(rows, width, F32), out(rows, width, BF16)]
    shapes += [out(rows, width, F32)] * 5
    fixed = [jax.ShapeDtypeStruct((2, count, width), F32)]
    fixed += [jax.ShapeDtypeStruct((2 * width, width), BF16), jax.ShapeDtypeStruct((16, width), F32)]
    return call(
        functools.partial(mixer_enter_kernel, block),
        (count,),
        [
            pl.BlockSpec((some, tall, model), lambda step: (step // some, 0, 0)),
            per_piece((rows, width)),
            pl.BlockSpec((chan, model), lambda step: (0, 0)),
            pl.BlockSpec((chan, model), lambda step: (0, 1)),
            pl.BlockSpec((chan, extra), lambda step: (0, 3 * model // extra)),
        ],
        [per_piece(s.shape[1:]) for s in shapes] + [resident(s.shape) for s in fixed],
        shapes + fixed,
        [pltpu.VMEM((2 * width, model), BF16), pltpu.VMEM((some, tall, 2 * width), F32)],
        SWEEP * count * rows * width,
        grown(26, count),
    )(h_all, same, w_in, w_in, w_in)


def column_tile(model):
    return next(t for t in (512, 256, 128) if model % t == 0)


def group_of(shape, blocks, pieces):
    first, stride = blocks[0], (blocks[-1] - blocks[0]) // max(1, len(blocks) - 1)
    rest = (0,) * len(shape)
    return pl.BlockSpec((pieces,) + shape, lambda group, step: (first + stride * group,) + rest)


def group_outs(rows, tile, steps, blocks, pieces):
    def spec(place):
        def index(group, step):
            at = jnp.clip((group - place) * steps + step, 0, steps - 1)
            return (0, 0, at)

        return pl.BlockSpec((pieces, rows, tile), index)

    return [spec(place) for place in range(len(blocks))]


def put_group(outs, total):
    for place, out in enumerate(outs):

        @pl.when(pl.program_id(0) == place)
        def _(out=out):
            out[...] = total.reshape(out.shape)


def mixer_leave_kernel(hops, pieces, blocks, *refs):
    groups = len(blocks)
    first, stride = blocks[0], (blocks[-1] - blocks[0]) // max(1, groups - 1)
    ends = refs[:hops]
    cum, local, y_pre, w_out = refs[hops : hops + 4]
    mixed = refs[-1]
    rows = cum.shape[1]

    @pl.when(pl.program_id(1) == 0)
    def _():
        for index in range(pieces):
            piece = (first + stride * pl.program_id(0)) * pieces + index
            states = local[index] + cum[index] * folded(ends, piece)
            mixed[index * rows : index * rows + rows, :] = (gelu_value(y_pre[index]) * states).astype(BF16)

    right = padded_rows(w_out[...], mixed.shape[1])
    put_group(refs[hops + 4 : hops + 4 + groups], dot_nn(mixed[...], right).astype(BF16))


def mixer_leave(ends, cum, local, y_pre, w_in, model, blocks, pieces):
    rows, width = cum.shape[1:]
    tile = column_tile(model)
    steps = model // tile
    groups = len(blocks)
    return call(
        functools.partial(mixer_leave_kernel, len(ends), pieces, blocks),
        (groups, steps),
        [pl.BlockSpec(ends[0].shape, lambda group, step: (0, 0, 0))] * len(ends)
        + [group_of((rows, width), blocks, pieces)] * 3
        + [pl.BlockSpec((w_in.shape[0], tile), lambda group, step: (0, 2 * steps + step))],
        group_outs(rows, tile, steps, blocks, pieces),
        [jax.ShapeDtypeStruct((pieces, rows, model), BF16)] * groups,
        [pltpu.VMEM((pieces * rows, width), BF16)],
        3.5 + 3.5 * groups * pieces / 2,
        grown(20, pieces, 2),
    )(*ends, cum, local, y_pre, w_in)


def head_back_kernel(count, hops, *refs):
    d_refs = refs[:count]
    ends = refs[count : count + hops]
    (cum, local, y_pre, keep_ref, w_out, dy_out, mixed_out, cb_out, lb_out, ends_out, all_out, buf, w_all, d_some, sems, all_sems) = refs[count + hops :]
    some = 1
    step = pl.program_id(0)

    @pl.when(step == 0)
    def _():
        fetch_all(d_refs, buf, sems)
        w_all[...] = padded_rows(w_out[...], w_all.shape[0])

    @pl.when(step % some == 0)
    def _():
        for place in range(some):
            fetched(d_refs, buf, sems, step + place)
            put(buf, all_out, all_sems, step + place).start()
        rows, model = buf.shape[1:]
        d_some[...] = dot_nt(buf[pl.ds(step, some)].reshape(some * rows, model), w_all[...]).reshape(d_some.shape)

    d_mixed = d_some[step % some]
    states = local[0] + cum[0] * folded(ends, step)
    value, slope = gelu_parts(y_pre[0])
    mixed_out[0] = (value * states).astype(BF16)
    dy_out[0] = (slope * d_mixed * states).astype(BF16)
    keep = keep_ref[0]
    width = keep.shape[1]
    next_keep = jnp.concatenate([keep[1:], jnp.ones((1, width), F32)], 0)
    mult, total = scan_into(next_keep, d_mixed * value, cb_out, lb_out, True)
    put_ends(ends_out, step, mult * keep[0:1], total * keep[0:1])

    @pl.when(step == count - 1)
    def _():
        for index in range(count):
            put(buf, all_out, all_sems, index).wait()


def head_back(pieces, ends, cum, local, y_pre, keep, w_in):
    count = len(pieces)
    rows, model = pieces[0].shape
    width = cum.shape[2]

    def out(height, dtype):
        return jax.ShapeDtypeStruct((count, height, width), dtype)

    shapes = [out(rows, BF16), out(rows, BF16), out(rows, F32), out(rows, F32)]
    ends_shape = jax.ShapeDtypeStruct((2, count, width), F32)
    return call(
        functools.partial(head_back_kernel, count, len(ends)),
        (count,),
        [ANY] * count
        + [resident(ends[0].shape)] * len(ends)
        + [per_piece((rows, width))] * 4
        + [pl.BlockSpec((w_in.shape[0], model), lambda step: (0, 2))],
        [per_piece(s.shape[1:]) for s in shapes] + [resident(ends_shape.shape), ANY],
        shapes + [ends_shape, jax.ShapeDtypeStruct((count, rows, model), BF16)],
        [
            pltpu.VMEM((count, rows, model), BF16),
            pltpu.VMEM((width, model), BF16),
            pltpu.VMEM((1, rows, width), F32),
            pltpu.SemaphoreType.DMA((count,)),
            pltpu.SemaphoreType.DMA((count,)),
        ],
        SWEEP * count * rows * width,
        grown(25, count),
    )(*pieces, *ends, cum, local, y_pre, keep, w_in)


def tail_back_kernel(hops, block, *refs):
    ends = refs[:hops]
    later = refs[hops : 2 * hops]
    (cb, lb, cum, local, r_ref, e_ref, k_ref, conv_ref, u_ref, m_ref, wz, par, du_out, edge_out, tail_out, small_out, gw_out) = refs[2 * hops :]
    step = pl.program_id(0)

    @pl.when(step == 0)
    def _():
        gw_out[...] = jnp.zeros_like(gw_out)
        small_out[...] = jnp.zeros_like(small_out)

    state_in = folded(ends, step)
    d_states = lb[0] + cb[0] * folded(later, step)
    states = local[0] + cum[0] * state_in
    prev = jnp.concatenate([state_in, states[:-1]], 0)
    recur, enter, keep = r_ref[0], e_ref[0], k_ref[0]
    conv_low = conv_ref[0]
    conv = conv_low.astype(F32)
    rows, width = conv.shape
    spare = 1.0 - keep * keep
    floored = jnp.maximum(spare, FLOOR)
    root = lax.rsqrt(floored)
    scaling = floored * root
    weight = jnp.where(spare > FLOOR, 0.5, jnp.where(spare == FLOOR, 0.25, 0.0)) * root
    d_enter_sum = d_states * conv
    d_spare = d_enter_sum * enter * weight
    d_expo = (d_states * prev - 2.0 * keep * d_spare) * keep
    d_recur = d_expo * par[7:8, :] * recur * (1.0 - recur)
    d_enter = d_enter_sum * scaling * enter * (1.0 - enter)
    d_pre = jnp.concatenate([d_recur.astype(BF16), d_enter.astype(BF16)], 1)
    d_conv = d_states * enter * scaling + dot_nn(d_pre, wz[...])
    gw_out[...] += dot_tn(d_pre, conv_low)
    d_pre_val = d_pre.astype(F32)
    same = m_ref[0].astype(F32)
    u_val = u_ref[0].astype(F32)
    sums = []
    d_u = jnp.zeros((rows, width), F32)
    head = jnp.zeros((8, width), F32)
    for back in range(4):
        masked = d_conv if back == 0 else jnp.where(same >= back, d_conv, 0.0)
        sums.append(jnp.sum(masked * u_val[HALO - back : HALO - back + rows], axis=0, keepdims=True))
        moved = masked * par[back : back + 1, :]
        if back == 0:
            d_u = d_u + moved
        else:
            nothing = jnp.zeros((back, width), F32)
            d_u = d_u + jnp.concatenate([moved[back:], nothing], 0)
            head = head + jnp.concatenate([jnp.zeros((8 - back, width), F32), moved[:back]], 0)
    sums.append(jnp.sum(d_conv, axis=0, keepdims=True))
    sums.append(jnp.sum(d_pre_val[:, :width], axis=0, keepdims=True))
    sums.append(jnp.sum(d_pre_val[:, width:], axis=0, keepdims=True))
    sums.append(jnp.sum(d_expo * recur, axis=0, keepdims=True))
    small_out[...] += jnp.concatenate(sums, 0)
    du_out[0] = d_u.astype(BF16)
    edge_out[0, 0:8, :] = head
    edge_out[0, 8:16, :] = d_u[rows - 8 :]

    @pl.when(step == pl.num_programs(0) - 1)
    def _():
        kept, wide = tail_out.shape
        inside, fold = block_masks(width, block)
        parts = []
        for gate in (0, 1):
            whole = jnp.where(inside, gw_out[gate * width : gate * width + width, :], 0.0).astype(BF16)
            parts.append(dot_nn(whole, fold))
        sums = small_out[...]
        slope = -SHARP * sigmoid(par[15:16, :])
        sums = jnp.concatenate([sums[:7], sums[7:8] * slope], 0).astype(BF16)
        row = lax.broadcasted_iota(jnp.int32, (width, width), 0)
        column = lax.broadcasted_iota(jnp.int32, (width, width), 1)
        parts.append(dot_nt(jnp.where(row == column, 1.0, 0.0).astype(BF16), sums))
        parts.append(jnp.zeros((width, wide - 2 * block - 8), F32))
        tail_out[...] = jnp.concatenate(parts, 1)[:kept].astype(BF16)


def tail_back(ends, later, cb, lb, cum, local, recur, enter, keep, conv, u_ext, same, wz, par, block, into, wide):
    count, rows, width = cb.shape
    shapes = [
        jax.ShapeDtypeStruct((count, rows, width), BF16),
        jax.ShapeDtypeStruct((count, 16, width), F32),
        jax.ShapeDtypeStruct(into.shape, BF16),
    ]
    last = into.shape[1] // wide - 1
    tall = u_ext.shape[1]
    return call(
        functools.partial(tail_back_kernel, len(ends), block),
        (count,),
        [resident(ends[0].shape)] * (2 * len(ends))
        + [per_piece((rows, width))] * 8
        + [per_piece((tall, width)), per_piece((rows, width)), resident(wz.shape), resident(par.shape)],
        [per_piece((rows, width)), per_piece((16, width)), pl.BlockSpec((into.shape[0], wide), lambda step: (0, last))],
        shapes,
        [pltpu.VMEM((8, width), F32), pltpu.VMEM(wz.shape, F32)],
        SWEEP * count * rows * width,
        60,
    )(*ends, *later, cb, lb, cum, local, recur, enter, keep, conv, u_ext, same, wz, par)


def rows_times_kernel(terms, gained, *refs):
    lefts, rights = refs[:terms], refs[terms : 2 * terms]
    outs = refs[2 * terms + gained :]
    total = None
    for left, right in zip(lefts, rights):
        pieces, rows, inner = left.shape
        term = dot_nn(left[...].reshape(pieces * rows, inner), padded_rows(right[...], inner))
        total = term if total is None else total + term
    if gained:
        factor = refs[2 * terms][...].reshape(total.shape).astype(F32)
        outs[-1][0] = jnp.sum(total * factor, axis=0, keepdims=True)
        outs = outs[:-1]
    put_group(outs, total.astype(BF16))


def rows_times(lefts, rights, blocks, pieces, factor=None):
    rows = lefts[0].shape[1]
    model = rights[0][2]
    tile = column_tile(model)
    steps = model // tile
    groups = len(blocks)
    inner = sum(right.shape[0] for right, _, _ in rights)
    gained = 0 if factor is None else 1

    def right_spec(right, place):
        return pl.BlockSpec((right.shape[0], tile), lambda group, step: (0, place * steps + step))

    out_specs = group_outs(rows, tile, steps, blocks, pieces)
    shapes = [jax.ShapeDtypeStruct((pieces, rows, model), BF16)] * groups
    extra_specs = []
    if gained:
        first, stride = blocks[0], (blocks[-1] - blocks[0]) // max(1, groups - 1)
        out_specs.append(pl.BlockSpec((1, 1, tile), lambda group, step: (group, 0, step)))
        shapes.append(jax.ShapeDtypeStruct((groups, 1, model), F32))
        extra_specs.append(
            pl.BlockSpec((pieces, rows, tile), lambda group, step: (first + stride * group, 0, step))
        )
    return call(
        functools.partial(rows_times_kernel, len(lefts), gained),
        (groups, steps),
        [group_of(left.shape[1:], blocks, pieces) for left in lefts]
        + [right_spec(right, place) for right, place, _ in rights]
        + extra_specs,
        out_specs,
        shapes,
        [],
        3 + 2 * groups * pieces * rows * inner * model / RATE,
        grown(20, pieces, 4),
    )(*lefts, *[right for right, _, _ in rights], *([factor] if gained else []))


def assemble_kernel(count, *refs):
    parts, whole, buf, sems, all_sems = refs[:count], refs[count], *refs[count + 1 :]
    fetch_all(parts, buf, sems)
    for index in range(count):
        fetched(parts, buf, sems, index)
        put(buf, whole, all_sems, index).start()
    for index in range(count):
        put(buf, whole, all_sems, index).wait()


def assemble(pieces):
    count = len(pieces)
    shape = (count,) + pieces[0].shape
    return call(
        functools.partial(assemble_kernel, count),
        (1,),
        [ANY] * count,
        ANY,
        jax.ShapeDtypeStruct(shape, pieces[0].dtype),
        [pltpu.VMEM(shape, pieces[0].dtype), pltpu.SemaphoreType.DMA((count,)), pltpu.SemaphoreType.DMA((count,))],
        6.5,
        grown(16, count),
    )(*pieces)


def mlp_kernel(count, first, *refs):
    sources = count if first else 1
    h_refs = refs[:count] if first else [refs[0].at[index] for index in range(count)]
    c_ref, wg, wu, wo, hid_out, dg_out, du_out = refs[sources : sources + 7]
    rest = refs[sources + 7 :]
    all_out = rest[0] if first else None
    h_buf, c_buf, h_sems, c_sems, all_sems = rest[-5:]
    step = pl.program_id(0)
    pair = 2 if count % 2 == 0 else 1
    rows, tile = hid_out.shape[1:]
    model = h_buf.shape[2]

    @pl.when(step == 0)
    def _():
        for index in range(count):
            pltpu.make_async_copy(h_refs[index], h_buf.at[index], h_sems.at[index]).start()
            pltpu.make_async_copy(c_ref.at[index], c_buf.at[index], c_sems.at[index]).start()

    def some_pieces(index, carry):
        @pl.when(step == 0)
        def _():
            for place in range(pair):
                at = index * pair + place
                fetched(h_refs, h_buf, h_sems, at)
                pltpu.make_async_copy(c_ref.at[0], c_buf.at[at], c_sems.at[at]).wait()
                if first:
                    put(h_buf, all_out, all_sems, at).start()

        span = pl.ds(index * pair, pair)
        h_low = h_buf[span].reshape(pair * rows, model)
        gate = dot_nt(h_low, wg[...])
        up = dot_nt(h_low, wu[...])
        d_hidden = dot_nt(c_buf[span].reshape(pair * rows, model), wo[...])
        value, slope = gelu_parts(gate)
        shape = (pair, rows, tile)
        hid_out[span] = (value * up).astype(BF16).reshape(shape)
        dg_out[span] = (d_hidden * up * slope).astype(BF16).reshape(shape)
        du_out[span] = (d_hidden * value).astype(BF16).reshape(shape)
        return carry

    lax.fori_loop(0, count // pair, some_pieces, 0)

    if first:

        @pl.when(step == pl.num_programs(0) - 1)
        def _():
            for index in range(count):
                put(h_buf, all_out, all_sems, index).wait()


def hidden_tile(hidden):
    return next(t for t in (256, 128, hidden) if hidden % t == 0)


def mlp_part(h_rows, c_all, weights):
    first = isinstance(h_rows, list)
    count, rows, model = c_all.shape
    hidden = weights.shape[0]
    tile = hidden_tile(hidden)
    spec = pl.BlockSpec((count, rows, tile), lambda step: (0, 0, step))
    whole = jax.ShapeDtypeStruct((count, rows, model), BF16)
    sources = h_rows if first else [h_rows]

    def column(place):
        return pl.BlockSpec((tile, model), lambda step: (step, place))

    return call(
        functools.partial(mlp_kernel, count, first),
        (hidden // tile,),
        [ANY] * (len(sources) + 1) + [column(0), column(1), column(2)],
        [spec] * 3 + [ANY] * first,
        [jax.ShapeDtypeStruct((count, rows, hidden), BF16)] * 3 + [whole] * first,
        [
            pltpu.VMEM((count, rows, model), BF16),
            pltpu.VMEM((count, rows, model), BF16),
            pltpu.SemaphoreType.DMA((count,)),
            pltpu.SemaphoreType.DMA((count,)),
            pltpu.SemaphoreType.DMA((count,)),
        ],
        2 + 6 * count * rows * model * hidden / RATE,
        grown(42, count) if first else 60,
    )(*sources, c_all, weights, weights, weights)


def mlp_grads_kernel(dg, du, hid, h_tile, c_tile, out, turned, slots, sems):
    step = pl.program_id(0)
    steps = pl.num_programs(0)
    tall, tile = slots.shape[2:]
    model = steps * tile
    slot = step % 2

    def sending(place, at, slot):
        columns = pl.ds(pl.multiple_of(place * model + at * tile, tile), tile)
        return pltpu.make_async_copy(slots.at[slot, place], out.at[:, columns], sems.at[slot, place])

    @pl.when(step == 0)
    def _():
        for place, left in enumerate((dg, du, hid)):
            turned[place * tall : place * tall + tall, :] = left[...].T

    @pl.when(step >= 2)
    def _():
        for place in range(3):
            sending(place, step - 2, slot).wait()

    both = dot_nn(turned[: 2 * tall, :], h_tile[...]).astype(BF16)
    slots[slot, 0] = both[:tall]
    slots[slot, 1] = both[tall:]
    slots[slot, 2] = dot_nn(turned[2 * tall :, :], c_tile[...]).astype(BF16)
    for place in range(3):
        sending(place, step, slot).start()

    @pl.when(step == steps - 1)
    def _():
        for place in range(3):
            sending(place, step - 1, 1 - slot).wait()
            sending(place, step, slot).wait()


def mlp_grads(d_gate, d_up, hidden, h_all, c_all):
    model = h_all.shape[2]
    lefts = [v.reshape(-1, v.shape[2]) for v in (d_gate, d_up, hidden)]
    rights = [v.reshape(-1, model) for v in (h_all, c_all)]
    inner, tall = lefts[0].shape
    tile = min(column_tile(model), model // 2)
    return call(
        mlp_grads_kernel,
        (model // tile,),
        [resident((inner, tall))] * 3 + [pl.BlockSpec((inner, tile), lambda step: (0, step))] * 2,
        ANY,
        jax.ShapeDtypeStruct((tall, 3 * model), BF16),
        [
            pltpu.VMEM((3 * tall, inner), BF16),
            pltpu.VMEM((2, 3, tall, tile), BF16),
            pltpu.SemaphoreType.DMA((2, 3)),
        ],
        3 + 6 * inner * tall * model / RATE,
        grown(40, inner, 2048),
    )(*lefts, *rights)


def weight_grad_kernel(left, right, *refs):
    out, turned = refs[-2:]

    @pl.when(pl.program_id(0) == 0)
    def _():
        turned[...] = left[...].T

    out[...] = dot_nn(turned[...], right[...])[: out.shape[0]].astype(BF16)


def weight_grad(rows_left, rows_right, kept, wide=None, into=None, place=0):
    left = rows_left.reshape(-1, rows_left.shape[-1])
    right = rows_right.reshape(-1, rows_right.shape[-1])
    inner, tall = left.shape
    model = right.shape[1]
    tile = column_tile(model)
    steps = model // tile
    extra = [] if into is None else [into]
    wide = model if wide is None else wide
    shape = (kept, wide) if into is None else into.shape
    return pl.pallas_call(
        weight_grad_kernel,
        grid=(steps,),
        in_specs=[resident(left.shape), pl.BlockSpec((inner, tile), lambda step: (0, step))] + [ANY] * len(extra),
        out_specs=pl.BlockSpec((kept, tile), lambda step: (0, place * steps + step)),
        out_shape=jax.ShapeDtypeStruct(shape, BF16),
        scratch_shapes=[pltpu.VMEM((tall, inner), BF16)],
        input_output_aliases={2: 0} if extra else {},
        **settings(3 + 2 * inner * tall * model / RATE, 1, grown(16, inner, 2048)),
    )(left, right, *extra)


def add_kernel(counts, *refs):
    at = 0
    for count, out in zip(counts, refs[sum(counts) :]):
        total = refs[at][0].astype(F32)
        for ref in refs[at + 1 : at + count]:
            total = total + ref[0].astype(F32)
        out[...] = total.astype(BF16)
        at += count


def add_rows(sums, memory=12):
    arrays = [array for terms in sums for array, _ in terms]
    places = [index for terms in sums for _, index in terms]
    _, rows, width = arrays[0].shape
    steps = 4
    tall = rows // steps

    def spec(place):
        return pl.BlockSpec((1, tall, width), lambda step: (place, step, 0))

    counts = [len(terms) for terms in sums]
    return call(
        functools.partial(add_kernel, counts),
        (steps,),
        [spec(place) for place in places],
        [pl.BlockSpec((tall, width), lambda step: (step, 0))] * len(sums),
        [jax.ShapeDtypeStruct((rows, width), BF16)] * len(sums),
        [],
        1 + 0.6 * len(arrays),
        memory,
    )(*arrays)


def last_kernel(terms, *refs):
    rows, base, gain, out = refs[terms:]
    total = refs[0][0].astype(F32)
    for ref in refs[1:terms]:
        total = total + ref[0].astype(F32)
    if gain is not None:
        x_val = rows[...].astype(F32)
        root = lax.rsqrt(jnp.mean(x_val * x_val, axis=-1, keepdims=True) + EPS)
        x_val = x_val * root
        total = total * gain[...]
        total = root * (total - x_val * jnp.mean(total * x_val, axis=-1, keepdims=True))
    out[...] = (base[...] + total).astype(BF16)


def last_rows(terms, base, rows=None, gain=None):
    tall, model = base.shape
    steps = 4
    block = pl.BlockSpec((tall // steps, model), lambda step: (step, 0))

    def spec(place):
        return pl.BlockSpec((1, tall // steps, model), lambda step: (place, step, 0))

    extra = [] if gain is None else [rows]
    kernel = last_kernel if gain is not None else lambda count, *refs: last_kernel(
        count, *refs[:count], None, refs[count], None, refs[count + 1]
    )
    return call(
        functools.partial(kernel, len(terms)),
        (steps,),
        [spec(place) for _, place in terms]
        + [block] * (len(extra) + 1)
        + ([] if gain is None else [resident(gain.shape)]),
        block,
        jax.ShapeDtypeStruct((tall, model), BF16),
        [],
        6.0,
        60,
    )(*[array for array, _ in terms], *extra, base, *([] if gain is None else [gain]))


def finish_grads_kernel(one_gate, one_up, one_down, two_gate, two_up, two_down, second, both, down, out):
    cut = one_gate.shape[0]
    both[:cut, 0, :] = one_gate[...].astype(F32)
    both[:cut, 1, :] = one_up[...].astype(F32)
    both[cut:, 0, :] = two_gate[...].astype(F32)
    both[cut:, 1, :] = two_up[...].astype(F32)
    down[:cut, :] = one_down[...].astype(F32)
    down[cut:, :] = two_down[...].astype(F32)
    out[...] = second[...].astype(F32)


def finish_grads(one, two, mix, model):
    rows = one.shape[0] + two.shape[0]
    own = mix.shape[0]
    tile = column_tile(model)
    steps = model // tile

    def spec(tall, place):
        return pl.BlockSpec((tall, tile), lambda step: (0, place * steps + step))

    return call(
        finish_grads_kernel,
        (steps,),
        [spec(part.shape[0], place) for part in (one, two) for place in range(3)] + [spec(own, 1)],
        [pl.BlockSpec((rows, 2, tile), lambda step: (0, 0, step)), spec(rows, 0), spec(own, 0)],
        [
            jax.ShapeDtypeStruct((rows, 2, model), F32),
            jax.ShapeDtypeStruct((rows, model), F32),
            jax.ShapeDtypeStruct((own, model), F32),
        ],
        [],
        5.0,
        16,
    )(one, one, one, two, two, two, mix)


def part_grads_kernel(block, first, second, tail, both, gate_w, rows):
    both[:, 0, :] = first[...].astype(F32)
    both[:, 1, :] = second[...].astype(F32)

    @pl.when(pl.program_id(0) == 0)
    def _():
        held = tail[...]
        gate_w[:, 0, :] = held[:, :block].astype(F32)
        gate_w[:, 1, :] = held[:, block : 2 * block].astype(F32)
        count = held.shape[0]
        row = lax.broadcasted_iota(jnp.int32, (count, count), 0)
        column = lax.broadcasted_iota(jnp.int32, (count, count), 1)
        rows[...] = dot_tn(held[:, 2 * block : 2 * block + 8], jnp.where(row == column, 1.0, 0.0).astype(BF16))


def part_grads(grads, last, model, wide, block):
    rows = grads.shape[0]
    tile = column_tile(model)
    steps = model // tile
    spec = pl.BlockSpec((rows, tile), lambda step: (0, step))
    return call(
        functools.partial(part_grads_kernel, block),
        (steps,),
        [spec, spec, pl.BlockSpec((rows, wide), lambda step: (0, model // wide))],
        [pl.BlockSpec((rows, 2, tile), lambda step: (0, 0, step)), resident((rows, 2, block)), resident((8, rows))],
        [
            jax.ShapeDtypeStruct((rows, 2, model), F32),
            jax.ShapeDtypeStruct((rows, 2, block), F32),
            jax.ShapeDtypeStruct((8, rows), F32),
        ],
        [],
        3.0,
        16,
    )(grads, last, last)


def seq_gather(shard):
    return lax.all_gather(shard, "seq", axis=0, tiled=True)


def seq_scatter(whole):
    return lax.psum_scatter(whole, "seq", scatter_dimension=0, tiled=True)


def per_device(
    tokens,
    cotangent,
    doc_ids,
    mix_in,
    mix_out,
    gate_w,
    conv_w,
    conv_bias,
    gate_bias,
    decay_param,
    gain_one,
    gain_two,
    mlp_in,
    mlp_out,
):
    run_len, model = tokens.shape[1:]
    n_seq = lax.axis_size("seq")
    n_dev = lax.axis_size("dp") * n_seq
    own = mix_out.shape[0]
    block = gate_w.shape[2]
    chan = own * n_seq
    width = -(-chan // 128) * 128
    blocks = chan // block

    x_low = tokens.reshape(run_len, model)
    x_pieces, _ = gather_rows(x_low)
    x_zero = x_low.astype(F32)
    cot_low = cotangent.reshape(run_len, model)
    lead = hand_on(x_low[run_len - HALO :], 1)
    part = gain_one.shape[0]
    gains = jnp.concatenate([gain_one, gain_two]).astype(BF16)[None]
    my_run = lax.axis_index("seq")
    first_token = my_run * run_len
    places = lax.broadcasted_iota(jnp.int32, (n_seq, 1), 0)
    gain_rows = jnp.where(places == my_run, gains, jnp.zeros((), BF16))
    for hop in range(1, n_seq):
        ring = [(source, (source + hop) % n_seq) for source in range(n_seq)]
        arrived = lax.ppermute(gains, "seq", ring)
        gain_rows = jnp.where(places == (my_run - hop) % n_seq, arrived, gain_rows)
    gain_rows = jnp.pad(gain_rows.reshape(1, -1), ((0, 0), (0, model - 2 * part * n_seq)))
    padded = jnp.concatenate([jnp.full((3,), -1, jnp.int32), doc_ids.reshape(-1)])
    own_docs = lax.dynamic_slice_in_dim(padded, first_token + 3, run_len)
    same = sum(
        jnp.where(lax.dynamic_slice_in_dim(padded, first_token + 3 - back, run_len) == own_docs, 1.0, 0.0)
        for back in (1, 2, 3)
    )
    info = jnp.pad(same, (0, model - run_len)).astype(BF16)[None]
    tops, _ = gather_rows(jnp.concatenate([info, gain_rows, lead[2:]], 0))
    count = len(tops)
    half = count // 2

    small = jnp.concatenate(
        [
            gate_w.reshape(own, 2 * block),
            conv_w.T,
            conv_bias[:, None],
            gate_bias.T,
            decay_param[:, None],
        ],
        1,
    )
    extra = -(-small.shape[1] // 128) * 128
    small = jnp.pad(small, ((0, 0), (0, extra - small.shape[1])))
    w_in = jnp.concatenate([mix_in[:, 1, :], mix_in[:, 0, :], mix_out, small], 1).astype(BF16)
    w_in = seq_gather(w_in)
    mlp_in, mlp_out = after((mlp_in, mlp_out), lead)
    shard = jnp.concatenate([mlp_in.astype(BF16).reshape(-1, 2 * model), mlp_out.astype(BF16)], 1)
    cut = 2 * shard.shape[0] // 3
    shards = [shard[:cut], shard[cut:]]
    w_one, w_two = [seq_gather(rows) for rows in shards]

    orders = jnp.asarray(piece_order(count), jnp.int32)
    order = lax.dynamic_index_in_dim(after(orders, lead), lax.axis_index("dp"), 0, False)
    places = lax.broadcasted_iota(jnp.int32, (count, 1), 0)
    gain_rows = jnp.zeros((count, 2 * part * n_seq), F32)
    for index, piece in enumerate(tops):
        row = piece[1:2, : 2 * part * n_seq].astype(F32)
        gain_rows = jnp.where(places == order[index], row, gain_rows)
    gain_rows = gain_rows.reshape(n_dev, 2 * part)
    g_one = gain_rows[:, :part].reshape(1, model)
    g_two = gain_rows[:, part:].reshape(1, model)

    h_all, h_one, same = first_norm(after(x_pieces, shards), tops, g_one, width)
    c_pieces, (same, entered) = gather_rows(
        after(cot_low, x_pieces[half - 1]),
        [
            ((1, 2), lambda sent, done: same),
            ((3,), lambda sent, done: mixer_enter(h_all, done[0], w_in, extra, block)),
        ],
    )
    (u_ext, y_pre, conv, recur, enter, keep, cum, local, ends, w_z, par) = entered
    earlier = [hand_on(ends, steps) for steps in range(1, n_seq)]

    def leaving(blocks_at, pieces, before):
        return mixer_leave(earlier, cum, local, after(y_pre, *before), w_in, model, blocks_at, pieces)

    kept = []
    x_one = x_zero + scatter_rows(leaving, count, None)
    n_two, norm_two_back = jax.vjp(rms_norm, x_one, g_two)
    h_two = n_two.astype(BF16)

    h_pieces, (c_all,) = gather_rows(h_two, [((1, 2), lambda sent, done: assemble(after(c_pieces, sent)))])
    hid_one, gate_one, up_one, h_all = mlp_part(h_pieces, c_all, w_one)
    grad_one = mlp_grads(gate_one, up_one, hid_one, h_all, c_all)
    hid_two, gate_two, up_two = mlp_part(after(h_all, grad_one), c_all, w_two)
    grad_one = seq_scatter(grad_one)

    def d_entering(blocks_at, pieces, before):
        lefts = [after(gate_one, *before), up_one, gate_two, up_two]
        rights = [(w_one, 0, model), (w_one, 1, model), (w_two, 0, model), (w_two, 1, model)]
        return rows_times(lefts, rights, blocks_at, pieces)

    def second_grads(sent, done):
        return mlp_grads(after(gate_two, sent), up_two, hid_two, h_all, c_all), grad_one

    def mlp_leaving(blocks_at, pieces, before):
        return rows_times([after(hid_one, *before), hid_two], [(w_one, 2, model), (w_two, 2, model)], blocks_at, pieces)

    def mlp_out_rows(sent):
        return mlp_leaving([1, 0], half, (sent,))

    d_h_two = scatter_rows(d_entering, count, beside(mlp_out_rows, kept))
    d_x_norm, d_gain_two = norm_two_back(d_h_two)
    d_x_one = cot_low.astype(F32) + d_x_norm
    d_mix = d_x_one.astype(BF16)

    stages, twin = plane_stages(lax.axis_size("dp"))

    def mlp_out_sums(sent, done):
        theirs, mine = after(kept.pop(), sent)
        there = lax.ppermute(theirs, "dp", twin)
        return mine, there, add_rows([[(mine, k), (there, k)] for k in range(half // 2, half)])

    d_pieces, done = gather_rows(d_mix, [((1, 2), second_grads), ((3,), mlp_out_sums)])
    (grad_two, grad_one), (mine, there, far) = done
    grad_two = seq_scatter(after(grad_two, grad_one))
    d_y, mixed, cum_back, local_back, ends_back, d_all = head_back(
        after(d_pieces, far), earlier, cum, local, y_pre, keep, w_in
    )
    got = [lax.ppermute(part, "dp", stages[-1]) for part in far]
    mixed, got = lax.optimization_barrier((mixed, got))
    later = [hand_on(ends_back, -steps) for steps in range(1, n_seq)]
    wide = next(t for t in (128, 256, 512, 1024) if t >= 2 * block + 8 and model % t == 0)
    terms = [[(mine, k), (there, k), (got[k][None], 0)] for k in range(half // 2)]
    layer_sums = add_rows(terms[half // 4 :])
    grad_mix = weight_grad(after(d_y, ends_back, layer_sums), h_one, chan, 2 * model)
    grad_mix = weight_grad(mixed, d_all, chan, into=grad_mix, place=1)
    later, grad_mix, grad_two = lax.optimization_barrier((later, grad_mix, grad_two))
    grad_mix = seq_scatter(grad_mix)
    layer_got = [lax.ppermute(part, "dp", stages[-2]) for part in layer_sums]
    tailed = tail_back(
        earlier,
        later,
        cum_back,
        local_back,
        cum,
        local,
        recur,
        enter,
        keep,
        conv,
        u_ext,
        same,
        w_z,
        par,
        block,
        jax.ShapeDtypeStruct((chan, model + wide), BF16),
        wide,
    )
    (d_u, edges, grad_u), layer_got = lax.optimization_barrier((tailed, layer_got))
    terms = [[*those, (one[None], 0)] for those, one in zip(terms, layer_got)]
    from_next = hand_on(edges[:, :8], -1)
    layer_terms = scatter_tail(terms, stages[:-2], [])
    arrays = after([array for array, _ in layer_terms], edges)
    layer_out = last_rows([(v, at) for v, (_, at) in zip(arrays, layer_terms)], x_one)
    from_next, layer_out = lax.optimization_barrier((from_next, layer_out))
    layer_out = layer_out.reshape(1, run_len, model)
    d_u = lax.dynamic_update_slice(d_u, (edges[:, 8:] + from_next).astype(BF16), (0, run_len - 8, 0))
    gain_terms = []

    def d_leaving(blocks_at, pieces, before):
        *part_rows, gain_term = rows_times(
            [after(d_y, *before), d_u], [(w_in, 1, model), (w_in, 0, model)], blocks_at, pieces, h_one
        )
        gain_terms.append(gain_term.sum(0))
        return part_rows

    def u_grad(sent):
        return weight_grad(after(d_u, sent), h_one, chan, into=grad_u, place=0)

    def finished(sent):
        return finish_grads(after(grad_one, sent), grad_two, grad_mix, model)

    ready = []
    d_h_one, grad_u = scatter_terms(d_leaving, count, beside(finished, ready), u_grad)
    grad_mlp_in, grad_mlp_out, grad_out = ready.pop()
    grad_u = seq_scatter(after(grad_u, grad_mix))
    input_grad = last_rows(d_h_one, d_x_one, x_low, g_one)
    d_gain_one = sum(gain_terms) / g_one
    d_gains = jnp.concatenate([d_gain_one.reshape(n_dev, part), d_gain_two.reshape(n_dev, part)], 1)
    d_gains = lax.all_to_all(after(d_gains, d_h_one[-1][0]), ("dp", "seq"), 0, 0, tiled=True)
    grad_mix_in, grad_gate_w, rows = part_grads(after(grad_mix, grad_out), grad_u, model, wide, block)
    d_gains = after(d_gains, grad_mix_in).sum(0)
    return (
        layer_out,
        input_grad.reshape(1, run_len, model),
        grad_mix_in,
        grad_out,
        grad_gate_w,
        rows[:4],
        rows[4],
        rows[5:7],
        rows[7],
        d_gains[:part],
        d_gains[part:],
        grad_mlp_in,
        grad_mlp_out,
    )


def solution(mesh):
    rows = P(("dp", "seq"))
    placed = (
        P("dp", "seq", None),
        P("dp", "seq", None),
        P("dp", None),
        P(("dp", "seq"), None, None),
        P(("dp", "seq"), None),
        P(("dp", "seq"), None, None),
        P(None, ("dp", "seq")),
        rows,
        P(None, ("dp", "seq")),
        rows,
        rows,
        rows,
        P(("dp", "seq"), None, None),
        P(("dp", "seq"), None),
    )
    return jax.shard_map(
        per_device,
        mesh=mesh,
        in_specs=placed,
        out_specs=placed[:2] + placed[3:],
        check_vma=False,
    )
```

```python
import functools

import jax
import jax.numpy as jnp
from jax import lax
from jax.experimental import pallas as pl
from jax.experimental.pallas import tpu as pltpu
from jax.sharding import PartitionSpec as P

EPS = 1e-06
FLOOR = 0.0001
SHARP = 8.0
HALO = 16
F32 = jnp.float32
BF16 = jnp.bfloat16
MEBI = 1024 * 1024
ANY = pl.BlockSpec(memory_space=pl.ANY)
ROOT = 0.7978845608028654
CUBE = 0.044715
SLOW = 4.5
RATE = 650e6
SWEEP = 25e-6


def dot_nt(left, right):
    return lax.dot_general(left, right, (((1,), (1,)), ((), ())), preferred_element_type=F32)


def dot_nn(left, right):
    return lax.dot_general(left, right, (((1,), (0,)), ((), ())), preferred_element_type=F32)


def dot_tn(left, right):
    return lax.dot_general(left, right, (((0,), (0,)), ((), ())), preferred_element_type=F32)


def rms_norm(values, gain_vec):
    return values * lax.rsqrt(jnp.mean(values * values, axis=-1, keepdims=True) + EPS) * gain_vec


def gelu_parts(values):
    squared = values * values
    bend = jnp.tanh(ROOT * (values + CUBE * values * squared))
    half = 0.5 * (1.0 + bend)
    slope = half + 0.5 * values * (1.0 - bend * bend) * (ROOT * (1.0 + 3.0 * CUBE * squared))
    return values * half, slope


def gelu_value(values):
    bend = jnp.tanh(ROOT * (values + CUBE * values * values * values))
    return values * (0.5 * (1.0 + bend))


def plane_stages(count):
    bits = count.bit_length() - 1
    upper = list(range(1, bits))
    stages = []
    for place in range(len(upper)):
        pairs = []
        for source in range(count):
            shift = place if source % 2 == 0 else (place + 1) % len(upper)
            pairs.append((source, source ^ (1 << upper[shift])))
        stages.append(pairs)
    twin = [(source, source ^ 1) for source in range(count)]
    return stages, twin


def gather_rows(piece, beside=()):
    stages, twin = plane_stages(lax.axis_size("dp"))
    held = [piece] + [None] * (2 ** len(stages) - 1)
    done = []
    before = ()

    def arrival(m):
        top = m.bit_length() - 1
        return lax.ppermute(held[m ^ (1 << top)], "dp", stages[top])

    for members, work in beside:
        arrived = [arrival(m) for m in members]
        sent = [held[m ^ (1 << (m.bit_length() - 1))] for m in members]
        arrived, made = lax.optimization_barrier((arrived, work((sent, before), done)))
        before = arrived
        done.append(made)
        for m, part in zip(members, arrived):
            held[m] = part
    for m in range(1, len(held)):
        if held[m] is None:
            held[m] = arrival(m)
    return held + [lax.ppermute(part, "dp", twin) for part in held], done


def after(value, *others):
    return lax.optimization_barrier((value, others))[0]


def total_of(terms):
    return sum(array[place].astype(F32) for array, place in terms)


def scatter_tail(terms, stages, waits, late=()):
    for place, pairs in enumerate(reversed(stages)):
        split = len(terms) // 2
        sent = add_rows(terms[split:], 60)
        if late:
            sent, late = lax.optimization_barrier((sent, late))
            terms = [[*those, (one[None], 0)] for those, one in zip(terms, late)] + terms[split:]
            late = ()
        got = [lax.ppermute(part, "dp", pairs) for part in sent]
        if place < len(waits):
            got = waits[place](sent, got)
        terms = [[*those, (one[None], 0)] for those, one in zip(terms, got)]
    return terms[0]


def scatter_terms(make, count, wait, ahead=None):
    stages, twin = plane_stages(lax.axis_size("dp"))
    quarter = count // 4
    theirs = make([3], quarter, ())[0]
    there = lax.ppermute(theirs, "dp", twin)
    far = make([1], quarter, (theirs,))[0]
    sent = add_rows([[(far, k), (there, k)] for k in range(quarter)])
    got = [lax.ppermute(part, "dp", stages[-1]) for part in sent]
    split = quarter // 2
    theirs, near = make([2, 0], quarter, (sent,))
    extra = () if ahead is None else ahead(theirs)
    theirs, near, got[split:], extra = lax.optimization_barrier((theirs, near, got[split:], extra))
    there = lax.ppermute(theirs, "dp", twin)
    terms = [[(near, k), (there, k)] for k in range(quarter)]
    terms = terms[:split] + [[*terms[k], (got[k][None], 0)] for k in range(split, quarter)]
    late = got[:split]
    return scatter_tail(terms, stages[:-1], [wait] if wait else [], late), extra


def scatter_rows(make, count, wait):
    return total_of(scatter_terms(make, count, wait)[0])


def beside(work, done):
    def wait(sent, got):
        got, made = lax.optimization_barrier((got, work(sent)))
        done.append(made)
        return got

    return wait


def piece_order(count):
    stages, twin = plane_stages(count)
    orders = []
    for device in range(count):
        held, other = [device], [twin[device][1]]
        for pairs in stages:
            held = held + [pairs[place][1] for place in held]
            other = other + [pairs[place][1] for place in other]
        orders.append(held + other)
    return orders


def hand_on(value, steps):
    count = lax.axis_size("seq")
    first, last = (max(0, -steps), min(count, count - steps))
    return lax.ppermute(value, "seq", [(source, source + steps) for source in range(first, last)])


def scan_into(keep, entry, cum_ref, state_ref, backward):
    rows, width = keep.shape
    groups = rows // 8
    mult = keep.reshape(groups, 8, width)
    total = entry.reshape(groups, 8, width)
    place = lax.broadcasted_iota(jnp.int32, (groups, 8, width), 1)
    for hop in (1, 2, 4):
        if backward:
            shift, valid = 8 - hop, place < 8 - hop
        else:
            shift, valid = hop, place >= hop
        near_mult = pltpu.roll(mult, shift, 1)
        near_total = pltpu.roll(total, shift, 1)
        total = jnp.where(valid, total + mult * near_total, total)
        mult = jnp.where(valid, mult * near_mult, mult)
    carry_total = jnp.zeros((1, width), F32)
    carry_mult = jnp.ones((1, width), F32)
    edge = 0 if backward else 7
    order = range(groups - 1, -1, -1) if backward else range(groups)
    for group in order:
        now_total = total[group] + mult[group] * carry_total
        now_mult = mult[group] * carry_mult
        state_ref[0, group * 8 : group * 8 + 8, :] = now_total
        cum_ref[0, group * 8 : group * 8 + 8, :] = now_mult
        carry_total = now_total[edge : edge + 1]
        carry_mult = now_mult[edge : edge + 1]
    return carry_mult, carry_total


def folded(refs, piece):
    at = pl.ds(piece, 1)
    carry = refs[-1][1, at, :]
    for ref in refs[-2::-1]:
        carry = ref[1, at, :] + ref[0, at, :] * carry
    return carry


def put_ends(ref, piece, mult, total):
    ref[0, pl.ds(piece, 1), :] = mult
    ref[1, pl.ds(piece, 1), :] = total


def fetch_all(refs, buf, sems):
    for index, ref in enumerate(refs):
        pltpu.make_async_copy(ref, buf.at[index], sems.at[index]).start()


def fetched(refs, buf, sems, index):
    pltpu.make_async_copy(refs[0], buf.at[index], sems.at[index]).wait()


def put(buf, whole, sems, index):
    return pltpu.make_async_copy(buf.at[index], whole.at[index], sems.at[index])


def padded_rows(rows, width):
    missing = width - rows.shape[0]
    return jnp.concatenate([rows, jnp.zeros((missing, rows.shape[1]), rows.dtype)], 0) if missing else rows


def first_norm_kernel(count, *refs):
    x_refs, top_refs = refs[:count], refs[count : 2 * count]
    gain, all_out, h_out, m_out, buf, top, sems, top_sems = refs[2 * count :]
    step = pl.program_id(0)

    @pl.when(step == 0)
    def _():
        fetch_all(top_refs, top, top_sems)
        fetch_all(x_refs, buf, sems)

    fetched(top_refs, top, top_sems, step)
    fetched(x_refs, buf, sems, step)
    rows, width = m_out.shape[1:]
    top_val = top[step].astype(F32)
    info = jnp.broadcast_to(top_val[0:1, :rows], (width, rows)).astype(BF16)
    across = lax.broadcasted_iota(jnp.int32, (rows, rows), 0)
    down = lax.broadcasted_iota(jnp.int32, (rows, rows), 1)
    m_out[0] = dot_nt(jnp.where(across == down, 1.0, 0.0).astype(BF16), info).astype(BF16)
    all_out[0, :HALO] = rms_norm(top_val, gain[...]).astype(BF16)
    h_low = rms_norm(buf[step].astype(F32), gain[...]).astype(BF16)
    all_out[0, HALO:] = h_low
    h_out[0] = h_low


def first_norm(pieces, tops, gain, width):
    count = len(pieces)
    rows, model = pieces[0].shape
    shapes = [
        jax.ShapeDtypeStruct((count, rows + HALO, model), BF16),
        jax.ShapeDtypeStruct((count, rows, model), BF16),
        jax.ShapeDtypeStruct((count, rows, width), BF16),
    ]
    return call(
        functools.partial(first_norm_kernel, count),
        (count,),
        [ANY] * (2 * count) + [resident(gain.shape)],
        [per_piece(s.shape[1:]) for s in shapes],
        shapes,
        [
            pltpu.VMEM((count, rows, model), BF16),
            pltpu.VMEM((count, HALO, model), BF16),
            pltpu.SemaphoreType.DMA((count,)),
            pltpu.SemaphoreType.DMA((count,)),
        ],
        2.6e-6 * count * rows * model,
        60,
    )(*pieces, *tops, gain)


def block_masks(width, block):
    row = lax.broadcasted_iota(jnp.int32, (width, width), 0)
    column = lax.broadcasted_iota(jnp.int32, (width, width), 1)
    inside = None
    for start in range(0, width, block):
        here = (row >= start) & (row < start + block) & (column >= start) & (column < start + block)
        inside = here if inside is None else inside | here
    row = lax.broadcasted_iota(jnp.int32, (width, block), 0)
    column = lax.broadcasted_iota(jnp.int32, (width, block), 1)
    fold = None
    for start in range(0, width, block):
        here = row - start == column
        fold = here if fold is None else fold | here
    return inside, jnp.where(fold, 1.0, 0.0).astype(BF16)


def sigmoid(values):
    return 0.5 * jnp.tanh(0.5 * values) + 0.5


def softplus(values):
    small = jnp.exp(-jnp.abs(values))
    grown = 1.0 + small
    exact = jnp.where(grown == 1.0, small, jnp.log(grown) * small / jnp.where(grown == 1.0, 1.0, grown - 1.0))
    return jnp.maximum(values, 0.0) + exact


def mixer_enter_kernel(
    block,
    h_ref,
    m_ref,
    wu,
    wy,
    small,
    raw,
    u_out,
    y_out,
    conv_out,
    r_out,
    e_out,
    k_out,
    a_out,
    s_out,
    ends,
    wz,
    par,
    w_all,
    both,
):
    width = wz.shape[1]
    some, tall, model = h_ref.shape
    rows = tall - HALO
    place = pl.program_id(0) % some

    @pl.when(pl.program_id(0) == 0)
    def _():
        w_all[:width, :] = padded_rows(wu[...], width)
        w_all[width:, :] = padded_rows(wy[...], width)
        params = padded_rows(small[...], width)
        inside, fold = block_masks(width, block)
        for gate in (0, 1):
            spread = dot_nt(params[:, gate * block : gate * block + block], fold)
            wz[gate * width : gate * width + width, :] = jnp.where(inside, spread, 0.0).astype(BF16)
        turned = raw[...]
        par[0:8, :] = turned
        par[8:16, :] = turned
        par[7:8, :] = -SHARP * softplus(turned[7:8, :])

    @pl.when(place == 0)
    def _():
        both[...] = dot_nt(h_ref[...].reshape(some * tall, model), w_all[...]).reshape(both.shape)

    u_low = both[place, :, :width].astype(BF16)
    u_out[0] = u_low
    y_out[0] = both[place, HALO:, width:]
    same = m_ref[0].astype(F32)
    u_val = u_low.astype(F32)
    conv = par[4:5, :] + par[0:1, :] * u_val[HALO:]
    for back in (1, 2, 3):
        term = par[back : back + 1, :] * u_val[HALO - back : HALO - back + rows]
        conv = conv + jnp.where(same >= back, term, 0.0)
    conv_low = conv.astype(BF16)
    conv_out[0] = conv_low
    conv = conv_low.astype(F32)
    pre = dot_nt(conv_low, wz[...])
    recur = sigmoid(pre[:, :width] + par[5:6, :])
    enter = sigmoid(pre[:, width:] + par[6:7, :])
    keep = jnp.where(same >= 1.0, jnp.exp(par[7:8, :] * recur), 0.0)
    r_out[0] = recur
    e_out[0] = enter
    k_out[0] = keep
    spare = jnp.maximum(1.0 - keep * keep, FLOOR)
    inputs = conv * enter * (spare * lax.rsqrt(spare))
    mult, total = scan_into(keep, inputs, a_out, s_out, False)
    put_ends(ends, pl.program_id(0), mult, total)


def resident(shape):
    zeros = (0,) * len(shape)
    return pl.BlockSpec(shape, lambda step: zeros)


def per_piece(shape, first=0):
    rest = (0,) * len(shape)
    return pl.BlockSpec((1,) + shape, lambda step: (step + first,) + rest)


def grown(memory, count, usual=8):
    return min(60, memory * max(count, usual) // usual)


def settings(micros, axes, memory):
    return dict(
        compiler_params=pltpu.CompilerParams(
            vmem_limit_bytes=memory * MEBI, dimension_semantics=("arbitrary",) * axes if axes else None
        ),
        cost_estimate=pl.CostEstimate(flops=int(micros / SLOW * 1.15e9), bytes_accessed=1024, transcendentals=0),
    )


def call(kernel, grid, in_specs, out_specs, out_shape, scratch, micros, memory, aliases={}):
    return pl.pallas_call(
        kernel,
        grid=grid,
        in_specs=in_specs,
        out_specs=out_specs,
        out_shape=out_shape,
        scratch_shapes=scratch,
        input_output_aliases=aliases,
        **settings(micros, len(grid), memory),
    )


def stream(kernel, grid, in_specs, out_specs, out_shape, micros):
    def outer(*refs):
        pltpu.emit_pipeline(kernel, grid=grid, in_specs=in_specs, out_specs=[out_specs])(*refs)

    here = pl.BlockSpec(memory_space=pltpu.HBM)
    return pl.pallas_call(
        outer,
        in_specs=[here] * len(in_specs),
        out_specs=here,
        out_shape=out_shape,
        **settings(micros, 0, 16),
    )


def mixer_enter(h_all, same, w_in, raw, extra, block):
    count, tall, model = h_all.shape
    rows = tall - HALO
    chan = w_in.shape[0]
    width = same.shape[2]
    some = 1

    def out(height, columns, dtype):
        return jax.ShapeDtypeStruct((count, height, columns), dtype)

    shapes = [out(tall, width, BF16), out(rows, width, F32), out(rows, width, BF16)]
    shapes += [out(rows, width, F32)] * 5
    fixed = [jax.ShapeDtypeStruct((2, count, width), F32)]
    fixed += [jax.ShapeDtypeStruct((2 * width, width), BF16), jax.ShapeDtypeStruct((16, width), F32)]
    return call(
        functools.partial(mixer_enter_kernel, block),
        (count,),
        [
            pl.BlockSpec((some, tall, model), lambda step: (step // some, 0, 0)),
            per_piece((rows, width)),
            pl.BlockSpec((chan, model), lambda step: (0, 0)),
            pl.BlockSpec((chan, model), lambda step: (0, 1)),
            pl.BlockSpec((chan, extra), lambda step: (0, 3 * model // extra)),
            resident(raw.shape),
        ],
        [per_piece(s.shape[1:]) for s in shapes] + [resident(s.shape) for s in fixed],
        shapes + fixed,
        [pltpu.VMEM((2 * width, model), BF16), pltpu.VMEM((some, tall, 2 * width), F32)],
        SWEEP * count * rows * width,
        grown(26, count),
    )(h_all, same, w_in, w_in, w_in, raw)


def column_tile(model):
    return next(t for t in (512, 256, 128) if model % t == 0)


def group_of(shape, blocks, pieces):
    first, stride = blocks[0], (blocks[-1] - blocks[0]) // max(1, len(blocks) - 1)
    rest = (0,) * len(shape)
    return pl.BlockSpec((pieces,) + shape, lambda group, step: (first + stride * group,) + rest)


def group_outs(rows, tile, steps, blocks, pieces):
    def spec(place):
        def index(group, step):
            at = jnp.clip((group - place) * steps + step, 0, steps - 1)
            return (0, 0, at)

        return pl.BlockSpec((pieces, rows, tile), index)

    return [spec(place) for place in range(len(blocks))]


def put_group(outs, total):
    for place, out in enumerate(outs):

        @pl.when(pl.program_id(0) == place)
        def _(out=out):
            out[...] = total.reshape(out.shape)


def mixer_leave_kernel(hops, pieces, blocks, *refs):
    groups = len(blocks)
    first, stride = blocks[0], (blocks[-1] - blocks[0]) // max(1, groups - 1)
    ends = refs[:hops]
    cum, local, y_pre, w_out = refs[hops : hops + 4]
    mixed = refs[-1]
    rows = cum.shape[1]

    @pl.when(pl.program_id(1) == 0)
    def _():
        for index in range(pieces):
            piece = (first + stride * pl.program_id(0)) * pieces + index
            states = local[index] + cum[index] * folded(ends, piece)
            mixed[index * rows : index * rows + rows, :] = (gelu_value(y_pre[index]) * states).astype(BF16)

    right = padded_rows(w_out[...], mixed.shape[1])
    put_group(refs[hops + 4 : hops + 4 + groups], dot_nn(mixed[...], right).astype(BF16))


def mixer_leave(ends, cum, local, y_pre, w_in, model, blocks, pieces):
    rows, width = cum.shape[1:]
    tile = column_tile(model)
    steps = model // tile
    groups = len(blocks)
    return call(
        functools.partial(mixer_leave_kernel, len(ends), pieces, blocks),
        (groups, steps),
        [pl.BlockSpec(ends[0].shape, lambda group, step: (0, 0, 0))] * len(ends)
        + [group_of((rows, width), blocks, pieces)] * 3
        + [pl.BlockSpec((w_in.shape[0], tile), lambda group, step: (0, 2 * steps + step))],
        group_outs(rows, tile, steps, blocks, pieces),
        [jax.ShapeDtypeStruct((pieces, rows, model), BF16)] * groups,
        [pltpu.VMEM((pieces * rows, width), BF16)],
        3.5 + 3.5 * groups * pieces / 2,
        grown(20, pieces, 2),
    )(*ends, cum, local, y_pre, w_in)


def head_back_kernel(count, hops, *refs):
    d_refs = refs[:count]
    ends = refs[count : count + hops]
    (cum, local, y_pre, keep_ref, w_out, dy_out, mixed_out, cb_out, lb_out, ends_out, all_out, buf, w_all, d_some, sems, all_sems) = refs[count + hops :]
    some = 1
    step = pl.program_id(0)

    @pl.when(step == 0)
    def _():
        fetch_all(d_refs, buf, sems)
        w_all[...] = padded_rows(w_out[...], w_all.shape[0])

    @pl.when(step % some == 0)
    def _():
        for place in range(some):
            fetched(d_refs, buf, sems, step + place)
            put(buf, all_out, all_sems, step + place).start()
        rows, model = buf.shape[1:]
        d_some[...] = dot_nt(buf[pl.ds(step, some)].reshape(some * rows, model), w_all[...]).reshape(d_some.shape)

    d_mixed = d_some[step % some]
    states = local[0] + cum[0] * folded(ends, step)
    value, slope = gelu_parts(y_pre[0])
    mixed_out[0] = (value * states).astype(BF16)
    dy_out[0] = (slope * d_mixed * states).astype(BF16)
    keep = keep_ref[0]
    width = keep.shape[1]
    next_keep = jnp.concatenate([keep[1:], jnp.ones((1, width), F32)], 0)
    mult, total = scan_into(next_keep, d_mixed * value, cb_out, lb_out, True)
    put_ends(ends_out, step, mult * keep[0:1], total * keep[0:1])

    @pl.when(step == count - 1)
    def _():
        for index in range(count):
            put(buf, all_out, all_sems, index).wait()


def head_back(pieces, ends, cum, local, y_pre, keep, w_in):
    count = len(pieces)
    rows, model = pieces[0].shape
    width = cum.shape[2]

    def out(height, dtype):
        return jax.ShapeDtypeStruct((count, height, width), dtype)

    shapes = [out(rows, BF16), out(rows, BF16), out(rows, F32), out(rows, F32)]
    ends_shape = jax.ShapeDtypeStruct((2, count, width), F32)
    return call(
        functools.partial(head_back_kernel, count, len(ends)),
        (count,),
        [ANY] * count
        + [resident(ends[0].shape)] * len(ends)
        + [per_piece((rows, width))] * 4
        + [pl.BlockSpec((w_in.shape[0], model), lambda step: (0, 2))],
        [per_piece(s.shape[1:]) for s in shapes] + [resident(ends_shape.shape), ANY],
        shapes + [ends_shape, jax.ShapeDtypeStruct((count, rows, model), BF16)],
        [
            pltpu.VMEM((count, rows, model), BF16),
            pltpu.VMEM((width, model), BF16),
            pltpu.VMEM((1, rows, width), F32),
            pltpu.SemaphoreType.DMA((count,)),
            pltpu.SemaphoreType.DMA((count,)),
        ],
        SWEEP * count * rows * width,
        grown(25, count),
    )(*pieces, *ends, cum, local, y_pre, keep, w_in)


def tail_back_kernel(hops, block, *refs):
    ends = refs[:hops]
    later = refs[hops : 2 * hops]
    (cb, lb, cum, local, r_ref, e_ref, k_ref, conv_ref, u_ref, m_ref, wz, par, du_out, edge_out, tail_out, small_out, gw_out) = refs[2 * hops :]
    step = pl.program_id(0)

    @pl.when(step == 0)
    def _():
        gw_out[...] = jnp.zeros_like(gw_out)
        small_out[...] = jnp.zeros_like(small_out)

    state_in = folded(ends, step)
    d_states = lb[0] + cb[0] * folded(later, step)
    states = local[0] + cum[0] * state_in
    prev = jnp.concatenate([state_in, states[:-1]], 0)
    recur, enter, keep = r_ref[0], e_ref[0], k_ref[0]
    conv_low = conv_ref[0]
    conv = conv_low.astype(F32)
    rows, width = conv.shape
    spare = 1.0 - keep * keep
    floored = jnp.maximum(spare, FLOOR)
    root = lax.rsqrt(floored)
    scaling = floored * root
    weight = jnp.where(spare > FLOOR, 0.5, jnp.where(spare == FLOOR, 0.25, 0.0)) * root
    d_enter_sum = d_states * conv
    d_spare = d_enter_sum * enter * weight
    d_expo = (d_states * prev - 2.0 * keep * d_spare) * keep
    d_recur = d_expo * par[7:8, :] * recur * (1.0 - recur)
    d_enter = d_enter_sum * scaling * enter * (1.0 - enter)
    d_pre = jnp.concatenate([d_recur.astype(BF16), d_enter.astype(BF16)], 1)
    d_conv = d_states * enter * scaling + dot_nn(d_pre, wz[...])
    gw_out[...] += dot_tn(d_pre, conv_low)
    d_pre_val = d_pre.astype(F32)
    same = m_ref[0].astype(F32)
    u_val = u_ref[0].astype(F32)
    sums = []
    d_u = jnp.zeros((rows, width), F32)
    head = jnp.zeros((8, width), F32)
    for back in range(4):
        masked = d_conv if back == 0 else jnp.where(same >= back, d_conv, 0.0)
        sums.append(jnp.sum(masked * u_val[HALO - back : HALO - back + rows], axis=0, keepdims=True))
        moved = masked * par[back : back + 1, :]
        if back == 0:
            d_u = d_u + moved
        else:
            nothing = jnp.zeros((back, width), F32)
            d_u = d_u + jnp.concatenate([moved[back:], nothing], 0)
            head = head + jnp.concatenate([jnp.zeros((8 - back, width), F32), moved[:back]], 0)
    sums.append(jnp.sum(d_conv, axis=0, keepdims=True))
    sums.append(jnp.sum(d_pre_val[:, :width], axis=0, keepdims=True))
    sums.append(jnp.sum(d_pre_val[:, width:], axis=0, keepdims=True))
    sums.append(jnp.sum(d_expo * recur, axis=0, keepdims=True))
    small_out[...] += jnp.concatenate(sums, 0)
    du_out[0] = d_u.astype(BF16)
    edge_out[0, 0:8, :] = head
    edge_out[0, 8:16, :] = d_u[rows - 8 :]

    @pl.when(step == pl.num_programs(0) - 1)
    def _():
        kept, wide = tail_out.shape
        inside, fold = block_masks(width, block)
        parts = []
        for gate in (0, 1):
            whole = jnp.where(inside, gw_out[gate * width : gate * width + width, :], 0.0).astype(BF16)
            parts.append(dot_nn(whole, fold))
        sums = small_out[...]
        slope = -SHARP * sigmoid(par[15:16, :])
        sums = jnp.concatenate([sums[:7], sums[7:8] * slope], 0).astype(BF16)
        row = lax.broadcasted_iota(jnp.int32, (width, width), 0)
        column = lax.broadcasted_iota(jnp.int32, (width, width), 1)
        parts.append(dot_nt(jnp.where(row == column, 1.0, 0.0).astype(BF16), sums))
        parts.append(jnp.zeros((width, wide - 2 * block - 8), F32))
        tail_out[...] = jnp.concatenate(parts, 1)[:kept].astype(BF16)


def tail_back(ends, later, cb, lb, cum, local, recur, enter, keep, conv, u_ext, same, wz, par, block, into, wide):
    count, rows, width = cb.shape
    shapes = [
        jax.ShapeDtypeStruct((count, rows, width), BF16),
        jax.ShapeDtypeStruct((count, 16, width), F32),
        jax.ShapeDtypeStruct(into.shape, BF16),
    ]
    last = into.shape[1] // wide - 1
    tall = u_ext.shape[1]
    return call(
        functools.partial(tail_back_kernel, len(ends), block),
        (count,),
        [resident(ends[0].shape)] * (2 * len(ends))
        + [per_piece((rows, width))] * 8
        + [per_piece((tall, width)), per_piece((rows, width)), resident(wz.shape), resident(par.shape)],
        [per_piece((rows, width)), per_piece((16, width)), pl.BlockSpec((into.shape[0], wide), lambda step: (0, last))],
        shapes,
        [pltpu.VMEM((8, width), F32), pltpu.VMEM(wz.shape, F32)],
        SWEEP * count * rows * width,
        60,
    )(*ends, *later, cb, lb, cum, local, recur, enter, keep, conv, u_ext, same, wz, par)


def rows_times_kernel(terms, gained, *refs):
    lefts, rights = refs[:terms], refs[terms : 2 * terms]
    outs = refs[2 * terms + gained :]
    total = None
    for left, right in zip(lefts, rights):
        pieces, rows, inner = left.shape
        term = dot_nn(left[...].reshape(pieces * rows, inner), padded_rows(right[...], inner))
        total = term if total is None else total + term
    if gained:
        factor = refs[2 * terms][...].reshape(total.shape).astype(F32)
        outs[-1][0] = jnp.sum(total * factor, axis=0, keepdims=True)
        outs = outs[:-1]
    put_group(outs, total.astype(BF16))


def rows_times(lefts, rights, blocks, pieces, factor=None):
    rows = lefts[0].shape[1]
    model = rights[0][2]
    tile = column_tile(model)
    steps = model // tile
    groups = len(blocks)
    inner = sum(right.shape[0] for right, _, _ in rights)
    gained = 0 if factor is None else 1

    def right_spec(right, place):
        return pl.BlockSpec((right.shape[0], tile), lambda group, step: (0, place * steps + step))

    out_specs = group_outs(rows, tile, steps, blocks, pieces)
    shapes = [jax.ShapeDtypeStruct((pieces, rows, model), BF16)] * groups
    extra_specs = []
    if gained:
        first, stride = blocks[0], (blocks[-1] - blocks[0]) // max(1, groups - 1)
        out_specs.append(pl.BlockSpec((1, 1, tile), lambda group, step: (group, 0, step)))
        shapes.append(jax.ShapeDtypeStruct((groups, 1, model), F32))
        extra_specs.append(
            pl.BlockSpec((pieces, rows, tile), lambda group, step: (first + stride * group, 0, step))
        )
    return call(
        functools.partial(rows_times_kernel, len(lefts), gained),
        (groups, steps),
        [group_of(left.shape[1:], blocks, pieces) for left in lefts]
        + [right_spec(right, place) for right, place, _ in rights]
        + extra_specs,
        out_specs,
        shapes,
        [],
        3 + 2 * groups * pieces * rows * inner * model / RATE,
        grown(20, pieces, 4),
    )(*lefts, *[right for right, _, _ in rights], *([factor] if gained else []))


def assemble_kernel(count, *refs):
    parts, whole, buf, sems, all_sems = refs[:count], refs[count], *refs[count + 1 :]
    fetch_all(parts, buf, sems)
    for index in range(count):
        fetched(parts, buf, sems, index)
        put(buf, whole, all_sems, index).start()
    for index in range(count):
        put(buf, whole, all_sems, index).wait()


def assemble(pieces):
    count = len(pieces)
    shape = (count,) + pieces[0].shape
    return call(
        functools.partial(assemble_kernel, count),
        (1,),
        [ANY] * count,
        ANY,
        jax.ShapeDtypeStruct(shape, pieces[0].dtype),
        [pltpu.VMEM(shape, pieces[0].dtype), pltpu.SemaphoreType.DMA((count,)), pltpu.SemaphoreType.DMA((count,))],
        6.5,
        grown(16, count),
    )(*pieces)


def mlp_kernel(count, first, *refs):
    sources = count if first else 1
    h_refs = refs[:count] if first else [refs[0].at[index] for index in range(count)]
    c_ref, wg, wu, wo, hid_out, dg_out, du_out = refs[sources : sources + 7]
    rest = refs[sources + 7 :]
    all_out = rest[0] if first else None
    h_buf, c_buf, h_sems, c_sems, all_sems = rest[-5:]
    step = pl.program_id(0)
    pair = 2 if count % 2 == 0 else 1
    rows, tile = hid_out.shape[1:]
    model = h_buf.shape[2]

    @pl.when(step == 0)
    def _():
        for index in range(count):
            pltpu.make_async_copy(h_refs[index], h_buf.at[index], h_sems.at[index]).start()
            pltpu.make_async_copy(c_ref.at[index], c_buf.at[index], c_sems.at[index]).start()

    def some_pieces(index, carry):
        @pl.when(step == 0)
        def _():
            for place in range(pair):
                at = index * pair + place
                fetched(h_refs, h_buf, h_sems, at)
                pltpu.make_async_copy(c_ref.at[0], c_buf.at[at], c_sems.at[at]).wait()
                if first:
                    put(h_buf, all_out, all_sems, at).start()

        span = pl.ds(index * pair, pair)
        h_low = h_buf[span].reshape(pair * rows, model)
        gate = dot_nt(h_low, wg[...])
        up = dot_nt(h_low, wu[...])
        d_hidden = dot_nt(c_buf[span].reshape(pair * rows, model), wo[...])
        value, slope = gelu_parts(gate)
        shape = (pair, rows, tile)
        hid_out[span] = (value * up).astype(BF16).reshape(shape)
        dg_out[span] = (d_hidden * up * slope).astype(BF16).reshape(shape)
        du_out[span] = (d_hidden * value).astype(BF16).reshape(shape)
        return carry

    lax.fori_loop(0, count // pair, some_pieces, 0)

    if first:

        @pl.when(step == pl.num_programs(0) - 1)
        def _():
            for index in range(count):
                put(h_buf, all_out, all_sems, index).wait()


def hidden_tile(hidden):
    return next(t for t in (256, 128, hidden) if hidden % t == 0)


def mlp_part(h_rows, c_all, weights):
    first = isinstance(h_rows, list)
    count, rows, model = c_all.shape
    hidden = weights.shape[0]
    tile = hidden_tile(hidden)
    spec = pl.BlockSpec((count, rows, tile), lambda step: (0, 0, step))
    whole = jax.ShapeDtypeStruct((count, rows, model), BF16)
    sources = h_rows if first else [h_rows]

    def column(place):
        return pl.BlockSpec((tile, model), lambda step: (step, place))

    return call(
        functools.partial(mlp_kernel, count, first),
        (hidden // tile,),
        [ANY] * (len(sources) + 1) + [column(0), column(1), column(2)],
        [spec] * 3 + [ANY] * first,
        [jax.ShapeDtypeStruct((count, rows, hidden), BF16)] * 3 + [whole] * first,
        [
            pltpu.VMEM((count, rows, model), BF16),
            pltpu.VMEM((count, rows, model), BF16),
            pltpu.SemaphoreType.DMA((count,)),
            pltpu.SemaphoreType.DMA((count,)),
            pltpu.SemaphoreType.DMA((count,)),
        ],
        2 + 6 * count * rows * model * hidden / RATE,
        grown(42, count) if first else 60,
    )(*sources, c_all, weights, weights, weights)


def mlp_grads_kernel(dg, du, hid, h_tile, c_tile, out, turned, slots, sems):
    step = pl.program_id(0)
    steps = pl.num_programs(0)
    tall, tile = slots.shape[2:]
    model = steps * tile
    slot = step % 2

    def sending(place, at, slot):
        columns = pl.ds(pl.multiple_of(place * model + at * tile, tile), tile)
        return pltpu.make_async_copy(slots.at[slot, place], out.at[:, columns], sems.at[slot, place])

    @pl.when(step == 0)
    def _():
        for place, left in enumerate((dg, du, hid)):
            turned[place * tall : place * tall + tall, :] = left[...].T

    @pl.when(step >= 2)
    def _():
        for place in range(3):
            sending(place, step - 2, slot).wait()

    both = dot_nn(turned[: 2 * tall, :], h_tile[...]).astype(BF16)
    slots[slot, 0] = both[:tall]
    slots[slot, 1] = both[tall:]
    slots[slot, 2] = dot_nn(turned[2 * tall :, :], c_tile[...]).astype(BF16)
    for place in range(3):
        sending(place, step, slot).start()

    @pl.when(step == steps - 1)
    def _():
        for place in range(3):
            sending(place, step - 1, 1 - slot).wait()
            sending(place, step, slot).wait()


def mlp_grads(d_gate, d_up, hidden, h_all, c_all):
    model = h_all.shape[2]
    lefts = [v.reshape(-1, v.shape[2]) for v in (d_gate, d_up, hidden)]
    rights = [v.reshape(-1, model) for v in (h_all, c_all)]
    inner, tall = lefts[0].shape
    tile = min(column_tile(model), model // 2)
    return call(
        mlp_grads_kernel,
        (model // tile,),
        [resident((inner, tall))] * 3 + [pl.BlockSpec((inner, tile), lambda step: (0, step))] * 2,
        ANY,
        jax.ShapeDtypeStruct((tall, 3 * model), BF16),
        [
            pltpu.VMEM((3 * tall, inner), BF16),
            pltpu.VMEM((2, 3, tall, tile), BF16),
            pltpu.SemaphoreType.DMA((2, 3)),
        ],
        3 + 6 * inner * tall * model / RATE,
        grown(40, inner, 2048),
    )(*lefts, *rights)


def weight_grad_kernel(left, right, *refs):
    out, turned = refs[-2:]

    @pl.when(pl.program_id(0) == 0)
    def _():
        turned[...] = left[...].T

    out[...] = dot_nn(turned[...], right[...])[: out.shape[0]].astype(BF16)


def weight_grad(rows_left, rows_right, kept, wide=None, into=None, place=0):
    left = rows_left.reshape(-1, rows_left.shape[-1])
    right = rows_right.reshape(-1, rows_right.shape[-1])
    inner, tall = left.shape
    model = right.shape[1]
    tile = column_tile(model)
    steps = model // tile
    extra = [] if into is None else [into]
    wide = model if wide is None else wide
    shape = (kept, wide) if into is None else into.shape
    return pl.pallas_call(
        weight_grad_kernel,
        grid=(steps,),
        in_specs=[resident(left.shape), pl.BlockSpec((inner, tile), lambda step: (0, step))] + [ANY] * len(extra),
        out_specs=pl.BlockSpec((kept, tile), lambda step: (0, place * steps + step)),
        out_shape=jax.ShapeDtypeStruct(shape, BF16),
        scratch_shapes=[pltpu.VMEM((tall, inner), BF16)],
        input_output_aliases={2: 0} if extra else {},
        **settings(3 + 2 * inner * tall * model / RATE, 1, grown(16, inner, 2048)),
    )(left, right, *extra)


def add_kernel(counts, *refs):
    at = 0
    for count, out in zip(counts, refs[sum(counts) :]):
        total = refs[at][0].astype(F32)
        for ref in refs[at + 1 : at + count]:
            total = total + ref[0].astype(F32)
        out[...] = total.astype(BF16)
        at += count


def add_rows(sums, memory=12):
    arrays = [array for terms in sums for array, _ in terms]
    places = [index for terms in sums for _, index in terms]
    _, rows, width = arrays[0].shape
    steps = 4
    tall = rows // steps

    def spec(place):
        return pl.BlockSpec((1, tall, width), lambda step: (place, step, 0))

    counts = [len(terms) for terms in sums]
    return call(
        functools.partial(add_kernel, counts),
        (steps,),
        [spec(place) for place in places],
        [pl.BlockSpec((tall, width), lambda step: (step, 0))] * len(sums),
        [jax.ShapeDtypeStruct((rows, width), BF16)] * len(sums),
        [],
        1 + 0.6 * len(arrays),
        memory,
    )(*arrays)


def last_kernel(terms, *refs):
    rows, base, gain, out = refs[terms:]
    total = refs[0][0].astype(F32)
    for ref in refs[1:terms]:
        total = total + ref[0].astype(F32)
    if gain is not None:
        x_val = rows[...].astype(F32)
        root = lax.rsqrt(jnp.mean(x_val * x_val, axis=-1, keepdims=True) + EPS)
        x_val = x_val * root
        total = total * gain[...]
        total = root * (total - x_val * jnp.mean(total * x_val, axis=-1, keepdims=True))
    out[...] = (base[...] + total).astype(BF16)


def last_rows(terms, base, rows=None, gain=None):
    tall, model = base.shape
    steps = 4
    block = pl.BlockSpec((tall // steps, model), lambda step: (step, 0))

    def spec(place):
        return pl.BlockSpec((1, tall // steps, model), lambda step: (place, step, 0))

    extra = [] if gain is None else [rows]
    kernel = last_kernel if gain is not None else lambda count, *refs: last_kernel(
        count, *refs[:count], None, refs[count], None, refs[count + 1]
    )
    return call(
        functools.partial(kernel, len(terms)),
        (steps,),
        [spec(place) for _, place in terms]
        + [block] * (len(extra) + 1)
        + ([] if gain is None else [resident(gain.shape)]),
        block,
        jax.ShapeDtypeStruct((tall, model), BF16),
        [],
        6.0,
        60,
    )(*[array for array, _ in terms], *extra, base, *([] if gain is None else [gain]))


def finish_grads_kernel(one_gate, one_up, one_down, two_gate, two_up, two_down, second, both, down, out):
    cut = one_gate.shape[0]
    both[:cut, 0, :] = one_gate[...].astype(F32)
    both[:cut, 1, :] = one_up[...].astype(F32)
    both[cut:, 0, :] = two_gate[...].astype(F32)
    both[cut:, 1, :] = two_up[...].astype(F32)
    down[:cut, :] = one_down[...].astype(F32)
    down[cut:, :] = two_down[...].astype(F32)
    out[...] = second[...].astype(F32)


def finish_grads(one, two, mix, model):
    rows = one.shape[0] + two.shape[0]
    own = mix.shape[0]
    tile = column_tile(model)
    steps = model // tile

    def spec(tall, place):
        return pl.BlockSpec((tall, tile), lambda step: (0, place * steps + step))

    return call(
        finish_grads_kernel,
        (steps,),
        [spec(part.shape[0], place) for part in (one, two) for place in range(3)] + [spec(own, 1)],
        [pl.BlockSpec((rows, 2, tile), lambda step: (0, 0, step)), spec(rows, 0), spec(own, 0)],
        [
            jax.ShapeDtypeStruct((rows, 2, model), F32),
            jax.ShapeDtypeStruct((rows, model), F32),
            jax.ShapeDtypeStruct((own, model), F32),
        ],
        [],
        5.0,
        16,
    )(one, one, one, two, two, two, mix)


def part_grads_kernel(block, first, second, tail, both, gate_w, rows):
    both[:, 0, :] = first[...].astype(F32)
    both[:, 1, :] = second[...].astype(F32)

    @pl.when(pl.program_id(0) == 0)
    def _():
        held = tail[...]
        gate_w[:, 0, :] = held[:, :block].astype(F32)
        gate_w[:, 1, :] = held[:, block : 2 * block].astype(F32)
        count = held.shape[0]
        row = lax.broadcasted_iota(jnp.int32, (count, count), 0)
        column = lax.broadcasted_iota(jnp.int32, (count, count), 1)
        rows[...] = dot_tn(held[:, 2 * block : 2 * block + 8], jnp.where(row == column, 1.0, 0.0).astype(BF16))


def part_grads(grads, last, model, wide, block):
    rows = grads.shape[0]
    tile = column_tile(model)
    steps = model // tile
    spec = pl.BlockSpec((rows, tile), lambda step: (0, step))
    return call(
        functools.partial(part_grads_kernel, block),
        (steps,),
        [spec, spec, pl.BlockSpec((rows, wide), lambda step: (0, model // wide))],
        [pl.BlockSpec((rows, 2, tile), lambda step: (0, 0, step)), resident((rows, 2, block)), resident((8, rows))],
        [
            jax.ShapeDtypeStruct((rows, 2, model), F32),
            jax.ShapeDtypeStruct((rows, 2, block), F32),
            jax.ShapeDtypeStruct((8, rows), F32),
        ],
        [],
        3.0,
        16,
    )(grads, last, last)


def seq_gather(shard):
    return lax.all_gather(shard, "seq", axis=0, tiled=True)


def seq_scatter(whole):
    return lax.psum_scatter(whole, "seq", scatter_dimension=0, tiled=True)


def per_device(
    tokens,
    cotangent,
    doc_ids,
    mix_in,
    mix_out,
    gate_w,
    conv_w,
    conv_bias,
    gate_bias,
    decay_param,
    gain_one,
    gain_two,
    mlp_in,
    mlp_out,
):
    run_len, model = tokens.shape[1:]
    n_seq = lax.axis_size("seq")
    n_dev = lax.axis_size("dp") * n_seq
    own = mix_out.shape[0]
    block = gate_w.shape[2]
    chan = own * n_seq
    width = -(-chan // 128) * 128
    blocks = chan // block

    x_low = tokens.reshape(run_len, model)
    x_pieces, _ = gather_rows(x_low)
    x_zero = x_low.astype(F32)
    cot_low = cotangent.reshape(run_len, model)
    lead = hand_on(x_low[run_len - HALO :], 1)
    part = gain_one.shape[0]
    vectors = [conv_w.reshape(-1), conv_bias, gate_bias.reshape(-1), decay_param]
    gains = jnp.concatenate([gain_one, gain_two, *vectors]).astype(BF16)[None]
    my_run = lax.axis_index("seq")
    first_token = my_run * run_len
    places = lax.broadcasted_iota(jnp.int32, (n_seq, 1), 0)
    gain_rows = jnp.where(places == my_run, gains, jnp.zeros((), BF16))
    for hop in range(1, n_seq):
        ring = [(source, (source + hop) % n_seq) for source in range(n_seq)]
        arrived = lax.ppermute(gains, "seq", ring)
        gain_rows = jnp.where(places == (my_run - hop) % n_seq, arrived, gain_rows)
    raw = gain_rows[:, 2 * part :].reshape(n_seq, 8, own).transpose(1, 0, 2).reshape(8, chan)
    raw = jnp.pad(raw.astype(F32), ((0, 0), (0, width - chan)))
    gain_rows = jnp.pad(gain_rows[:, : 2 * part].reshape(1, -1), ((0, 0), (0, model - 2 * part * n_seq)))
    padded = jnp.concatenate([jnp.full((3,), -1, jnp.int32), doc_ids.reshape(-1)])
    own_docs = lax.dynamic_slice_in_dim(padded, first_token + 3, run_len)
    same = sum(
        jnp.where(lax.dynamic_slice_in_dim(padded, first_token + 3 - back, run_len) == own_docs, 1.0, 0.0)
        for back in (1, 2, 3)
    )
    info = jnp.pad(same, (0, model - run_len)).astype(BF16)[None]
    tops, _ = gather_rows(jnp.concatenate([info, gain_rows, lead[2:]], 0))
    count = len(tops)
    half = count // 2

    small = gate_w.reshape(own, 2 * block)
    extra = -(-small.shape[1] // 128) * 128
    small = jnp.pad(small, ((0, 0), (0, extra - small.shape[1])))
    w_in = jnp.concatenate([mix_in[:, 1, :], mix_in[:, 0, :], mix_out, small], 1).astype(BF16)
    w_in = seq_gather(w_in)
    mlp_in, mlp_out = after((mlp_in, mlp_out), lead)
    shard = jnp.concatenate([mlp_in.astype(BF16).reshape(-1, 2 * model), mlp_out.astype(BF16)], 1)
    cut = 2 * shard.shape[0] // 3
    shards = [shard[:cut], shard[cut:]]
    w_one, w_two = [seq_gather(rows) for rows in shards]

    orders = jnp.asarray(piece_order(count), jnp.int32)
    order = lax.dynamic_index_in_dim(after(orders, lead), lax.axis_index("dp"), 0, False)
    places = lax.broadcasted_iota(jnp.int32, (count, 1), 0)
    gain_rows = jnp.zeros((count, 2 * part * n_seq), F32)
    for index, piece in enumerate(tops):
        row = piece[1:2, : 2 * part * n_seq].astype(F32)
        gain_rows = jnp.where(places == order[index], row, gain_rows)
    gain_rows = gain_rows.reshape(n_dev, 2 * part)
    g_one = gain_rows[:, :part].reshape(1, model)
    g_two = gain_rows[:, part:].reshape(1, model)

    h_all, h_one, same = first_norm(after(x_pieces, shards), tops, g_one, width)
    c_pieces, (same, entered) = gather_rows(
        after(cot_low, x_pieces[half - 1]),
        [
            ((1, 2), lambda sent, done: same),
            ((3,), lambda sent, done: mixer_enter(h_all, done[0], w_in, raw, extra, block)),
        ],
    )
    (u_ext, y_pre, conv, recur, enter, keep, cum, local, ends, w_z, par) = entered
    earlier = [hand_on(ends, steps) for steps in range(1, n_seq)]

    def leaving(blocks_at, pieces, before):
        return mixer_leave(earlier, cum, local, after(y_pre, *before), w_in, model, blocks_at, pieces)

    kept = []
    x_one = x_zero + scatter_rows(leaving, count, None)
    n_two, norm_two_back = jax.vjp(rms_norm, x_one, g_two)
    h_two = n_two.astype(BF16)

    h_pieces, (c_all,) = gather_rows(h_two, [((1, 2), lambda sent, done: assemble(after(c_pieces, sent)))])
    hid_one, gate_one, up_one, h_all = mlp_part(h_pieces, c_all, w_one)
    grad_one = mlp_grads(gate_one, up_one, hid_one, h_all, c_all)
    hid_two, gate_two, up_two = mlp_part(after(h_all, grad_one), c_all, w_two)
    grad_one = seq_scatter(grad_one)

    def d_entering(blocks_at, pieces, before):
        lefts = [after(gate_one, *before), up_one, gate_two, up_two]
        rights = [(w_one, 0, model), (w_one, 1, model), (w_two, 0, model), (w_two, 1, model)]
        return rows_times(lefts, rights, blocks_at, pieces)

    def second_grads(sent, done):
        return mlp_grads(after(gate_two, sent), up_two, hid_two, h_all, c_all), grad_one

    def mlp_leaving(blocks_at, pieces, before):
        return rows_times([after(hid_one, *before), hid_two], [(w_one, 2, model), (w_two, 2, model)], blocks_at, pieces)

    def mlp_out_rows(sent):
        return mlp_leaving([1, 0], half, (sent,))

    d_h_two = scatter_rows(d_entering, count, beside(mlp_out_rows, kept))
    d_x_norm, d_gain_two = norm_two_back(d_h_two)
    d_x_one = cot_low.astype(F32) + d_x_norm
    d_mix = d_x_one.astype(BF16)

    stages, twin = plane_stages(lax.axis_size("dp"))

    def mlp_out_sums(sent, done):
        theirs, mine = after(kept.pop(), sent)
        there = lax.ppermute(theirs, "dp", twin)
        return mine, there, add_rows([[(mine, k), (there, k)] for k in range(half // 2, half)])

    d_pieces, done = gather_rows(d_mix, [((1, 2), second_grads), ((3,), mlp_out_sums)])
    (grad_two, grad_one), (mine, there, far) = done
    grad_two = seq_scatter(after(grad_two, grad_one))
    d_y, mixed, cum_back, local_back, ends_back, d_all = head_back(
        after(d_pieces, far), earlier, cum, local, y_pre, keep, w_in
    )
    got = [lax.ppermute(part, "dp", stages[-1]) for part in far]
    mixed, got = lax.optimization_barrier((mixed, got))
    later = [hand_on(ends_back, -steps) for steps in range(1, n_seq)]
    wide = next(t for t in (128, 256, 512, 1024) if t >= 2 * block + 8 and model % t == 0)
    terms = [[(mine, k), (there, k), (got[k][None], 0)] for k in range(half // 2)]
    layer_sums = add_rows(terms[half // 4 :])
    grad_mix = weight_grad(after(d_y, ends_back, layer_sums), h_one, chan, 2 * model)
    grad_mix = weight_grad(mixed, d_all, chan, into=grad_mix, place=1)
    later, grad_mix, grad_two = lax.optimization_barrier((later, grad_mix, grad_two))
    grad_mix = seq_scatter(grad_mix)
    layer_got = [lax.ppermute(part, "dp", stages[-2]) for part in layer_sums]
    tailed = tail_back(
        earlier,
        later,
        cum_back,
        local_back,
        cum,
        local,
        recur,
        enter,
        keep,
        conv,
        u_ext,
        same,
        w_z,
        par,
        block,
        jax.ShapeDtypeStruct((chan, model + wide), BF16),
        wide,
    )
    (d_u, edges, grad_u), layer_got = lax.optimization_barrier((tailed, layer_got))
    terms = [[*those, (one[None], 0)] for those, one in zip(terms, layer_got)]
    from_next = hand_on(edges[:, :8], -1)
    layer_terms = scatter_tail(terms, stages[:-2], [])
    arrays = after([array for array, _ in layer_terms], edges)
    layer_out = last_rows([(v, at) for v, (_, at) in zip(arrays, layer_terms)], x_one)
    from_next, layer_out = lax.optimization_barrier((from_next, layer_out))
    layer_out = layer_out.reshape(1, run_len, model)
    d_u = lax.dynamic_update_slice(d_u, (edges[:, 8:] + from_next).astype(BF16), (0, run_len - 8, 0))
    gain_terms = []

    def d_leaving(blocks_at, pieces, before):
        *part_rows, gain_term = rows_times(
            [after(d_y, *before), d_u], [(w_in, 1, model), (w_in, 0, model)], blocks_at, pieces, h_one
        )
        gain_terms.append(gain_term.sum(0))
        return part_rows

    def u_grad(sent):
        return weight_grad(after(d_u, sent), h_one, chan, into=grad_u, place=0)

    def finished(sent):
        return finish_grads(after(grad_one, sent), grad_two, grad_mix, model)

    ready = []
    d_h_one, grad_u = scatter_terms(d_leaving, count, beside(finished, ready), u_grad)
    grad_mlp_in, grad_mlp_out, grad_out = ready.pop()
    grad_u = seq_scatter(after(grad_u, grad_mix))
    input_grad = last_rows(d_h_one, d_x_one, x_low, g_one)
    d_gain_one = sum(gain_terms) / g_one
    d_gains = jnp.concatenate([d_gain_one.reshape(n_dev, part), d_gain_two.reshape(n_dev, part)], 1)
    d_gains = lax.all_to_all(after(d_gains, d_h_one[-1][0]), ("dp", "seq"), 0, 0, tiled=True)
    grad_mix_in, grad_gate_w, rows = part_grads(after(grad_mix, grad_out), grad_u, model, wide, block)
    d_gains = after(d_gains, grad_mix_in).sum(0)
    return (
        layer_out,
        input_grad.reshape(1, run_len, model),
        grad_mix_in,
        grad_out,
        grad_gate_w,
        rows[:4],
        rows[4],
        rows[5:7],
        rows[7],
        d_gains[:part],
        d_gains[part:],
        grad_mlp_in,
        grad_mlp_out,
    )


def solution(mesh):
    rows = P(("dp", "seq"))
    placed = (
        P("dp", "seq", None),
        P("dp", "seq", None),
        P("dp", None),
        P(("dp", "seq"), None, None),
        P(("dp", "seq"), None),
        P(("dp", "seq"), None, None),
        P(None, ("dp", "seq")),
        rows,
        P(None, ("dp", "seq")),
        rows,
        rows,
        rows,
        P(("dp", "seq"), None, None),
        P(("dp", "seq"), None),
    )
    return jax.shard_map(
        per_device,
        mesh=mesh,
        in_specs=placed,
        out_specs=placed[:2] + placed[3:],
        check_vma=False,
    )
```
